512 devices in a mesh: win: 32 (over x, z), grp: 16 (over y, core).
Axes of the slice: x: 4, y: 8, z: 8, core: 2. Of those that a mesh axis runs over, the one named last changes fastest.
Arguments:
- query_rows: bfloat16 [65536, 1024], P(('grp', 'win')), may hold values from -5 to 5
- key_rows: bfloat16 [65536, 1024], P(('grp', 'win')), may hold values from -5 to 5
- value_rows: bfloat16 [65536, 1024], P(('grp', 'win')), may hold values from -6 to 6
- out_grad: bfloat16 [65536, 1024], P(('grp', 'win')), may hold values from -48 to 48
- far_blocks: int32 [1024, 8], P(('grp', 'win')), may hold values from 0 to 1023, as said below
Outputs:
- attended: bfloat16 [65536, 1024], P(('grp', 'win'))
- query_grad: bfloat16 [65536, 1024], P(('grp', 'win'))
- key_grad: bfloat16 [65536, 1024], P(('grp', 'win'))
- value_grad: bfloat16 [65536, 1024], P(('grp', 'win'))
The draws below stay inside these ranges and needn't reach their ends.
Inputs may be any that keep to these rules, and one draw needn't show every extreme that they name: far_blocks[b] names 8 blocks on devices with the win index of block b; the entries of the 2 rows of one device name exactly 1 block of every window group, its own included; a block may be named more than once.
All inputs are finite; a program needn't handle non-finite values.
Results may differ from the reference program's by a relative error of at most 0.024.
Values may be sent and summed in bfloat16 or wider, within the bound.
No kernel may reach another device: no remote copies, remote signals or barrier semaphores. Data moves between devices by JAX's collectives and lax.ppermute only.
A program may use at most 128 MiB of HBM per device.

```python
import jax
import jax.numpy as jnp
from jax import lax

HEADS = 8
HEAD_DIM = 128
BLOCK = 64
FAR = 8
GTOK = 1
TOK_DEV = 128
BLK_DEV = 2
CAP = 1
TOKENS = 65536
QBLOCKS = 1024
N_WIN = 32
N_GRP = 16


def base_rows(key, salt):
    full_shape = (N_GRP * N_WIN, TOK_DEV, HEADS * HEAD_DIM)
    return jnp.clip(jax.random.normal(jax.random.fold_in(key, salt), full_shape, jnp.float32), -4.0, 4.0)


def draw_query_rows(key, part):
    values = base_rows(key, 21)
    return values.reshape(TOKENS, HEADS * HEAD_DIM).astype(jnp.bfloat16)


def draw_key_rows(key, part):
    values = base_rows(key, 22)
    return values.reshape(TOKENS, HEADS * HEAD_DIM).astype(jnp.bfloat16)


def draw_far_blocks(key, part):
    devices = N_GRP * N_WIN
    entries = BLK_DEV * FAR
    device_keys = jax.random.split(key, devices)

    def one_device(device_key, device):
        first_key, second_key = jax.random.split(device_key, 2)
        groups_all = jnp.repeat(jnp.arange(N_GRP, dtype=jnp.int32), CAP, total_repeat_length=entries)
        shuffle = jax.random.permutation(first_key, entries)
        owner_group = groups_all[shuffle]
        column = device % N_WIN
        inner_block = jax.random.randint(second_key, (entries,), 0, BLK_DEV)
        block_ids = (owner_group * N_WIN + column) * BLK_DEV + inner_block
        return block_ids.reshape(BLK_DEV, FAR)
    listed = jax.vmap(one_device)(device_keys, jnp.arange(devices, dtype=jnp.int32))
    return listed.reshape(devices * BLK_DEV, FAR).astype(jnp.int32)


def shard_levels(key, dims, cuts, low, high):
    gain, own = 1.0, jax.random.fold_in(key, 6)
    for dim, shards_of in cuts:
        draws = jnp.exp(jax.random.uniform(jax.random.fold_in(own, dim), (shards_of,), jnp.float32, low / len(cuts), high / len(cuts)))
        gain = gain * jnp.repeat(draws, dims[dim] // shards_of).reshape([-1 if axis == dim else 1 for axis in range(len(dims))])
    return gain


def centred(key, shape, spread, bound, shards=(), kind=jnp.bfloat16):
    result = spread * jax.random.normal(key, shape, jnp.float32)
    if shards:
        result = result * shard_levels(key, shape, shards, -0.22, 0.18)
    return jnp.clip(result, -bound, bound).astype(kind)


def setup_inputs(seed: int = 0) -> dict:
    arg_keys = jax.random.split(jax.random.key(seed), 6)
    query_rows = draw_query_rows(jax.random.fold_in(arg_keys[5], 71), 0)
    key_rows = draw_key_rows(jax.random.fold_in(arg_keys[5], 71), 0)
    value_rows = centred(arg_keys[2], (TOKENS, HEADS * HEAD_DIM), 1.0, 6.0, ((0, 512),))
    out_grad = centred(arg_keys[3], (TOKENS, HEADS * HEAD_DIM), 8.0, 48.0, ((0, 512),))
    far_blocks = draw_far_blocks(jax.random.fold_in(arg_keys[5], 71), 0)
    return {"query_rows": query_rows, "key_rows": key_rows, "value_rows": value_rows, "out_grad": out_grad, "far_blocks": far_blocks}


def round_half(matrix):
    return lax.optimization_barrier(matrix.astype(jnp.bfloat16)).astype(jnp.float32)


def split_heads(matrix):
    return matrix.astype(jnp.float32).reshape(matrix.shape[:-1] + (HEADS, HEAD_DIM))


def attend_ref(query_part, near_key, near_value, near_mask, far_key, far_value, grad_part):
    scaling = HEAD_DIM ** -0.5
    near_scores = jnp.einsum('bqhd,khd->bhqk', query_part, near_key) * scaling
    near_scores = jnp.where(near_mask[None, None, None, :], near_scores, -jnp.inf)
    far_scores = jnp.einsum('bqhd,bkhd->bhqk', query_part, far_key) * scaling
    row_max = jnp.maximum(jnp.max(near_scores, axis=-1), jnp.max(far_scores, axis=-1))
    near_exp = jnp.exp(near_scores - row_max[..., None])
    far_exp = jnp.exp(far_scores - row_max[..., None])
    row_sum = jnp.sum(near_exp, axis=-1) + jnp.sum(far_exp, axis=-1)
    near_weight = near_exp / row_sum[..., None]
    far_weight = far_exp / row_sum[..., None]
    near_half = round_half(near_weight)
    far_half = round_half(far_weight)
    attended = round_half(jnp.einsum('bhqk,khd->bqhd', near_half, near_value)
                          + jnp.einsum('bhqk,bkhd->bqhd', far_half, far_value))
    row_delta = jnp.sum(grad_part * attended, axis=-1).transpose(0, 2, 1)
    near_sgrad = round_half(near_weight * (jnp.einsum('bqhd,khd->bhqk', grad_part, near_value) - row_delta[..., None]))
    far_sgrad = round_half(far_weight * (jnp.einsum('bqhd,bkhd->bhqk', grad_part, far_value) - row_delta[..., None]))
    query_grad = scaling * (jnp.einsum('bhqk,khd->bqhd', near_sgrad, near_key)
                            + jnp.einsum('bhqk,bkhd->bqhd', far_sgrad, far_key))
    near_kgrad = scaling * jnp.einsum('bhqk,bqhd->khd', near_sgrad, query_part)
    near_vgrad = jnp.einsum('bhqk,bqhd->khd', near_half, grad_part)
    far_kgrad = scaling * jnp.einsum('bhqk,bqhd->bkhd', far_sgrad, query_part)
    far_vgrad = jnp.einsum('bhqk,bqhd->bkhd', far_half, grad_part)
    return attended, query_grad, near_kgrad, near_vgrad, far_kgrad, far_vgrad


def reference(query_rows, key_rows, value_rows, out_grad, far_blocks):
    devices = N_GRP * N_WIN
    features = HEADS * HEAD_DIM
    entries = BLK_DEV * FAR
    query_dev = query_rows.reshape(devices, TOK_DEV, features)
    key_dev = key_rows.reshape(devices, TOK_DEV, features)
    value_dev = value_rows.reshape(devices, TOK_DEV, features)
    grad_dev = out_grad.reshape(devices, TOK_DEV, features)
    key_blocks = key_rows.reshape(QBLOCKS, BLOCK, features)
    value_blocks = value_rows.reshape(QBLOCKS, BLOCK, features)
    block_lists = far_blocks.reshape(devices, entries)
    glob_column = jnp.arange(N_WIN * GTOK, dtype=jnp.int32) // GTOK

    def device_step(running, device):
        key_acc, value_acc = running
        group_index = device // N_WIN
        column = device % N_WIN
        own_query = lax.dynamic_index_in_dim(query_dev, device, 0, False)
        own_key = lax.dynamic_index_in_dim(key_dev, device, 0, False)
        own_value = lax.dynamic_index_in_dim(value_dev, device, 0, False)
        own_grad = lax.dynamic_index_in_dim(grad_dev, device, 0, False)
        glob_key = lax.dynamic_slice_in_dim(key_dev, group_index * N_WIN, N_WIN, 0)[:, :GTOK].reshape(N_WIN * GTOK, features)
        glob_value = lax.dynamic_slice_in_dim(value_dev, group_index * N_WIN, N_WIN, 0)[:, :GTOK].reshape(N_WIN * GTOK, features)
        near_key = jnp.concatenate([own_key, glob_key], axis=0)
        near_value = jnp.concatenate([own_value, glob_value], axis=0)
        near_mask = jnp.concatenate([jnp.ones((TOK_DEV,), jnp.bool_), glob_column != column])
        far_ids = lax.dynamic_index_in_dim(block_lists, device, 0, False).astype(jnp.int32)
        far_key = jnp.take(key_blocks, far_ids, axis=0).reshape(BLK_DEV, FAR * BLOCK, features)
        far_value = jnp.take(value_blocks, far_ids, axis=0).reshape(BLK_DEV, FAR * BLOCK, features)
        outputs = attend_ref(split_heads(own_query).reshape(BLK_DEV, BLOCK, HEADS, HEAD_DIM),
                             split_heads(near_key), split_heads(near_value), near_mask,
                             split_heads(far_key), split_heads(far_value),
                             split_heads(own_grad).reshape(BLK_DEV, BLOCK, HEADS, HEAD_DIM))
        attended, query_grad, near_kgrad, near_vgrad, far_kgrad, far_vgrad = outputs
        own_blocks = device * BLK_DEV + jnp.arange(BLK_DEV, dtype=jnp.int32)
        glob_blocks = (group_index * N_WIN + jnp.arange(N_WIN, dtype=jnp.int32)) * BLK_DEV

        def accumulate(total, near_grad, far_grad):
            near_flat = near_grad.reshape(TOK_DEV + N_WIN * GTOK, features)
            total = total.at[own_blocks].add(near_flat[:TOK_DEV].reshape(BLK_DEV, BLOCK, features))
            total = total.at[glob_blocks, :GTOK].add(near_flat[TOK_DEV:].reshape(N_WIN, GTOK, features))
            rounded = round_half(far_grad.reshape(entries, BLOCK, features))
            return total.at[far_ids].add(rounded)

        key_acc = accumulate(key_acc, near_kgrad, far_kgrad)
        value_acc = accumulate(value_acc, near_vgrad, far_vgrad)
        return (key_acc, value_acc), (attended.reshape(TOK_DEV, features), query_grad.reshape(TOK_DEV, features).astype(jnp.bfloat16))

    empty_grads = jnp.zeros((QBLOCKS, BLOCK, features), jnp.float32)
    finals, stacked = lax.scan(device_step, (empty_grads, empty_grads), jnp.arange(devices, dtype=jnp.int32))
    key_acc, value_acc = finals
    attended, query_grad = stacked
    return (attended.reshape(TOKENS, features).astype(jnp.bfloat16),
            query_grad.reshape(TOKENS, features).astype(jnp.bfloat16),
            key_acc.reshape(TOKENS, features).astype(jnp.bfloat16),
            value_acc.reshape(TOKENS, features).astype(jnp.bfloat16))
```

```python
import functools
import math

import jax
import jax.numpy as jnp
from jax import lax
from jax.experimental import pallas as pl
from jax.experimental.pallas import tpu as pltpu
from jax.sharding import Mesh
from jax.sharding import PartitionSpec as P

HEAD_DIM = 128
BLOCK = 64
TOK = 128
BLK = 2
FAR = 8
NX, NZ, NY, NC = 4, 8, 8, 2
WINDOWS = NX * NZ
HALF = 512
HEADS = HALF // HEAD_DIM
NEAR = 256
FKEYS = FAR * BLOCK
SCALE = 1.0 / math.sqrt(HEAD_DIM)
EXP_SCALE = SCALE * math.log2(math.e)
BF16 = jnp.bfloat16
F32 = jnp.float32


def dot_nt(a, b):
    return lax.dot_general(a, b, (((1,), (1,)), ((), ())), preferred_element_type=F32)


def dot_nn(a, b):
    return lax.dot_general(a, b, (((1,), (0,)), ((), ())), preferred_element_type=F32)


def dot_tn(a, b):
    return lax.dot_general(a, b, (((0,), (0,)), ((), ())), preferred_element_type=F32)


def attend_kernel(*refs):
    pos, far_own, far_peer, qdo_own, qdo_peer, glob = refs[:6]
    sources = refs[6:22]
    res_own, res_peer, base, gglob = refs[22:26]
    parts = refs[26:40]
    slots, near, fgrad, table = refs[40:]
    my_y, my_c, my_w = pos[0], pos[1], pos[2]
    for who, far in enumerate((far_own, far_peer)):
        for row in range(BLK):
            for entry in range(FAR):
                block = far[row, entry]
                group = lax.shift_right_logical(block, 6)
                offset = lax.bitwise_and(lax.shift_right_logical(group, 1) - my_y, NY - 1)
                chain = lax.bitwise_xor(lax.bitwise_and(group, 1), my_c)
                inner = lax.bitwise_and(block, 1)
                table[who, chain * NY + offset] = (row * FAR + entry) * 2 + inner
    for source in range(2 * NY):
        for who in range(2):
            code = table[who, source]
            slot = lax.shift_right_logical(code, 1)
            inner = lax.bitwise_and(code, 1)
            at = pl.ds(pl.multiple_of(slot * BLOCK, BLOCK), BLOCK)
            rows = pl.ds(pl.multiple_of(inner * BLOCK, BLOCK), BLOCK)
            for kind in range(2):
                slots[kind, who, at, :] = sources[source][kind, rows, :]
    for who in range(2):
        for kind in range(2):
            near[kind, who, :TOK, :] = sources[who * NY][kind]
            first = (who * 2 + kind) * HALF
            near[kind, who, TOK : TOK + WINDOWS, :] = glob[:, first : first + HALF]
            near[kind, who, TOK + WINDOWS :, :] = jnp.zeros((NEAR - TOK - WINDOWS, HALF), BF16)
    column = lax.broadcasted_iota(jnp.int32, (TOK, NEAR), 1)
    hidden = (column >= TOK + WINDOWS) | (column == TOK + my_w)

    def head_step(head, carry):
        lanes = pl.ds(pl.multiple_of(head * HEAD_DIM, HEAD_DIM), HEAD_DIM)
        for who, (qdo, res) in enumerate(((qdo_own, res_own), (qdo_peer, res_peer))):
            query = qdo[0, :, lanes]
            grad = qdo[1, :, lanes]
            near_key = near[0, who, :, lanes]
            near_value = near[1, who, :, lanes]
            near_score = jnp.where(hidden, -1e30, dot_nt(query, near_key))
            near_dprod = dot_nt(grad, near_value)
            halves, near_dscore = [], []
            near_half = []
            for row in range(BLK):
                rows = slice(row * BLOCK, (row + 1) * BLOCK)
                keys = slice(row * FKEYS, (row + 1) * FKEYS)
                far_key = slots[0, who, keys, lanes]
                far_value = slots[1, who, keys, lanes]
                far_score = dot_nt(query[rows], far_key)
                ns = near_score[rows]
                top = jnp.maximum(
                    jnp.max(ns, axis=1, keepdims=True), jnp.max(far_score, axis=1, keepdims=True)
                )
                near_exp = jnp.exp2((ns - top) * EXP_SCALE)
                far_exp = jnp.exp2((far_score - top) * EXP_SCALE)
                total = jnp.sum(near_exp, axis=1, keepdims=True) + jnp.sum(
                    far_exp, axis=1, keepdims=True
                )
                inverse = 1.0 / total
                near_weight = near_exp * inverse
                far_weight = far_exp * inverse
                nh = near_weight.astype(BF16)
                fh = far_weight.astype(BF16)
                out = (dot_nn(nh, near_value) + dot_nn(fh, far_value)).astype(BF16)
                res[0, rows, lanes] = out
                g = grad[rows]
                delta = jnp.sum(g.astype(F32) * out.astype(F32), axis=1, keepdims=True)
                far_dprod = dot_nt(g, far_value)
                nd = (near_weight * (near_dprod[rows] - delta)).astype(BF16)
                fd = (far_weight * (far_dprod - delta)).astype(BF16)
                dq = (dot_nn(nd, near_key) + dot_nn(fd, far_key)) * SCALE
                res[1, rows, lanes] = dq.astype(BF16)
                fgrad[0, who, keys, lanes] = (dot_tn(fd, query[rows]) * SCALE).astype(BF16)
                fgrad[1, who, keys, lanes] = dot_tn(fh, g).astype(BF16)
                near_half.append(nh)
                near_dscore.append(nd)
            near_kgrad = dot_tn(jnp.concatenate(near_dscore, axis=0), query) * SCALE
            near_vgrad = dot_tn(jnp.concatenate(near_half, axis=0), grad)
            for kind, value in enumerate((near_kgrad, near_vgrad)):
                base[who, kind, :, lanes] = value[:TOK]
                first = (who * 2 + kind) * HALF
                cols = pl.ds(pl.multiple_of(first + head * HEAD_DIM, HEAD_DIM), HEAD_DIM)
                gglob[:, cols] = value[TOK : TOK + WINDOWS].astype(BF16)
        return carry

    lax.fori_loop(0, HEADS, head_step, 0)

    for source in range(2 * NY):
        for kind in range(2):
            for inner in range(BLK):
                rows = slice(inner * BLOCK, (inner + 1) * BLOCK)
                value = None
                for who in range(2):
                    code = table[who, source]
                    slot = lax.shift_right_logical(code, 1)
                    at = pl.ds(pl.multiple_of(slot * BLOCK, BLOCK), BLOCK)
                    here = (lax.bitwise_and(code, 1) == inner).astype(F32)
                    term = fgrad[kind, who, at, :].astype(F32) * here
                    value = term if value is None else value + term
                if source % NY == 0:
                    base[source // NY, kind, rows, :] += value
                else:
                    index = source - 1 - source // NY
                    parts[index][kind, rows, :] = value.astype(BF16)


def attend(pos, far_own, far_peer, qdo_own, qdo_peer, glob, sources):
    smem = pl.BlockSpec(memory_space=pltpu.SMEM)
    vmem = pl.BlockSpec(memory_space=pltpu.VMEM)
    piece = jax.ShapeDtypeStruct((2, TOK, HALF), BF16)
    return pl.pallas_call(
        attend_kernel,
        out_shape=[
            piece,
            piece,
            jax.ShapeDtypeStruct((2, 2, TOK, HALF), F32),
            jax.ShapeDtypeStruct((WINDOWS, 4 * HALF), BF16),
        ]
        + [piece] * 14,
        in_specs=[smem] * 3 + [vmem] * 19,
        out_specs=[vmem] * 18,
        scratch_shapes=[
            pltpu.VMEM((2, 2, BLK * FKEYS, HALF), BF16),
            pltpu.VMEM((2, 2, NEAR, HALF), BF16),
            pltpu.VMEM((2, 2, BLK * FKEYS, HALF), BF16),
            pltpu.SMEM((2, 2 * NY), jnp.int32),
        ],
        compiler_params=pltpu.CompilerParams(vmem_limit_bytes=44 * 1024 * 1024),
        cost_estimate=pl.CostEstimate(
            flops=1_200_000_000, bytes_accessed=12_000_000, transcendentals=800_000
        ),
    )(pos, far_own, far_peer, qdo_own, qdo_peer, glob, *sources)


UP = [(i, (i + 1) % NY) for i in range(NY)]
DOWN = [(i, (i - 1) % NY) for i in range(NY)]
SWAP = [(0, 1), (1, 0)]


def per_device(query_rows, key_rows, value_rows, out_grad, far_blocks):
    my_y = lax.axis_index("y")
    my_c = lax.axis_index("c")
    my_w = lax.axis_index("x") * NZ + lax.axis_index("z")
    swap = functools.partial(lax.ppermute, axis_name="c", perm=SWAP)
    up = functools.partial(lax.ppermute, axis_name="y", perm=UP)
    down = functools.partial(lax.ppermute, axis_name="y", perm=DOWN)
    low = my_c == 0

    def split(first, second):
        mine = [jnp.where(low, a[:, :HALF], a[:, HALF:]) for a in (first, second)]
        other = [jnp.where(low, a[:, HALF:], a[:, :HALF]) for a in (first, second)]
        return jnp.stack(mine), jnp.stack(other)

    kv_own, kv_send = split(key_rows, value_rows)
    qdo_own, qdo_send = split(query_rows, out_grad)
    kv_peer = swap(kv_send)
    sources = [None] * 16
    sources[0], sources[NY] = kv_own, kv_peer
    chains = [
        (0, up, 4, -1),
        (0, down, 3, 1),
        (NY, up, 3, -1),
        (NY, down, 4, 1),
    ]
    held = [kv_own, kv_own, kv_peer, kv_peer]
    for step in range(1, 5):
        for i, (first, move, count, sign) in enumerate(chains):
            if step <= count:
                held[i] = move(held[i])
                sources[first + (sign * step) % NY] = held[i]
    qdo_peer = swap(qdo_send)
    far_peer = swap(far_blocks)
    row = jnp.concatenate([kv_own[0, 0], kv_own[1, 0], kv_peer[0, 0], kv_peer[1, 0]])
    glob = lax.all_to_all(
        jnp.broadcast_to(row, (WINDOWS, 4 * HALF)), ("x", "z"), 0, 0, tiled=True
    )
    pos = jnp.stack([my_y, my_c, my_w]).astype(jnp.int32)
    res_own, res_peer, base, gglob, *parts = attend(
        pos, far_blocks, far_peer, qdo_own, qdo_peer, glob, sources
    )
    part = parts[:7], parts[7:]

    held = [
        part[0][4 - 1],
        part[0][5 - 1],
        part[1][3 - 1],
        part[1][4 - 1],
    ]
    at = [4, 5, 3, 4]
    for step in range(1, 5):
        for i, (first, move, count, sign) in enumerate(chains):
            if step <= count:
                held[i] = move(held[i])
                at[i] = (at[i] + sign) % NY
                if at[i]:
                    mine = part[first // NY][at[i] - 1]
                    held[i] = (held[i].astype(F32) + mine.astype(F32)).astype(BF16)
    gback = lax.all_to_all(gglob, ("x", "z"), 0, 0, tiled=True)
    gsum = jnp.sum(gback.astype(F32), axis=0).reshape(2, 2, 1, HALF)
    res_back = swap(res_peer)
    first_row = lax.broadcasted_iota(jnp.int32, (1, TOK, 1), 1) == 0

    def finish(who):
        total = base[who] + held[2 * who].astype(F32) + held[2 * who + 1].astype(F32)
        return (total + jnp.where(first_row, gsum[who], 0.0)).astype(BF16)

    peer_grad = swap(finish(1))
    own_grad = finish(0)

    def join(mine, other):
        return jnp.where(
            low,
            jnp.concatenate([mine, other], axis=1),
            jnp.concatenate([other, mine], axis=1),
        )

    return (
        join(res_own[0], res_back[0]),
        join(res_own[1], res_back[1]),
        join(own_grad[0], peer_grad[0]),
        join(own_grad[1], peer_grad[1]),
    )


def solution(mesh):
    fine = Mesh(mesh.devices.reshape(NX, NZ, NY, NC), ("x", "z", "y", "c"))
    spec = P(("y", "c", "x", "z"), None)
    return jax.shard_map(
        per_device, mesh=fine, in_specs=(spec,) * 5, out_specs=(spec,) * 4, check_vma=False
    )
```

```python
import functools
import math

import jax
import jax.numpy as jnp
from jax import lax
from jax.experimental import pallas as pl
from jax.experimental.pallas import tpu as pltpu
from jax.sharding import Mesh
from jax.sharding import PartitionSpec as P

HEAD_DIM = 128
BLOCK = 64
TOK = 128
BLK = 2
FAR = 8
NX, NZ, NY, NC = 4, 8, 8, 2
WINDOWS = NX * NZ
HALF = 512
HEADS = HALF // HEAD_DIM
NEAR = 256
GROWS = 4 * HEADS
SEND_ORDER = [11, 12, 5, 4, 14, 13, 2, 3, 9, 10, 7, 6, 15, 1, 8, 0]
FKEYS = FAR * BLOCK
SCALE = 1.0 / math.sqrt(HEAD_DIM)
EXP_SCALE = SCALE * math.log2(math.e)
BF16 = jnp.bfloat16
F32 = jnp.float32


def dot_nt(a, b):
    return lax.dot_general(a, b, (((1,), (1,)), ((), ())), preferred_element_type=F32)


def dot_nn(a, b):
    return lax.dot_general(a, b, (((1,), (0,)), ((), ())), preferred_element_type=F32)


def dot_tn(a, b):
    return lax.dot_general(a, b, (((0,), (0,)), ((), ())), preferred_element_type=F32)


def attend_kernel(*refs):
    pos, far_own, far_peer, qdo_own, qdo_peer, glob = refs[:6]
    sources = refs[6:22]
    outputs = refs[22:26]
    parts = refs[26:40]
    slots, near, fgrad, gwide, res_own, res_peer, base, gglob, spare, table, in_sem, out_sem = refs[40:]
    my_y, my_c, my_w, my_sign = pos[0], pos[1], pos[2], pos[3]
    for who, far in enumerate((far_own, far_peer)):
        for row in range(BLK):
            for entry in range(FAR):
                block = far[row, entry]
                group = lax.shift_right_logical(block, 6)
                offset = lax.bitwise_and(
                    (lax.shift_right_logical(group, 1) - my_y) * my_sign, NY - 1
                )
                chain = lax.bitwise_xor(lax.bitwise_and(group, 1), my_c)
                inner = lax.bitwise_and(block, 1)
                table[who, chain * NY + offset] = (row * FAR + entry) * 2 + inner
    copies = []
    for who in range(2):
        copies.append(
            pltpu.make_async_copy(
                sources[who * NY], near.at[:, who, :TOK, :], in_sem.at[len(copies)]
            )
        )
    for source in range(2 * NY):
        for who in range(2):
            code = table[who, source]
            slot = lax.shift_right_logical(code, 1)
            inner = lax.bitwise_and(code, 1)
            at = pl.ds(pl.multiple_of(slot * BLOCK, BLOCK), BLOCK)
            rows = pl.ds(pl.multiple_of(inner * BLOCK, BLOCK), BLOCK)
            copies.append(
                pltpu.make_async_copy(
                    sources[source].at[:, rows, :],
                    slots.at[:, who, at, :],
                    in_sem.at[len(copies)],
                )
            )
    for copy in copies:
        copy.start()
    gwide[...] = glob[...].astype(F32).reshape(WINDOWS * GROWS, HEAD_DIM)
    for who in range(2):
        for kind in range(2):
            for head in range(HEADS):
                first = (who * 2 + kind) * HEADS + head
                near[kind, who, TOK : TOK + WINDOWS, head * HEAD_DIM : (head + 1) * HEAD_DIM] = (
                    gwide[pl.ds(first, WINDOWS, stride=GROWS), :].astype(BF16)
                )
            near[kind, who, TOK + WINDOWS :, :] = jnp.zeros((NEAR - TOK - WINDOWS, HALF), BF16)
    column = lax.broadcasted_iota(jnp.int32, (TOK, NEAR), 1)
    hidden = (column >= TOK + WINDOWS) | (column == TOK + my_w)
    for copy in copies:
        copy.wait()

    def head_step(head, carry):
        lanes = pl.ds(pl.multiple_of(head * HEAD_DIM, HEAD_DIM), HEAD_DIM)
        for who, (qdo, res) in enumerate(((qdo_own, res_own), (qdo_peer, res_peer))):
            query = qdo[0, :, lanes]
            grad = qdo[1, :, lanes]
            near_key = near[0, who, :, lanes]
            near_value = near[1, who, :, lanes]
            near_score = jnp.where(hidden, -1e30, dot_nt(query, near_key))
            near_dprod = dot_nt(grad, near_value)
            halves, near_dscore = [], []
            near_half = []
            for row in range(BLK):
                rows = slice(row * BLOCK, (row + 1) * BLOCK)
                keys = slice(row * FKEYS, (row + 1) * FKEYS)
                far_key = slots[0, who, keys, lanes]
                far_value = slots[1, who, keys, lanes]
                far_score = dot_nt(query[rows], far_key)
                ns = near_score[rows]
                top = jnp.maximum(
                    jnp.max(ns, axis=1, keepdims=True), jnp.max(far_score, axis=1, keepdims=True)
                )
                near_exp = jnp.exp2((ns - top) * EXP_SCALE)
                far_exp = jnp.exp2((far_score - top) * EXP_SCALE)
                total = jnp.sum(near_exp, axis=1, keepdims=True) + jnp.sum(
                    far_exp, axis=1, keepdims=True
                )
                inverse = 1.0 / total
                near_weight = near_exp * inverse
                far_weight = far_exp * inverse
                nh = near_weight.astype(BF16)
                fh = far_weight.astype(BF16)
                out = (dot_nn(nh, near_value) + dot_nn(fh, far_value)).astype(BF16)
                res[0, rows, lanes] = out
                g = grad[rows]
                delta = jnp.sum(g.astype(F32) * out.astype(F32), axis=1, keepdims=True)
                far_dprod = dot_nt(g, far_value)
                nd = (near_weight * (near_dprod[rows] - delta)).astype(BF16)
                fd = (far_weight * (far_dprod - delta)).astype(BF16)
                dq = (dot_nn(nd, near_key) + dot_nn(fd, far_key)) * SCALE
                res[1, rows, lanes] = dq.astype(BF16)
                fgrad[0, who, keys, lanes] = (dot_tn(fd, query[rows]) * SCALE).astype(BF16)
                fgrad[1, who, keys, lanes] = dot_tn(fh, g).astype(BF16)
                near_half.append(nh)
                near_dscore.append(nd)
            near_kgrad = dot_tn(jnp.concatenate(near_dscore, axis=0), query) * SCALE
            near_vgrad = dot_tn(jnp.concatenate(near_half, axis=0), grad)
            for kind, value in enumerate((near_kgrad, near_vgrad)):
                base[who, kind, :, lanes] = value[:TOK]
                first = (who * 2 + kind) * HEADS + head
                gwide[pl.ds(first, WINDOWS, stride=GROWS), :] = value[TOK : TOK + WINDOWS]
        return carry

    lax.fori_loop(0, HEADS, head_step, 0)
    gglob[...] = gwide[...].reshape(WINDOWS, GROWS, HEAD_DIM).astype(BF16)
    copies = []

    def send(value, output):
        copy = pltpu.make_async_copy(value, output, out_sem.at[len(copies)])
        copy.start()
        copies.append(copy)

    send(gglob, outputs[3])
    send(res_peer, outputs[1])
    send(res_own, outputs[0])
    for source in SEND_ORDER:
        for kind in range(2):
            for inner in range(BLK):
                rows = slice(inner * BLOCK, (inner + 1) * BLOCK)
                value = None
                for who in range(2):
                    code = table[who, source]
                    slot = lax.shift_right_logical(code, 1)
                    at = pl.ds(pl.multiple_of(slot * BLOCK, BLOCK), BLOCK)
                    here = (lax.bitwise_and(code, 1) == inner).astype(F32)
                    term = fgrad[kind, who, at, :].astype(F32) * here
                    value = term if value is None else value + term
                if source % NY == 0:
                    base[source // NY, kind, rows, :] += value
                else:
                    spare[source - 1 - source // NY, kind, rows, :] = value.astype(BF16)
        if source % NY:
            index = source - 1 - source // NY
            send(spare.at[index], parts[index])
    send(base, outputs[2])
    for copy in copies:
        copy.wait()


def attend(pos, far_own, far_peer, qdo_own, qdo_peer, glob, sources):
    smem = pl.BlockSpec(memory_space=pltpu.SMEM)
    vmem = pl.BlockSpec(memory_space=pltpu.VMEM)
    anywhere = pl.BlockSpec(memory_space=pl.ANY)
    piece = jax.ShapeDtypeStruct((2, TOK, HALF), BF16)
    return pl.pallas_call(
        attend_kernel,
        out_shape=[
            piece,
            piece,
            jax.ShapeDtypeStruct((2, 2, TOK, HALF), F32),
            jax.ShapeDtypeStruct((WINDOWS, GROWS, HEAD_DIM), BF16),
        ]
        + [piece] * 14,
        in_specs=[smem] * 3 + [vmem] * 3 + [anywhere] * 16,
        out_specs=[anywhere] * 18,
        scratch_shapes=[
            pltpu.VMEM((2, 2, BLK * FKEYS, HALF), BF16),
            pltpu.VMEM((2, 2, NEAR, HALF), BF16),
            pltpu.VMEM((2, 2, BLK * FKEYS, HALF), BF16),
            pltpu.VMEM((WINDOWS * GROWS, HEAD_DIM), F32),
            pltpu.VMEM((2, TOK, HALF), BF16),
            pltpu.VMEM((2, TOK, HALF), BF16),
            pltpu.VMEM((2, 2, TOK, HALF), F32),
            pltpu.VMEM((WINDOWS, GROWS, HEAD_DIM), BF16),
            pltpu.VMEM((2 * NY - 2, 2, TOK, HALF), BF16),
            pltpu.SMEM((2, 2 * NY), jnp.int32),
            pltpu.SemaphoreType.DMA((2 + 4 * NY,)),
            pltpu.SemaphoreType.DMA((2 + 2 * NY,)),
        ],
        compiler_params=pltpu.CompilerParams(vmem_limit_bytes=60 * 1024 * 1024),
        cost_estimate=pl.CostEstimate(
            flops=1_200_000_000, bytes_accessed=12_000_000, transcendentals=800_000
        ),
    )(pos, far_own, far_peer, qdo_own, qdo_peer, glob, *sources)


EVEN = [(i, i ^ 1) for i in range(NY)]
ODD = [(i, (((i + 1) ^ 1) - 1) % NY) for i in range(NY)]
SWAP = [(0, 1), (1, 0)]


def plus(a, b):
    return (a.astype(F32) + b.astype(F32)).astype(BF16)


def per_device(query_rows, key_rows, value_rows, out_grad, far_blocks):
    my_y = lax.axis_index("y")
    my_c = lax.axis_index("c")
    my_w = lax.axis_index("x") * NZ + lax.axis_index("z")
    swap = functools.partial(lax.ppermute, axis_name="c", perm=SWAP)
    even = functools.partial(lax.ppermute, axis_name="y", perm=EVEN)
    odd = functools.partial(lax.ppermute, axis_name="y", perm=ODD)
    low = my_c == 0

    def split(first, second):
        mine = [jnp.where(low, a[:, :HALF], a[:, HALF:]) for a in (first, second)]
        other = [jnp.where(low, a[:, HALF:], a[:, :HALF]) for a in (first, second)]
        return jnp.stack(mine), jnp.stack(other)

    kv_own, kv_send = split(key_rows, value_rows)
    qdo_own, qdo_send = split(query_rows, out_grad)
    a, b = {0: kv_own}, {0: swap(kv_send)}
    row = jnp.concatenate([a[0][:, 0], b[0][:, 0]]).reshape(GROWS, HEAD_DIM)
    glob = lax.all_to_all(
        jnp.broadcast_to(row, (WINDOWS, GROWS, HEAD_DIM)), ("x", "z"), 0, 0, tiled=True
    )
    a[1], b[-1] = even(a[0]), odd(b[0])
    a[-1], b[1] = odd(a[0]), even(b[0])
    a[-2], b[2] = odd(a[1]), even(b[-1])
    a[2], b[-2] = even(a[-1]), odd(b[1])
    a[3], b[-3] = even(a[-2]), odd(b[2])
    qdo_peer = swap(qdo_send)
    far_peer = swap(far_blocks)
    glob, a[2], a[3], b[-2], b[-3] = lax.optimization_barrier((glob, a[2], a[3], b[-2], b[-3]))
    a[-3], b[3] = odd(a[2]), even(b[-2])
    a[-4], b[4] = odd(a[3]), even(b[-3])
    sources = [x[r] if r in x else x[r - NY] for x in (a, b) for r in range(NY)]
    pos = jnp.stack([my_y, my_c, my_w, 1 - 2 * (my_y % 2)]).astype(jnp.int32)
    res_own, res_peer, base, gglob, *parts = attend(
        pos, far_blocks, far_peer, qdo_own, qdo_peer, glob, sources
    )
    a = {r: parts[r % NY - 1] for r in range(-4, 4) if r}
    b = {r: parts[NY - 2 + r % NY] for r in range(-3, 5) if r}
    gback = lax.all_to_all(gglob, ("x", "z"), 0, 0, tiled=True)
    b[-2], a[2] = plus(b[-2], even(b[3])), plus(a[2], odd(a[-3]))
    b[-3], a[3] = plus(b[-3], even(b[4])), plus(a[3], odd(a[-4]))
    b[1], a[-1] = plus(b[1], odd(b[-2])), plus(a[-1], even(a[2]))
    b[2], a[-2] = plus(b[2], odd(b[-3])), plus(a[-2], even(a[3]))
    b[-1], a[1] = plus(b[-1], even(b[2])), plus(a[1], odd(a[-2]))
    far_own = odd(a[-1]), even(a[1])
    far_peer = even(b[1]), odd(b[-1])
    gsum = jnp.sum(gback.astype(F32), axis=0).reshape(2, 2, 1, HALF)
    res_back = swap(res_peer)
    first_row = lax.broadcasted_iota(jnp.int32, (1, TOK, 1), 1) == 0

    def finish(who, far):
        total = base[who] + far[0].astype(F32) + far[1].astype(F32)
        return (total + jnp.where(first_row, gsum[who], 0.0)).astype(BF16)

    peer_grad = swap(finish(1, far_peer))
    own_grad = finish(0, far_own)

    def join(mine, other):
        return jnp.where(
            low,
            jnp.concatenate([mine, other], axis=1),
            jnp.concatenate([other, mine], axis=1),
        )

    return (
        join(res_own[0], res_back[0]),
        join(res_own[1], res_back[1]),
        join(own_grad[0], peer_grad[0]),
        join(own_grad[1], peer_grad[1]),
    )


def solution(mesh):
    fine = Mesh(mesh.devices.reshape(NX, NZ, NY, NC), ("x", "z", "y", "c"))
    spec = P(("y", "c", "x", "z"), None)
    return jax.shard_map(
        per_device, mesh=fine, in_specs=(spec,) * 5, out_specs=(spec,) * 4, check_vma=False
    )
```

```python
import functools
import math

import jax
import jax.numpy as jnp
from jax import lax
from jax.experimental import pallas as pl
from jax.experimental.pallas import tpu as pltpu
from jax.sharding import Mesh
from jax.sharding import PartitionSpec as P

HEAD_DIM = 128
BLOCK = 64
TOK = 128
BLK = 2
FAR = 8
NX, NZ, NY, NC = 4, 8, 8, 2
WINDOWS = NX * NZ
HALF = 512
HEADS = HALF // HEAD_DIM
NEAR = 256
GROWS = 4 * HEADS
ROUNDS = ((0,), (1,), (-1, -2), (2, 3), (-3, -4))
FKEYS = FAR * BLOCK
SCALE = 1.0 / math.sqrt(HEAD_DIM)
EXP_SCALE = SCALE * math.log2(math.e)
BF16 = jnp.bfloat16
F32 = jnp.float32


def dot_nt(a, b):
    return lax.dot_general(a, b, (((1,), (1,)), ((), ())), preferred_element_type=F32)


def dot_nn(a, b):
    return lax.dot_general(a, b, (((1,), (0,)), ((), ())), preferred_element_type=F32)


def dot_tn(a, b):
    return lax.dot_general(a, b, (((0,), (0,)), ((), ())), preferred_element_type=F32)


def at_step(chain, step):
    return chain * NY + (-step if chain else step) % NY


def attend_kernel(*refs):
    pos, far_own, far_peer, qdo_own, qdo_peer, glob = refs[:6]
    arrays = refs[6:16]
    outputs = refs[16:20]
    parts = refs[20:28]
    slots, near, fgrad, gwide, res_own, res_peer, base, gglob, spare, table, in_sem, out_sem = refs[28:]
    sources = [None] * (2 * NY)
    for chain in range(2):
        for round_, steps in enumerate(ROUNDS):
            for i, step in enumerate(steps):
                array = arrays[chain * len(ROUNDS) + round_]
                sources[at_step(chain, step)] = array.at[i] if len(steps) > 1 else array
    my_y, my_c, my_w, my_sign = pos[0], pos[1], pos[2], pos[3]
    for who, far in enumerate((far_own, far_peer)):
        for row in range(BLK):
            for entry in range(FAR):
                block = far[row, entry]
                group = lax.shift_right_logical(block, 6)
                offset = lax.bitwise_and(
                    (lax.shift_right_logical(group, 1) - my_y) * my_sign, NY - 1
                )
                chain = lax.bitwise_xor(lax.bitwise_and(group, 1), my_c)
                inner = lax.bitwise_and(block, 1)
                table[who, chain * NY + offset] = (row * FAR + entry) * 2 + inner
    copies = []
    for who in range(2):
        copies.append(
            pltpu.make_async_copy(
                sources[who * NY], near.at[:, who, :TOK, :], in_sem.at[len(copies)]
            )
        )
    for source in range(2 * NY):
        for who in range(2):
            code = table[who, source]
            slot = lax.shift_right_logical(code, 1)
            inner = lax.bitwise_and(code, 1)
            at = pl.ds(pl.multiple_of(slot * BLOCK, BLOCK), BLOCK)
            rows = pl.ds(pl.multiple_of(inner * BLOCK, BLOCK), BLOCK)
            copies.append(
                pltpu.make_async_copy(
                    sources[source].at[:, rows, :],
                    slots.at[:, who, at, :],
                    in_sem.at[len(copies)],
                )
            )
    for copy in copies:
        copy.start()
    gwide[...] = glob[...].astype(F32).reshape(WINDOWS * GROWS, HEAD_DIM)
    for who in range(2):
        for kind in range(2):
            for head in range(HEADS):
                first = (who * 2 + kind) * HEADS + head
                near[kind, who, TOK : TOK + WINDOWS, head * HEAD_DIM : (head + 1) * HEAD_DIM] = (
                    gwide[pl.ds(first, WINDOWS, stride=GROWS), :].astype(BF16)
                )
            near[kind, who, TOK + WINDOWS :, :] = jnp.zeros((NEAR - TOK - WINDOWS, HALF), BF16)
    column = lax.broadcasted_iota(jnp.int32, (TOK, NEAR), 1)
    hidden = (column >= TOK + WINDOWS) | (column == TOK + my_w)
    for copy in copies:
        copy.wait()

    def head_step(head, carry):
        lanes = pl.ds(pl.multiple_of(head * HEAD_DIM, HEAD_DIM), HEAD_DIM)
        for who, (qdo, res) in enumerate(((qdo_own, res_own), (qdo_peer, res_peer))):
            query = qdo[0, :, lanes]
            grad = qdo[1, :, lanes]
            near_key = near[0, who, :, lanes]
            near_value = near[1, who, :, lanes]
            near_score = jnp.where(hidden, -1e30, dot_nt(query, near_key))
            near_dprod = dot_nt(grad, near_value)
            halves, near_dscore = [], []
            near_half = []
            for row in range(BLK):
                rows = slice(row * BLOCK, (row + 1) * BLOCK)
                keys = slice(row * FKEYS, (row + 1) * FKEYS)
                far_key = slots[0, who, keys, lanes]
                far_value = slots[1, who, keys, lanes]
                far_score = dot_nt(query[rows], far_key)
                ns = near_score[rows]
                top = jnp.maximum(
                    jnp.max(ns, axis=1, keepdims=True), jnp.max(far_score, axis=1, keepdims=True)
                )
                near_exp = jnp.exp2((ns - top) * EXP_SCALE)
                far_exp = jnp.exp2((far_score - top) * EXP_SCALE)
                total = jnp.sum(near_exp, axis=1, keepdims=True) + jnp.sum(
                    far_exp, axis=1, keepdims=True
                )
                inverse = 1.0 / total
                near_weight = near_exp * inverse
                far_weight = far_exp * inverse
                nh = near_weight.astype(BF16)
                fh = far_weight.astype(BF16)
                out = (dot_nn(nh, near_value) + dot_nn(fh, far_value)).astype(BF16)
                res[0, rows, lanes] = out
                g = grad[rows]
                delta = jnp.sum(g.astype(F32) * out.astype(F32), axis=1, keepdims=True)
                far_dprod = dot_nt(g, far_value)
                nd = (near_weight * (near_dprod[rows] - delta)).astype(BF16)
                fd = (far_weight * (far_dprod - delta)).astype(BF16)
                dq = (dot_nn(nd, near_key) + dot_nn(fd, far_key)) * SCALE
                res[1, rows, lanes] = dq.astype(BF16)
                fgrad[0, who, keys, lanes] = (dot_tn(fd, query[rows]) * SCALE).astype(BF16)
                fgrad[1, who, keys, lanes] = dot_tn(fh, g).astype(BF16)
                near_half.append(nh)
                near_dscore.append(nd)
            near_kgrad = dot_tn(jnp.concatenate(near_dscore, axis=0), query) * SCALE
            near_vgrad = dot_tn(jnp.concatenate(near_half, axis=0), grad)
            for kind, value in enumerate((near_kgrad, near_vgrad)):
                base[who, kind, :, lanes] = value[:TOK]
                first = (who * 2 + kind) * HEADS + head
                gwide[pl.ds(first, WINDOWS, stride=GROWS), :] = value[TOK : TOK + WINDOWS]
        return carry

    lax.fori_loop(0, HEADS, head_step, 0)
    gglob[...] = gwide[...].reshape(WINDOWS, GROWS, HEAD_DIM).astype(BF16)
    copies = []

    def send(value, output):
        copy = pltpu.make_async_copy(value, output, out_sem.at[len(copies)])
        copy.start()
        copies.append(copy)

    send(gglob, outputs[3])
    send(res_peer, outputs[1])
    send(res_own, outputs[0])
    for round_ in (4, 3, 2, 1, 0):
        for chain in (1, 0):
            for step in ROUNDS[round_]:
                source = at_step(chain, step)
                for kind in range(2):
                    for inner in range(BLK):
                        rows = slice(inner * BLOCK, (inner + 1) * BLOCK)
                        value = None
                        for who in range(2):
                            code = table[who, source]
                            slot = lax.shift_right_logical(code, 1)
                            at = pl.ds(pl.multiple_of(slot * BLOCK, BLOCK), BLOCK)
                            here = (lax.bitwise_and(code, 1) == inner).astype(F32)
                            term = fgrad[kind, who, at, :].astype(F32) * here
                            value = term if value is None else value + term
                        if round_ == 0:
                            base[chain, kind, rows, :] += value
                        else:
                            spare[source, kind, rows, :] = value.astype(BF16)
                if round_:
                    part = parts[chain * 4 + round_ - 1]
                    where = part.at[ROUNDS[round_].index(step)] if round_ > 1 else part
                    send(spare.at[source], where)
    send(base, outputs[2])
    for copy in copies:
        copy.wait()


def attend(pos, far_own, far_peer, qdo_own, qdo_peer, glob, arrays):
    smem = pl.BlockSpec(memory_space=pltpu.SMEM)
    vmem = pl.BlockSpec(memory_space=pltpu.VMEM)
    anywhere = pl.BlockSpec(memory_space=pl.ANY)
    piece = jax.ShapeDtypeStruct((2, TOK, HALF), BF16)
    double = jax.ShapeDtypeStruct((2, 2, TOK, HALF), BF16)
    return pl.pallas_call(
        attend_kernel,
        out_shape=[
            piece,
            piece,
            jax.ShapeDtypeStruct((2, 2, TOK, HALF), F32),
            jax.ShapeDtypeStruct((WINDOWS, GROWS, HEAD_DIM), BF16),
        ]
        + [piece, double, double, double] * 2,
        in_specs=[smem] * 3 + [vmem] * 3 + [anywhere] * 10,
        out_specs=[anywhere] * 12,
        scratch_shapes=[
            pltpu.VMEM((2, 2, BLK * FKEYS, HALF), BF16),
            pltpu.VMEM((2, 2, NEAR, HALF), BF16),
            pltpu.VMEM((2, 2, BLK * FKEYS, HALF), BF16),
            pltpu.VMEM((WINDOWS * GROWS, HEAD_DIM), F32),
            pltpu.VMEM((2, TOK, HALF), BF16),
            pltpu.VMEM((2, TOK, HALF), BF16),
            pltpu.VMEM((2, 2, TOK, HALF), F32),
            pltpu.VMEM((WINDOWS, GROWS, HEAD_DIM), BF16),
            pltpu.VMEM((2 * NY, 2, TOK, HALF), BF16),
            pltpu.SMEM((2, 2 * NY), jnp.int32),
            pltpu.SemaphoreType.DMA((2 + 4 * NY,)),
            pltpu.SemaphoreType.DMA((2 + 2 * NY,)),
        ],
        compiler_params=pltpu.CompilerParams(vmem_limit_bytes=60 * 1024 * 1024),
        cost_estimate=pl.CostEstimate(
            flops=1_200_000_000, bytes_accessed=12_000_000, transcendentals=800_000
        ),
    )(pos, far_own, far_peer, qdo_own, qdo_peer, glob, *arrays)


EVEN = [(i, i ^ 1) for i in range(NY)]
ODD = [(i, (((i + 1) ^ 1) - 1) % NY) for i in range(NY)]
SWAP = [(0, 1), (1, 0)]


def plus(a, b):
    return (a.astype(F32) + b.astype(F32)).astype(BF16)


def per_device(query_rows, key_rows, value_rows, out_grad, far_blocks):
    my_y = lax.axis_index("y")
    my_c = lax.axis_index("c")
    my_w = lax.axis_index("x") * NZ + lax.axis_index("z")
    swap = functools.partial(lax.ppermute, axis_name="c", perm=SWAP)
    even = functools.partial(lax.ppermute, axis_name="y", perm=EVEN)
    odd = functools.partial(lax.ppermute, axis_name="y", perm=ODD)
    low = my_c == 0

    def split(first, second):
        mine = [jnp.where(low, a[:, :HALF], a[:, HALF:]) for a in (first, second)]
        other = [jnp.where(low, a[:, HALF:], a[:, :HALF]) for a in (first, second)]
        return jnp.stack(mine), jnp.stack(other)

    kv_own, kv_send = split(key_rows, value_rows)
    qdo_own, qdo_send = split(query_rows, out_grad)
    moves = (even, odd), (odd, even)
    a, b = [kv_own], [swap(kv_send)]
    row = jnp.concatenate([a[0][:, 0], b[0][:, 0]]).reshape(GROWS, HEAD_DIM)
    chains = list(zip((a, b), moves))
    for held, (first, second) in chains:
        held.append(first(held[0]))
    row, a[1], b[1] = lax.optimization_barrier((row, a[1], b[1]))
    glob = lax.all_to_all(
        jnp.broadcast_to(row, (WINDOWS, GROWS, HEAD_DIM)), ("x", "z"), 0, 0, tiled=True
    )
    for held, (first, second) in chains:
        held.append(second(jnp.stack(held)))
    for held, (first, second) in chains:
        held.append(first(held[2]))
    glob, a[3], b[3] = lax.optimization_barrier((glob, a[3], b[3]))
    qdo_peer = swap(qdo_send)
    far_peer = swap(far_blocks)
    for held, (first, second) in chains:
        held.append(second(held[3]))
    pos = jnp.stack([my_y, my_c, my_w, 1 - 2 * (my_y % 2)]).astype(jnp.int32)
    res_own, res_peer, base, gglob, *parts = attend(
        pos, far_blocks, far_peer, qdo_own, qdo_peer, glob, a + b
    )
    chains = [(parts[4:], moves[1]), (parts[:4], moves[0])]
    back = [second(terms[3]) for terms, (first, second) in chains]
    gglob, *back = lax.optimization_barrier((gglob, *back))
    gback = lax.all_to_all(gglob, ("x", "z"), 0, 0, tiled=True)
    back = [
        first(plus(terms[2], got)) for got, (terms, (first, second)) in zip(back, chains)
    ]
    back = [
        second(plus(terms[1], got)) for got, (terms, (first, second)) in zip(back, chains)
    ]
    last = [
        first(plus(terms[0], got[1])) for got, (terms, (first, second)) in zip(back, chains)
    ]
    far_peer, far_own = [(x[0], y) for x, y in zip(back, last)]
    gsum = jnp.sum(gback.astype(F32), axis=0).reshape(2, 2, 1, HALF)
    res_back = swap(res_peer)
    first_row = lax.broadcasted_iota(jnp.int32, (1, TOK, 1), 1) == 0

    def finish(who, far):
        total = base[who] + far[0].astype(F32) + far[1].astype(F32)
        return (total + jnp.where(first_row, gsum[who], 0.0)).astype(BF16)

    peer_grad = swap(finish(1, far_peer))
    own_grad = finish(0, far_own)

    def join(mine, other):
        return jnp.where(
            low,
            jnp.concatenate([mine, other], axis=1),
            jnp.concatenate([other, mine], axis=1),
        )

    return (
        join(res_own[0], res_back[0]),
        join(res_own[1], res_back[1]),
        join(own_grad[0], peer_grad[0]),
        join(own_grad[1], peer_grad[1]),
    )


def solution(mesh):
    fine = Mesh(mesh.devices.reshape(NX, NZ, NY, NC), ("x", "z", "y", "c"))
    spec = P(("y", "c", "x", "z"), None)
    return jax.shard_map(
        per_device, mesh=fine, in_specs=(spec,) * 5, out_specs=(spec,) * 4, check_vma=False
    )
```

```python
import functools
import math

import jax
import jax.numpy as jnp
from jax import lax
from jax.experimental import pallas as pl
from jax.experimental.pallas import tpu as pltpu
from jax.sharding import Mesh
from jax.sharding import PartitionSpec as P

HEAD_DIM = 128
BLOCK = 64
TOK = 128
BLK = 2
FAR = 8
NX, NZ, NY, NC = 4, 8, 8, 2
WINDOWS = NX * NZ
HALF = 512
HEADS = HALF // HEAD_DIM
NEAR = 256
GROWS = 4 * HEADS
SEND_ORDER = (4, 12, 11, 5, 3, 6, 10, 13, 2, 7, 9, 14, 1, 15, 8, 0)
FKEYS = FAR * BLOCK
SCALE = 1.0 / math.sqrt(HEAD_DIM)
EXP_SCALE = SCALE * math.log2(math.e)
BF16 = jnp.bfloat16
F32 = jnp.float32


def dot_nt(a, b):
    return lax.dot_general(a, b, (((1,), (1,)), ((), ())), preferred_element_type=F32)


def dot_nn(a, b):
    return lax.dot_general(a, b, (((1,), (0,)), ((), ())), preferred_element_type=F32)


def dot_tn(a, b):
    return lax.dot_general(a, b, (((0,), (0,)), ((), ())), preferred_element_type=F32)


def attend_kernel(*refs):
    pos, far_own, far_peer, qdo_own, qdo_peer, glob = refs[:6]
    sources = refs[6:22]
    outputs = refs[22:26]
    parts = refs[26:40]
    slots, near, fgrad, gwide, res_own, res_peer, base, gglob, spare, table, in_sem, out_sem = refs[40:]
    my_y, my_c, my_w = pos[0], pos[1], pos[2]
    for who, far in enumerate((far_own, far_peer)):
        for row in range(BLK):
            for entry in range(FAR):
                block = far[row, entry]
                group = lax.shift_right_logical(block, 6)
                offset = lax.bitwise_and(
                    lax.shift_right_logical(group, 1) - my_y, NY - 1
                )
                chain = lax.bitwise_xor(lax.bitwise_and(group, 1), my_c)
                inner = lax.bitwise_and(block, 1)
                table[who, chain * NY + offset] = (row * FAR + entry) * 2 + inner
    copies = []
    for who in range(2):
        copies.append(
            pltpu.make_async_copy(
                sources[who * NY], near.at[:, who, :TOK, :], in_sem.at[len(copies)]
            )
        )
    for source in range(2 * NY):
        for who in range(2):
            code = table[who, source]
            slot = lax.shift_right_logical(code, 1)
            inner = lax.bitwise_and(code, 1)
            at = pl.ds(pl.multiple_of(slot * BLOCK, BLOCK), BLOCK)
            rows = pl.ds(pl.multiple_of(inner * BLOCK, BLOCK), BLOCK)
            copies.append(
                pltpu.make_async_copy(
                    sources[source].at[:, rows, :],
                    slots.at[:, who, at, :],
                    in_sem.at[len(copies)],
                )
            )
    for copy in copies:
        copy.start()
    gwide[...] = glob[...].astype(F32).reshape(WINDOWS * GROWS, HEAD_DIM)
    for who in range(2):
        for kind in range(2):
            for head in range(HEADS):
                first = (who * 2 + kind) * HEADS + head
                near[kind, who, TOK : TOK + WINDOWS, head * HEAD_DIM : (head + 1) * HEAD_DIM] = (
                    gwide[pl.ds(first, WINDOWS, stride=GROWS), :].astype(BF16)
                )
            near[kind, who, TOK + WINDOWS :, :] = jnp.zeros((NEAR - TOK - WINDOWS, HALF), BF16)
    column = lax.broadcasted_iota(jnp.int32, (TOK, NEAR), 1)
    hidden = (column >= TOK + WINDOWS) | (column == TOK + my_w)
    for copy in copies:
        copy.wait()

    def head_step(head, carry):
        lanes = pl.ds(pl.multiple_of(head * HEAD_DIM, HEAD_DIM), HEAD_DIM)
        for who, (qdo, res) in enumerate(((qdo_own, res_own), (qdo_peer, res_peer))):
            query = qdo[0, :, lanes]
            grad = qdo[1, :, lanes]
            near_key = near[0, who, :, lanes]
            near_value = near[1, who, :, lanes]
            near_score = jnp.where(hidden, -1e30, dot_nt(query, near_key))
            near_dprod = dot_nt(grad, near_value)
            halves, near_dscore = [], []
            near_half = []
            for row in range(BLK):
                rows = slice(row * BLOCK, (row + 1) * BLOCK)
                keys = slice(row * FKEYS, (row + 1) * FKEYS)
                far_key = slots[0, who, keys, lanes]
                far_value = slots[1, who, keys, lanes]
                far_score = dot_nt(query[rows], far_key)
                ns = near_score[rows]
                top = jnp.maximum(
                    jnp.max(ns, axis=1, keepdims=True), jnp.max(far_score, axis=1, keepdims=True)
                )
                near_exp = jnp.exp2((ns - top) * EXP_SCALE)
                far_exp = jnp.exp2((far_score - top) * EXP_SCALE)
                total = jnp.sum(near_exp, axis=1, keepdims=True) + jnp.sum(
                    far_exp, axis=1, keepdims=True
                )
                inverse = 1.0 / total
                near_weight = near_exp * inverse
                far_weight = far_exp * inverse
                nh = near_weight.astype(BF16)
                fh = far_weight.astype(BF16)
                out = (dot_nn(nh, near_value) + dot_nn(fh, far_value)).astype(BF16)
                res[0, rows, lanes] = out
                g = grad[rows]
                delta = jnp.sum(g.astype(F32) * out.astype(F32), axis=1, keepdims=True)
                far_dprod = dot_nt(g, far_value)
                nd = (near_weight * (near_dprod[rows] - delta)).astype(BF16)
                fd = (far_weight * (far_dprod - delta)).astype(BF16)
                dq = (dot_nn(nd, near_key) + dot_nn(fd, far_key)) * SCALE
                res[1, rows, lanes] = dq.astype(BF16)
                fgrad[0, who, keys, lanes] = (dot_tn(fd, query[rows]) * SCALE).astype(BF16)
                fgrad[1, who, keys, lanes] = dot_tn(fh, g).astype(BF16)
                near_half.append(nh)
                near_dscore.append(nd)
            near_kgrad = dot_tn(jnp.concatenate(near_dscore, axis=0), query) * SCALE
            near_vgrad = dot_tn(jnp.concatenate(near_half, axis=0), grad)
            for kind, value in enumerate((near_kgrad, near_vgrad)):
                base[who, kind, :, lanes] = value[:TOK]
                first = (who * 2 + kind) * HEADS + head
                gwide[pl.ds(first, WINDOWS, stride=GROWS), :] = value[TOK : TOK + WINDOWS]
        return carry

    lax.fori_loop(0, HEADS, head_step, 0)
    gglob[...] = gwide[...].reshape(WINDOWS, GROWS, HEAD_DIM).astype(BF16)
    copies = []

    def send(value, output):
        copy = pltpu.make_async_copy(value, output, out_sem.at[len(copies)])
        copy.start()
        copies.append(copy)

    send(gglob, outputs[3])
    send(res_peer, outputs[1])
    send(res_own, outputs[0])
    for source in SEND_ORDER:
        for kind in range(2):
            for inner in range(BLK):
                rows = slice(inner * BLOCK, (inner + 1) * BLOCK)
                value = None
                for who in range(2):
                    code = table[who, source]
                    slot = lax.shift_right_logical(code, 1)
                    at = pl.ds(pl.multiple_of(slot * BLOCK, BLOCK), BLOCK)
                    here = (lax.bitwise_and(code, 1) == inner).astype(F32)
                    term = fgrad[kind, who, at, :].astype(F32) * here
                    value = term if value is None else value + term
                if source % NY == 0:
                    base[source // NY, kind, rows, :] += value
                else:
                    spare[source, kind, rows, :] = value.astype(BF16)
        if source % NY:
            send(spare.at[source], parts[source - 1 - source // NY])
    send(base, outputs[2])
    for copy in copies:
        copy.wait()


def attend(pos, far_own, far_peer, qdo_own, qdo_peer, glob, sources):
    smem = pl.BlockSpec(memory_space=pltpu.SMEM)
    vmem = pl.BlockSpec(memory_space=pltpu.VMEM)
    anywhere = pl.BlockSpec(memory_space=pl.ANY)
    piece = jax.ShapeDtypeStruct((2, TOK, HALF), BF16)
    return pl.pallas_call(
        attend_kernel,
        out_shape=[
            piece,
            piece,
            jax.ShapeDtypeStruct((2, 2, TOK, HALF), F32),
            jax.ShapeDtypeStruct((WINDOWS, GROWS, HEAD_DIM), BF16),
        ]
        + [piece] * 14,
        in_specs=[smem] * 3 + [vmem] * 3 + [anywhere] * 16,
        out_specs=[anywhere] * 18,
        scratch_shapes=[
            pltpu.VMEM((2, 2, BLK * FKEYS, HALF), BF16),
            pltpu.VMEM((2, 2, NEAR, HALF), BF16),
            pltpu.VMEM((2, 2, BLK * FKEYS, HALF), BF16),
            pltpu.VMEM((WINDOWS * GROWS, HEAD_DIM), F32),
            pltpu.VMEM((2, TOK, HALF), BF16),
            pltpu.VMEM((2, TOK, HALF), BF16),
            pltpu.VMEM((2, 2, TOK, HALF), F32),
            pltpu.VMEM((WINDOWS, GROWS, HEAD_DIM), BF16),
            pltpu.VMEM((2 * NY, 2, TOK, HALF), BF16),
            pltpu.SMEM((2, 2 * NY), jnp.int32),
            pltpu.SemaphoreType.DMA((2 + 4 * NY,)),
            pltpu.SemaphoreType.DMA((2 + 2 * NY,)),
        ],
        compiler_params=pltpu.CompilerParams(vmem_limit_bytes=60 * 1024 * 1024),
        cost_estimate=pl.CostEstimate(
            flops=1_200_000_000, bytes_accessed=12_000_000, transcendentals=800_000
        ),
    )(pos, far_own, far_peer, qdo_own, qdo_peer, glob, *sources)


UP = [(i, (i + 1) % NY) for i in range(NY)]
DOWN = [(i, (i - 1) % NY) for i in range(NY)]
ROW_STEP, BACK_STEP = 1, 1
SWAP = [(0, 1), (1, 0)]


def plus(a, b):
    return (a.astype(F32) + b.astype(F32)).astype(BF16)


def per_device(query_rows, key_rows, value_rows, out_grad, far_blocks):
    my_y = lax.axis_index("y")
    my_c = lax.axis_index("c")
    my_w = lax.axis_index("x") * NZ + lax.axis_index("z")
    swap = functools.partial(lax.ppermute, axis_name="c", perm=SWAP)
    up = functools.partial(lax.ppermute, axis_name="y", perm=UP)
    down = functools.partial(lax.ppermute, axis_name="y", perm=DOWN)
    low = my_c == 0

    def split(first, second):
        mine = [jnp.where(low, a[:, :HALF], a[:, HALF:]) for a in (first, second)]
        other = [jnp.where(low, a[:, HALF:], a[:, :HALF]) for a in (first, second)]
        return jnp.stack(mine), jnp.stack(other)

    kv_own, kv_send = split(key_rows, value_rows)
    qdo_own, qdo_send = split(query_rows, out_grad)
    kv_peer = swap(kv_send)
    sources = [None] * 16
    sources[0], sources[NY] = kv_own, kv_peer
    row = jnp.concatenate([kv_own[:, 0], kv_peer[:, 0]]).reshape(GROWS, HEAD_DIM)
    chains = ((0, up, 4, -1), (0, down, 3, 1), (NY, up, 3, -1), (NY, down, 4, 1))
    held = [kv_own, kv_own, kv_peer, kv_peer]
    for step in range(1, 5):
        for i, (first, move, count, sign) in enumerate(chains):
            if step <= count:
                held[i] = move(held[i])
        if step == ROW_STEP:
            row, held[0] = lax.optimization_barrier((row, held[0]))
            glob = lax.all_to_all(
                jnp.broadcast_to(row, (WINDOWS, GROWS, HEAD_DIM)), ("x", "z"), 0, 0, tiled=True
            )
            qdo_peer = swap(qdo_send)
            far_peer = swap(far_blocks)
        if step == 3:
            glob, qdo_peer, far_peer, held[3] = lax.optimization_barrier(
                (glob, qdo_peer, far_peer, held[3])
            )
        for i, (first, move, count, sign) in enumerate(chains):
            if step <= count:
                sources[first + (sign * step) % NY] = held[i]
    pos = jnp.stack([my_y, my_c, my_w]).astype(jnp.int32)
    res_own, res_peer, base, gglob, *parts = attend(
        pos, far_blocks, far_peer, qdo_own, qdo_peer, glob, sources
    )
    part = parts[:7], parts[7:]
    at = [4, 5, 3, 4]
    held = [part[first // NY][o - 1] for o, (first, _, _, _) in zip(at, chains)]
    for step in range(1, 5):
        for i, (first, move, count, sign) in enumerate(chains):
            if step <= count:
                held[i] = move(held[i])
        if step == BACK_STEP:
            gglob, held[0] = lax.optimization_barrier((gglob, held[0]))
            gback = lax.all_to_all(gglob, ("x", "z"), 0, 0, tiled=True)
        for i, (first, move, count, sign) in enumerate(chains):
            if step <= count:
                at[i] = (at[i] + sign) % NY
                if at[i]:
                    held[i] = plus(held[i], part[first // NY][at[i] - 1])
    far_own, far_peer = held[:2], held[2:]
    gsum = jnp.sum(gback.astype(F32), axis=0).reshape(2, 2, 1, HALF)
    res_back = swap(res_peer)
    first_row = lax.broadcasted_iota(jnp.int32, (1, TOK, 1), 1) == 0

    def finish(who, far):
        total = base[who] + far[0].astype(F32) + far[1].astype(F32)
        return (total + jnp.where(first_row, gsum[who], 0.0)).astype(BF16)

    peer_grad = swap(finish(1, far_peer))
    own_grad = finish(0, far_own)

    def join(mine, other):
        return jnp.where(
            low,
            jnp.concatenate([mine, other], axis=1),
            jnp.concatenate([other, mine], axis=1),
        )

    return (
        join(res_own[0], res_back[0]),
        join(res_own[1], res_back[1]),
        join(own_grad[0], peer_grad[0]),
        join(own_grad[1], peer_grad[1]),
    )


def solution(mesh):
    fine = Mesh(mesh.devices.reshape(NX, NZ, NY, NC), ("x", "z", "y", "c"))
    spec = P(("y", "c", "x", "z"), None)
    return jax.shard_map(
        per_device, mesh=fine, in_specs=(spec,) * 5, out_specs=(spec,) * 4, check_vma=False
    )
```

```python
import functools
import math

import jax
import jax.numpy as jnp
from jax import lax
from jax.experimental import pallas as pl
from jax.experimental.pallas import tpu as pltpu
from jax.sharding import Mesh
from jax.sharding import PartitionSpec as P

HEAD_DIM = 128
BLOCK = 64
TOK = 128
BLK = 2
FAR = 8
NX, NZ, NY, NC = 4, 8, 8, 2
WINDOWS = NX * NZ
HALF = 512
HEADS = HALF // HEAD_DIM
NEAR = 256
GROWS = 4 * HEADS
SEND_ORDER = (4, 12, 11, 3, 5, 13, 2, 10, 6, 14, 1, 9, 7, 15, 8, 0)
FKEYS = FAR * BLOCK
SCALE = 1.0 / math.sqrt(HEAD_DIM)
EXP_SCALE = SCALE * math.log2(math.e)
BF16 = jnp.bfloat16
F32 = jnp.float32


def dot_nt(a, b):
    return lax.dot_general(a, b, (((1,), (1,)), ((), ())), preferred_element_type=F32)


def dot_nn(a, b):
    return lax.dot_general(a, b, (((1,), (0,)), ((), ())), preferred_element_type=F32)


def dot_tn(a, b):
    return lax.dot_general(a, b, (((0,), (0,)), ((), ())), preferred_element_type=F32)


def attend_kernel(*refs):
    pos, far_own, far_peer, qdo_own, qdo_peer, glob = refs[:6]
    arrays = refs[6:15]
    outputs = refs[15:19]
    parts = refs[19:27]
    slots, near, fgrad, gwide, res_own, res_peer, base, gglob, spare, table, in_sem, out_sem = refs[27:]
    sources = [
        arrays[offset if offset < 4 else offset + 1].at[chain] if offset != 4 else arrays[4 + chain]
        for chain in range(2)
        for offset in range(NY)
    ]
    my_y, my_c, my_w = pos[0], pos[1], pos[2]
    for who, far in enumerate((far_own, far_peer)):
        for row in range(BLK):
            for entry in range(FAR):
                block = far[row, entry]
                group = lax.shift_right_logical(block, 6)
                chain = lax.bitwise_xor(lax.bitwise_and(group, 1), my_c)
                offset = lax.bitwise_and(
                    lax.shift_right_logical(group, 1) - my_y, NY - 1
                )
                inner = lax.bitwise_and(block, 1)
                table[who, chain * NY + offset] = (row * FAR + entry) * 2 + inner
    copies = []
    for who in range(2):
        copies.append(
            pltpu.make_async_copy(
                sources[who * NY], near.at[:, who, :TOK, :], in_sem.at[len(copies)]
            )
        )
    for source in range(2 * NY):
        for who in range(2):
            code = table[who, source]
            slot = lax.shift_right_logical(code, 1)
            inner = lax.bitwise_and(code, 1)
            at = pl.ds(pl.multiple_of(slot * BLOCK, BLOCK), BLOCK)
            rows = pl.ds(pl.multiple_of(inner * BLOCK, BLOCK), BLOCK)
            copies.append(
                pltpu.make_async_copy(
                    sources[source].at[:, rows, :],
                    slots.at[:, who, at, :],
                    in_sem.at[len(copies)],
                )
            )
    for copy in copies:
        copy.start()
    gwide[...] = glob[...].astype(F32).reshape(WINDOWS * GROWS, HEAD_DIM)
    for who in range(2):
        for kind in range(2):
            for head in range(HEADS):
                first = (who * 2 + kind) * HEADS + head
                near[kind, who, TOK : TOK + WINDOWS, head * HEAD_DIM : (head + 1) * HEAD_DIM] = (
                    gwide[pl.ds(first, WINDOWS, stride=GROWS), :].astype(BF16)
                )
            near[kind, who, TOK + WINDOWS :, :] = jnp.zeros((NEAR - TOK - WINDOWS, HALF), BF16)
    column = lax.broadcasted_iota(jnp.int32, (TOK, NEAR), 1)
    hidden = (column >= TOK + WINDOWS) | (column == TOK + my_w)
    for copy in copies:
        copy.wait()

    def head_step(head, carry):
        lanes = pl.ds(pl.multiple_of(head * HEAD_DIM, HEAD_DIM), HEAD_DIM)
        both = range(2)
        pairs = [(who, row) for who in both for row in range(BLK)]
        rows = [slice(row * BLOCK, (row + 1) * BLOCK) for row in range(BLK)]
        keys = [slice(row * FKEYS, (row + 1) * FKEYS) for row in range(BLK)]
        res = res_own, res_peer
        query = [qdo[0, :, lanes] for qdo in (qdo_own, qdo_peer)]
        grad = [qdo[1, :, lanes] for qdo in (qdo_own, qdo_peer)]
        near_score = [
            jnp.where(hidden, -1e30, dot_nt(query[who], near[0, who, :, lanes])) for who in both
        ]
        far_score = [
            dot_nt(query[who][rows[row]], slots[0, who, keys[row], lanes]) for who, row in pairs
        ]
        near_dprod = [dot_nt(grad[who], near[1, who, :, lanes]) for who in both]
        far_dprod = [
            dot_nt(grad[who][rows[row]], slots[1, who, keys[row], lanes]) for who, row in pairs
        ]
        near_weight, far_weight, near_half, far_half = [], [], [], []
        for i, (who, row) in enumerate(pairs):
            ns = near_score[who][rows[row]]
            top = jnp.maximum(
                jnp.max(ns, axis=1, keepdims=True), jnp.max(far_score[i], axis=1, keepdims=True)
            )
            near_exp = jnp.exp2((ns - top) * EXP_SCALE)
            far_exp = jnp.exp2((far_score[i] - top) * EXP_SCALE)
            inverse = 1.0 / (
                jnp.sum(near_exp, axis=1, keepdims=True) + jnp.sum(far_exp, axis=1, keepdims=True)
            )
            near_weight.append(near_exp * inverse)
            far_weight.append(far_exp * inverse)
            near_half.append(near_weight[i].astype(BF16))
            far_half.append(far_weight[i].astype(BF16))
        delta = []
        for i, (who, row) in enumerate(pairs):
            out = dot_nn(near_half[i], near[1, who, :, lanes])
            out = (out + dot_nn(far_half[i], slots[1, who, keys[row], lanes])).astype(BF16)
            res[who][0, rows[row], lanes] = out
            g = grad[who][rows[row]]
            delta.append(jnp.sum(g.astype(F32) * out.astype(F32), axis=1, keepdims=True))
        for i, (who, row) in enumerate(pairs):
            g = grad[who][rows[row]]
            fgrad[1, who, keys[row], lanes] = dot_tn(far_half[i], g).astype(BF16)
        near_dscore, far_dscore = [], []
        for i, (who, row) in enumerate(pairs):
            nd = near_weight[i] * (near_dprod[who][rows[row]] - delta[i])
            near_dscore.append(nd.astype(BF16))
            far_dscore.append((far_weight[i] * (far_dprod[i] - delta[i])).astype(BF16))
        for i, (who, row) in enumerate(pairs):
            dq = dot_nn(near_dscore[i], near[0, who, :, lanes])
            dq = (dq + dot_nn(far_dscore[i], slots[0, who, keys[row], lanes])) * SCALE
            res[who][1, rows[row], lanes] = dq.astype(BF16)
        for i, (who, row) in enumerate(pairs):
            dk = dot_tn(far_dscore[i], query[who][rows[row]]) * SCALE
            fgrad[0, who, keys[row], lanes] = dk.astype(BF16)
        for who in both:
            two = slice(who * BLK, (who + 1) * BLK)
            near_kgrad = dot_tn(jnp.concatenate(near_dscore[two], axis=0), query[who]) * SCALE
            near_vgrad = dot_tn(jnp.concatenate(near_half[two], axis=0), grad[who])
            for kind, value in enumerate((near_kgrad, near_vgrad)):
                base[who, kind, :, lanes] = value[:TOK]
                first = (who * 2 + kind) * HEADS + head
                gwide[pl.ds(first, WINDOWS, stride=GROWS), :] = value[TOK : TOK + WINDOWS]
        return carry

    lax.fori_loop(0, HEADS, head_step, 0)
    gglob[...] = gwide[...].reshape(WINDOWS, GROWS, HEAD_DIM).astype(BF16)
    copies = []

    def send(value, output):
        copy = pltpu.make_async_copy(value, output, out_sem.at[len(copies)])
        copy.start()
        copies.append(copy)

    send(gglob, outputs[3])
    send(res_peer, outputs[1])
    send(res_own, outputs[0])
    for source in SEND_ORDER:
        for kind in range(2):
            for inner in range(BLK):
                rows = slice(inner * BLOCK, (inner + 1) * BLOCK)
                value = None
                for who in range(2):
                    code = table[who, source]
                    slot = lax.shift_right_logical(code, 1)
                    at = pl.ds(pl.multiple_of(slot * BLOCK, BLOCK), BLOCK)
                    here = (lax.bitwise_and(code, 1) == inner).astype(F32)
                    term = fgrad[kind, who, at, :].astype(F32) * here
                    value = term if value is None else value + term
                if source % NY == 0:
                    base[source // NY, kind, rows, :] += value
                else:
                    spare[source, kind, rows, :] = value.astype(BF16)
        chain, offset = source // NY, source % NY
        if offset:
            index = offset - 1 if offset < 4 else offset
            send(spare.at[source], parts[3 + chain] if offset == 4 else parts[index].at[chain])
    send(base, outputs[2])
    for copy in copies:
        copy.wait()


def attend(pos, far_own, far_peer, qdo_own, qdo_peer, glob, arrays):
    smem = pl.BlockSpec(memory_space=pltpu.SMEM)
    vmem = pl.BlockSpec(memory_space=pltpu.VMEM)
    anywhere = pl.BlockSpec(memory_space=pl.ANY)
    piece = jax.ShapeDtypeStruct((2, TOK, HALF), BF16)
    double = jax.ShapeDtypeStruct((2, 2, TOK, HALF), BF16)
    return pl.pallas_call(
        attend_kernel,
        out_shape=[
            piece,
            piece,
            jax.ShapeDtypeStruct((2, 2, TOK, HALF), F32),
            jax.ShapeDtypeStruct((WINDOWS, GROWS, HEAD_DIM), BF16),
        ]
        + [double] * 3
        + [piece] * 2
        + [double] * 3,
        in_specs=[smem] * 3 + [vmem] * 3 + [anywhere] * 9,
        out_specs=[anywhere] * 12,
        scratch_shapes=[
            pltpu.VMEM((2, 2, BLK * FKEYS, HALF), BF16),
            pltpu.VMEM((2, 2, NEAR, HALF), BF16),
            pltpu.VMEM((2, 2, BLK * FKEYS, HALF), BF16),
            pltpu.VMEM((WINDOWS * GROWS, HEAD_DIM), F32),
            pltpu.VMEM((2, TOK, HALF), BF16),
            pltpu.VMEM((2, TOK, HALF), BF16),
            pltpu.VMEM((2, 2, TOK, HALF), F32),
            pltpu.VMEM((WINDOWS, GROWS, HEAD_DIM), BF16),
            pltpu.VMEM((2 * NY, 2, TOK, HALF), BF16),
            pltpu.SMEM((2, 2 * NY), jnp.int32),
            pltpu.SemaphoreType.DMA((2 + 4 * NY,)),
            pltpu.SemaphoreType.DMA((2 + 2 * NY,)),
        ],
        compiler_params=pltpu.CompilerParams(vmem_limit_bytes=60 * 1024 * 1024),
        cost_estimate=pl.CostEstimate(
            flops=1_200_000_000, bytes_accessed=12_000_000, transcendentals=800_000
        ),
    )(pos, far_own, far_peer, qdo_own, qdo_peer, glob, *arrays)


UP = [(i, (i + 1) % NY) for i in range(NY)]
DOWN = [(i, (i - 1) % NY) for i in range(NY)]
SWAP = [(0, 1), (1, 0)]


def plus(a, b):
    return (a.astype(F32) + b.astype(F32)).astype(BF16)


def per_device(query_rows, key_rows, value_rows, out_grad, far_blocks):
    my_y = lax.axis_index("y")
    my_c = lax.axis_index("c")
    my_w = lax.axis_index("x") * NZ + lax.axis_index("z")
    swap = functools.partial(lax.ppermute, axis_name="c", perm=SWAP)
    up = functools.partial(lax.ppermute, axis_name="y", perm=UP)
    down = functools.partial(lax.ppermute, axis_name="y", perm=DOWN)
    low = my_c == 0

    def split(first, second):
        mine = [jnp.where(low, a[:, :HALF], a[:, HALF:]) for a in (first, second)]
        other = [jnp.where(low, a[:, HALF:], a[:, :HALF]) for a in (first, second)]
        return jnp.stack(mine), jnp.stack(other)

    kv_own, kv_send = split(key_rows, value_rows)
    qdo_own, qdo_send = split(query_rows, out_grad)
    kv_peer = swap(kv_send)
    row = jnp.concatenate([kv_own[:, 0], kv_peer[:, 0]]).reshape(GROWS, HEAD_DIM)
    ring = [None] * NY
    ring[0] = jnp.stack([kv_own, kv_peer])
    ring[7], ring[1] = up(ring[0]), down(ring[0])
    row, ring[7], ring[1] = lax.optimization_barrier((row, ring[7], ring[1]))
    glob = lax.all_to_all(
        jnp.broadcast_to(row, (WINDOWS, GROWS, HEAD_DIM)), ("x", "z"), 0, 0, tiled=True
    )
    ring[6], ring[2] = up(ring[7]), down(ring[1])
    qdo_peer = swap(qdo_send)
    far_peer = swap(far_blocks)
    ring[5], ring[3] = up(ring[6]), down(ring[2])
    glob, ring[5], ring[3] = lax.optimization_barrier((glob, ring[5], ring[3]))
    across = up(ring[5][0]), down(ring[3][1])
    pos = jnp.stack([my_y, my_c, my_w]).astype(jnp.int32)
    arrays = [*ring[:4], *across, *ring[5:]]
    res_own, res_peer, base, gglob, *parts = attend(
        pos, far_blocks, far_peer, qdo_own, qdo_peer, glob, arrays
    )
    rise, fall = up(parts[3]), down(parts[4])
    rise = jnp.stack([plus(parts[2][0], rise), parts[2][1]])
    fall = jnp.stack([parts[5][0], plus(parts[5][1], fall)])
    rise, fall = up(rise), down(fall)
    gglob, rise, fall = lax.optimization_barrier((gglob, rise, fall))
    gback = lax.all_to_all(gglob, ("x", "z"), 0, 0, tiled=True)
    rise, fall = plus(parts[1], rise), plus(parts[6], fall)
    rise, fall = up(rise), down(fall)
    rise, fall = plus(parts[0], rise), plus(parts[7], fall)
    rise, fall = up(rise), down(fall)
    gsum = jnp.sum(gback.astype(F32), axis=0).reshape(2, 2, 1, HALF)
    res_back = swap(res_peer)
    first_row = lax.broadcasted_iota(jnp.int32, (1, TOK, 1), 1) == 0

    def finish(who):
        total = base[who] + rise[who].astype(F32) + fall[who].astype(F32)
        return (total + jnp.where(first_row, gsum[who], 0.0)).astype(BF16)

    peer_grad = swap(finish(1))
    own_grad = finish(0)

    def join(mine, other):
        return jnp.where(
            low,
            jnp.concatenate([mine, other], axis=1),
            jnp.concatenate([other, mine], axis=1),
        )

    return (
        join(res_own[0], res_back[0]),
        join(res_own[1], res_back[1]),
        join(own_grad[0], peer_grad[0]),
        join(own_grad[1], peer_grad[1]),
    )


def solution(mesh):
    fine = Mesh(mesh.devices.reshape(NX, NZ, NY, NC), ("x", "z", "y", "c"))
    spec = P(("y", "c", "x", "z"), None)
    return jax.shard_map(
        per_device, mesh=fine, in_specs=(spec,) * 5, out_specs=(spec,) * 4, check_vma=False
    )
```

```python
import functools
import math

import jax
import jax.numpy as jnp
from jax import lax
from jax.experimental import pallas as pl
from jax.experimental.pallas import tpu as pltpu
from jax.sharding import Mesh
from jax.sharding import PartitionSpec as P

HEAD_DIM = 128
BLOCK = 64
TOK = 128
BLK = 2
FAR = 8
NX, NZ, NY, NC = 4, 8, 8, 2
WINDOWS = NX * NZ
HALF = 512
HEADS = HALF // HEAD_DIM
NEAR = 256
GROWS = 4 * HEADS
SEND_ORDER = (4, 12, 11, 5, 3, 6, 10, 13, 2, 7, 9, 14, 1, 15, 8, 0)
FKEYS = FAR * BLOCK
SCALE = 1.0 / math.sqrt(HEAD_DIM)
EXP_SCALE = SCALE * math.log2(math.e)
BF16 = jnp.bfloat16
F32 = jnp.float32


def dot_nt(a, b):
    return lax.dot_general(a, b, (((1,), (1,)), ((), ())), preferred_element_type=F32)


def dot_nn(a, b):
    return lax.dot_general(a, b, (((1,), (0,)), ((), ())), preferred_element_type=F32)


def dot_tn(a, b):
    return lax.dot_general(a, b, (((0,), (0,)), ((), ())), preferred_element_type=F32)


def attend_kernel(*refs):
    pos, far_own, far_peer, qdo_own, qdo_peer, glob = refs[:6]
    sources = refs[6:22]
    outputs = refs[22:26]
    parts = refs[26:40]
    slots, near, fgrad, gwide, res_own, res_peer, base, gglob, spare, table, in_sem, out_sem = refs[40:]
    my_y, my_c = pos[0], pos[1]
    for who, far in enumerate((far_own, far_peer)):
        for row in range(BLK):
            for entry in range(FAR):
                block = far[row, entry]
                group = lax.shift_right_logical(block, 6)
                offset = lax.bitwise_and(
                    lax.shift_right_logical(group, 1) - my_y, NY - 1
                )
                chain = lax.bitwise_xor(lax.bitwise_and(group, 1), my_c)
                inner = lax.bitwise_and(block, 1)
                table[who, chain * NY + offset] = (row * FAR + entry) * 2 + inner
    copies = []
    for who in range(2):
        copies.append(
            pltpu.make_async_copy(
                sources[who * NY], near.at[:, who, :TOK, :], in_sem.at[len(copies)]
            )
        )
    for source in range(2 * NY):
        for who in range(2):
            code = table[who, source]
            slot = lax.shift_right_logical(code, 1)
            inner = lax.bitwise_and(code, 1)
            at = pl.ds(pl.multiple_of(slot * BLOCK, BLOCK), BLOCK)
            rows = pl.ds(pl.multiple_of(inner * BLOCK, BLOCK), BLOCK)
            copies.append(
                pltpu.make_async_copy(
                    sources[source].at[:, rows, :],
                    slots.at[:, who, at, :],
                    in_sem.at[len(copies)],
                )
            )
    for copy in copies:
        copy.start()
    gwide[...] = glob[...].astype(F32).reshape(WINDOWS * GROWS, HEAD_DIM)
    for who in range(2):
        for kind in range(2):
            for head in range(HEADS):
                first = (who * 2 + kind) * HEADS + head
                near[kind, who, TOK : TOK + WINDOWS, head * HEAD_DIM : (head + 1) * HEAD_DIM] = (
                    gwide[pl.ds(first, WINDOWS, stride=GROWS), :].astype(BF16)
                )
            near[kind, who, TOK + WINDOWS :, :] = jnp.zeros((NEAR - TOK - WINDOWS, HALF), BF16)
    column = lax.broadcasted_iota(jnp.int32, (TOK, NEAR), 1)
    hidden = (column >= TOK + WINDOWS) | (column == TOK)
    for copy in copies:
        copy.wait()

    def head_step(head, carry):
        lanes = pl.ds(pl.multiple_of(head * HEAD_DIM, HEAD_DIM), HEAD_DIM)
        both = range(2)
        pairs = [(who, row) for who in both for row in range(BLK)]
        rows = [slice(row * BLOCK, (row + 1) * BLOCK) for row in range(BLK)]
        keys = [slice(row * FKEYS, (row + 1) * FKEYS) for row in range(BLK)]
        res = res_own, res_peer
        query = [qdo[0, :, lanes] for qdo in (qdo_own, qdo_peer)]
        grad = [qdo[1, :, lanes] for qdo in (qdo_own, qdo_peer)]
        near_score = [
            jnp.where(hidden, -1e30, dot_nt(query[who], near[0, who, :, lanes])) for who in both
        ]
        far_score = [
            dot_nt(query[who][rows[row]], slots[0, who, keys[row], lanes]) for who, row in pairs
        ]
        near_dprod = [dot_nt(grad[who], near[1, who, :, lanes]) for who in both]
        far_dprod = [
            dot_nt(grad[who][rows[row]], slots[1, who, keys[row], lanes]) for who, row in pairs
        ]
        near_weight, far_weight, near_half, far_half = [], [], [], []
        for i, (who, row) in enumerate(pairs):
            ns = near_score[who][rows[row]]
            top = jnp.maximum(
                jnp.max(ns, axis=1, keepdims=True), jnp.max(far_score[i], axis=1, keepdims=True)
            )
            near_exp = jnp.exp2((ns - top) * EXP_SCALE)
            far_exp = jnp.exp2((far_score[i] - top) * EXP_SCALE)
            inverse = 1.0 / (
                jnp.sum(near_exp, axis=1, keepdims=True) + jnp.sum(far_exp, axis=1, keepdims=True)
            )
            near_weight.append(near_exp * inverse)
            far_weight.append(far_exp * inverse)
            near_half.append(near_weight[i].astype(BF16))
            far_half.append(far_weight[i].astype(BF16))
        delta = []
        for i, (who, row) in enumerate(pairs):
            out = dot_nn(near_half[i], near[1, who, :, lanes])
            out = (out + dot_nn(far_half[i], slots[1, who, keys[row], lanes])).astype(BF16)
            res[who][0, rows[row], lanes] = out
            g = grad[who][rows[row]]
            delta.append(jnp.sum(g.astype(F32) * out.astype(F32), axis=1, keepdims=True))
        for i, (who, row) in enumerate(pairs):
            g = grad[who][rows[row]]
            fgrad[1, who, keys[row], lanes] = dot_tn(far_half[i], g).astype(BF16)
        near_dscore, far_dscore = [], []
        for i, (who, row) in enumerate(pairs):
            nd = near_weight[i] * (near_dprod[who][rows[row]] - delta[i])
            near_dscore.append(nd.astype(BF16))
            far_dscore.append((far_weight[i] * (far_dprod[i] - delta[i])).astype(BF16))
        for i, (who, row) in enumerate(pairs):
            dq = dot_nn(near_dscore[i], near[0, who, :, lanes])
            dq = (dq + dot_nn(far_dscore[i], slots[0, who, keys[row], lanes])) * SCALE
            res[who][1, rows[row], lanes] = dq.astype(BF16)
        for i, (who, row) in enumerate(pairs):
            dk = dot_tn(far_dscore[i], query[who][rows[row]]) * SCALE
            fgrad[0, who, keys[row], lanes] = dk.astype(BF16)
        for who in both:
            two = slice(who * BLK, (who + 1) * BLK)
            near_kgrad = dot_tn(jnp.concatenate(near_dscore[two], axis=0), query[who]) * SCALE
            near_vgrad = dot_tn(jnp.concatenate(near_half[two], axis=0), grad[who])
            for kind, value in enumerate((near_kgrad, near_vgrad)):
                base[who, kind, :, lanes] = value[:TOK]
                first = (who * 2 + kind) * HEADS + head
                gwide[pl.ds(first, WINDOWS, stride=GROWS), :] = value[TOK : TOK + WINDOWS]
        return carry

    lax.fori_loop(0, HEADS, head_step, 0)
    gglob[...] = gwide[...].reshape(WINDOWS, GROWS, HEAD_DIM).astype(BF16)
    copies = []

    def send(value, output):
        copy = pltpu.make_async_copy(value, output, out_sem.at[len(copies)])
        copy.start()
        copies.append(copy)

    send(gglob, outputs[3])
    send(res_peer, outputs[1])
    send(res_own, outputs[0])
    for source in SEND_ORDER:
        for kind in range(2):
            for inner in range(BLK):
                rows = slice(inner * BLOCK, (inner + 1) * BLOCK)
                value = None
                for who in range(2):
                    code = table[who, source]
                    slot = lax.shift_right_logical(code, 1)
                    at = pl.ds(pl.multiple_of(slot * BLOCK, BLOCK), BLOCK)
                    here = (lax.bitwise_and(code, 1) == inner).astype(F32)
                    term = fgrad[kind, who, at, :].astype(F32) * here
                    value = term if value is None else value + term
                if source % NY == 0:
                    base[source // NY, kind, rows, :] += value
                else:
                    spare[source, kind, rows, :] = value.astype(BF16)
        if source % NY:
            send(spare.at[source], parts[source - 1 - source // NY])
    send(base, outputs[2])
    for copy in copies:
        copy.wait()


def attend(pos, far_own, far_peer, qdo_own, qdo_peer, glob, sources):
    smem = pl.BlockSpec(memory_space=pltpu.SMEM)
    vmem = pl.BlockSpec(memory_space=pltpu.VMEM)
    anywhere = pl.BlockSpec(memory_space=pl.ANY)
    piece = jax.ShapeDtypeStruct((2, TOK, HALF), BF16)
    return pl.pallas_call(
        attend_kernel,
        out_shape=[
            piece,
            piece,
            jax.ShapeDtypeStruct((2, 2, TOK, HALF), F32),
            jax.ShapeDtypeStruct((WINDOWS, GROWS, HEAD_DIM), BF16),
        ]
        + [piece] * 14,
        in_specs=[smem] * 3 + [vmem] * 3 + [anywhere] * 16,
        out_specs=[anywhere] * 18,
        scratch_shapes=[
            pltpu.VMEM((2, 2, BLK * FKEYS, HALF), BF16),
            pltpu.VMEM((2, 2, NEAR, HALF), BF16),
            pltpu.VMEM((2, 2, BLK * FKEYS, HALF), BF16),
            pltpu.VMEM((WINDOWS * GROWS, HEAD_DIM), F32),
            pltpu.VMEM((2, TOK, HALF), BF16),
            pltpu.VMEM((2, TOK, HALF), BF16),
            pltpu.VMEM((2, 2, TOK, HALF), F32),
            pltpu.VMEM((WINDOWS, GROWS, HEAD_DIM), BF16),
            pltpu.VMEM((2 * NY, 2, TOK, HALF), BF16),
            pltpu.SMEM((2, 2 * NY), jnp.int32),
            pltpu.SemaphoreType.DMA((2 + 4 * NY,)),
            pltpu.SemaphoreType.DMA((2 + 2 * NY,)),
        ],
        compiler_params=pltpu.CompilerParams(vmem_limit_bytes=60 * 1024 * 1024),
        cost_estimate=pl.CostEstimate(
            flops=1_200_000_000, bytes_accessed=12_000_000, transcendentals=800_000
        ),
    )(pos, far_own, far_peer, qdo_own, qdo_peer, glob, *sources)


UP = [(i, (i + 1) % NY) for i in range(NY)]
DOWN = [(i, (i - 1) % NY) for i in range(NY)]
SPREAD = ((0, 1), (2, 3), (4,))
SWAP = [(0, 1), (1, 0)]


def plus(a, b):
    return (a.astype(F32) + b.astype(F32)).astype(BF16)


def flip(rows, bit):
    axis, size, step = ("z", NZ, 1 << bit) if bit < 3 else ("x", NX, 1 << (bit - 3))
    return lax.ppermute(rows, axis, [(i, i ^ step) for i in range(size)])


def per_device(query_rows, key_rows, value_rows, out_grad, far_blocks):
    my_y = lax.axis_index("y")
    my_c = lax.axis_index("c")
    swap = functools.partial(lax.ppermute, axis_name="c", perm=SWAP)
    up = functools.partial(lax.ppermute, axis_name="y", perm=UP)
    down = functools.partial(lax.ppermute, axis_name="y", perm=DOWN)
    low = my_c == 0

    def split(first, second):
        mine = [jnp.where(low, a[:, :HALF], a[:, HALF:]) for a in (first, second)]
        other = [jnp.where(low, a[:, HALF:], a[:, :HALF]) for a in (first, second)]
        return jnp.stack(mine), jnp.stack(other)

    kv_own, kv_send = split(key_rows, value_rows)
    qdo_own, qdo_send = split(query_rows, out_grad)
    kv_peer = swap(kv_send)
    sources = [None] * 16
    sources[0], sources[NY] = kv_own, kv_peer
    glob = jnp.concatenate([kv_own[:, 0], kv_peer[:, 0]]).reshape(1, GROWS, HEAD_DIM)
    chains = ((0, up, 4, -1), (0, down, 3, 1), (NY, up, 3, -1), (NY, down, 4, 1))
    held = [kv_own, kv_own, kv_peer, kv_peer]
    for step in range(1, 5):
        for i, (first, move, count, sign) in enumerate(chains):
            if step <= count:
                held[i] = move(held[i])
        if step <= 3:
            glob, held[0] = lax.optimization_barrier((glob, held[0]))
            for bit in SPREAD[step - 1]:
                glob = jnp.concatenate([glob, flip(glob, bit)])
        if step == 1:
            qdo_peer = swap(qdo_send)
            far_peer = swap(far_blocks)
        if step == 3:
            glob, qdo_peer, far_peer, held[3] = lax.optimization_barrier(
                (glob, qdo_peer, far_peer, held[3])
            )
        for i, (first, move, count, sign) in enumerate(chains):
            if step <= count:
                sources[first + (sign * step) % NY] = held[i]
    pos = jnp.stack([my_y, my_c]).astype(jnp.int32)
    res_own, res_peer, base, gglob, *parts = attend(
        pos, far_blocks, far_peer, qdo_own, qdo_peer, glob, sources
    )
    part = parts[:7], parts[7:]
    at = [4, 5, 3, 4]
    held = [part[first // NY][o - 1] for o, (first, _, _, _) in zip(at, chains)]
    for step in range(1, 5):
        for i, (first, move, count, sign) in enumerate(chains):
            if step <= count:
                held[i] = move(held[i])
        if step <= 3:
            gglob, held[0] = lax.optimization_barrier((gglob, held[0]))
            for bit in reversed(SPREAD[3 - step]):
                rows = 1 << bit
                gglob = gglob[:rows].astype(F32) + flip(gglob[rows:], bit).astype(F32)
                gglob = gglob.astype(BF16) if bit else gglob
        for i, (first, move, count, sign) in enumerate(chains):
            if step <= count:
                at[i] = (at[i] + sign) % NY
                if at[i]:
                    held[i] = plus(held[i], part[first // NY][at[i] - 1])
    far_own, far_peer = held[:2], held[2:]
    gsum = gglob.reshape(2, 2, 1, HALF)
    res_back = swap(res_peer)
    first_row = lax.broadcasted_iota(jnp.int32, (1, TOK, 1), 1) == 0

    def finish(who, far):
        total = base[who] + far[0].astype(F32) + far[1].astype(F32)
        return (total + jnp.where(first_row, gsum[who], 0.0)).astype(BF16)

    peer_grad = swap(finish(1, far_peer))
    own_grad = finish(0, far_own)

    def join(mine, other):
        return jnp.where(
            low,
            jnp.concatenate([mine, other], axis=1),
            jnp.concatenate([other, mine], axis=1),
        )

    return (
        join(res_own[0], res_back[0]),
        join(res_own[1], res_back[1]),
        join(own_grad[0], peer_grad[0]),
        join(own_grad[1], peer_grad[1]),
    )


def solution(mesh):
    fine = Mesh(mesh.devices.reshape(NX, NZ, NY, NC), ("x", "z", "y", "c"))
    spec = P(("y", "c", "x", "z"), None)
    return jax.shard_map(
        per_device, mesh=fine, in_specs=(spec,) * 5, out_specs=(spec,) * 4, check_vma=False
    )
```

```python
import functools
import math

import jax
import jax.numpy as jnp
from jax import lax
from jax.experimental import pallas as pl
from jax.experimental.pallas import tpu as pltpu
from jax.sharding import Mesh
from jax.sharding import PartitionSpec as P

HEAD_DIM = 128
BLOCK = 64
TOK = 128
BLK = 2
FAR = 8
NX, NZ, NY, NC = 4, 8, 8, 2
WINDOWS = NX * NZ
HALF = 512
HEADS = HALF // HEAD_DIM
NEAR = 256
GROWS = 4 * HEADS
SEND_ORDER = tuple(range(NY)) + (12, 13, 11, 14, 10, 15, 9, 8)
FKEYS = FAR * BLOCK
SCALE = 1.0 / math.sqrt(HEAD_DIM)
EXP_SCALE = SCALE * math.log2(math.e)
BF16 = jnp.bfloat16
F32 = jnp.float32


def dot_nt(a, b):
    return lax.dot_general(a, b, (((1,), (1,)), ((), ())), preferred_element_type=F32)


def dot_nn(a, b):
    return lax.dot_general(a, b, (((1,), (0,)), ((), ())), preferred_element_type=F32)


def dot_tn(a, b):
    return lax.dot_general(a, b, (((0,), (0,)), ((), ())), preferred_element_type=F32)


def attend_kernel(*refs):
    pos, far_own, far_peer, qdo_own, qdo_peer, glob = refs[:6]
    gathered = refs[6]
    ring = refs[7:15]
    outputs = refs[15:20]
    scattered = refs[20]
    parts = refs[21:28]
    slots, near, fgrad, gwide, res_own, res_peer, base, gglob, spare, table, in_sem, out_sem = refs[28:]
    sources = [gathered.at[y] for y in range(NY)] + list(ring)
    my_y, my_c, my_w = pos[0], pos[1], pos[2]
    for who, far in enumerate((far_own, far_peer)):
        for row in range(BLK):
            for entry in range(FAR):
                block = far[row, entry]
                group = lax.shift_right_logical(block, 6)
                chain = lax.bitwise_xor(lax.bitwise_and(group, 1), my_c)
                offset = lax.bitwise_and(
                    lax.shift_right_logical(group, 1) - my_y * chain, NY - 1
                )
                inner = lax.bitwise_and(block, 1)
                table[who, chain * NY + offset] = (row * FAR + entry) * 2 + inner
    copies = []
    for who in range(2):
        copies.append(
            pltpu.make_async_copy(
                ring[0] if who else gathered.at[my_y],
                near.at[:, who, :TOK, :],
                in_sem.at[len(copies)],
            )
        )
    for source in range(2 * NY):
        for who in range(2):
            code = table[who, source]
            slot = lax.shift_right_logical(code, 1)
            inner = lax.bitwise_and(code, 1)
            at = pl.ds(pl.multiple_of(slot * BLOCK, BLOCK), BLOCK)
            rows = pl.ds(pl.multiple_of(inner * BLOCK, BLOCK), BLOCK)
            copies.append(
                pltpu.make_async_copy(
                    sources[source].at[:, rows, :],
                    slots.at[:, who, at, :],
                    in_sem.at[len(copies)],
                )
            )
    for copy in copies:
        copy.start()
    gwide[...] = glob[...].astype(F32).reshape(WINDOWS * GROWS, HEAD_DIM)
    for who in range(2):
        for kind in range(2):
            for head in range(HEADS):
                first = (who * 2 + kind) * HEADS + head
                near[kind, who, TOK : TOK + WINDOWS, head * HEAD_DIM : (head + 1) * HEAD_DIM] = (
                    gwide[pl.ds(first, WINDOWS, stride=GROWS), :].astype(BF16)
                )
            near[kind, who, TOK + WINDOWS :, :] = jnp.zeros((NEAR - TOK - WINDOWS, HALF), BF16)
    column = lax.broadcasted_iota(jnp.int32, (TOK, NEAR), 1)
    hidden = (column >= TOK + WINDOWS) | (column == TOK + my_w)
    for copy in copies:
        copy.wait()

    def head_step(head, carry):
        lanes = pl.ds(pl.multiple_of(head * HEAD_DIM, HEAD_DIM), HEAD_DIM)
        both = range(2)
        pairs = [(who, row) for who in both for row in range(BLK)]
        rows = [slice(row * BLOCK, (row + 1) * BLOCK) for row in range(BLK)]
        keys = [slice(row * FKEYS, (row + 1) * FKEYS) for row in range(BLK)]
        res = res_own, res_peer
        query = [qdo[0, :, lanes] for qdo in (qdo_own, qdo_peer)]
        grad = [qdo[1, :, lanes] for qdo in (qdo_own, qdo_peer)]
        near_score = [
            jnp.where(hidden, -1e30, dot_nt(query[who], near[0, who, :, lanes])) for who in both
        ]
        far_score = [
            dot_nt(query[who][rows[row]], slots[0, who, keys[row], lanes]) for who, row in pairs
        ]
        near_dprod = [dot_nt(grad[who], near[1, who, :, lanes]) for who in both]
        far_dprod = [
            dot_nt(grad[who][rows[row]], slots[1, who, keys[row], lanes]) for who, row in pairs
        ]
        near_weight, far_weight, near_half, far_half = [], [], [], []
        for i, (who, row) in enumerate(pairs):
            ns = near_score[who][rows[row]]
            top = jnp.maximum(
                jnp.max(ns, axis=1, keepdims=True), jnp.max(far_score[i], axis=1, keepdims=True)
            )
            near_exp = jnp.exp2((ns - top) * EXP_SCALE)
            far_exp = jnp.exp2((far_score[i] - top) * EXP_SCALE)
            inverse = 1.0 / (
                jnp.sum(near_exp, axis=1, keepdims=True) + jnp.sum(far_exp, axis=1, keepdims=True)
            )
            near_weight.append(near_exp * inverse)
            far_weight.append(far_exp * inverse)
            near_half.append(near_weight[i].astype(BF16))
            far_half.append(far_weight[i].astype(BF16))
        delta = []
        for i, (who, row) in enumerate(pairs):
            out = dot_nn(near_half[i], near[1, who, :, lanes])
            out = (out + dot_nn(far_half[i], slots[1, who, keys[row], lanes])).astype(BF16)
            res[who][0, rows[row], lanes] = out
            g = grad[who][rows[row]]
            delta.append(jnp.sum(g.astype(F32) * out.astype(F32), axis=1, keepdims=True))
        for i, (who, row) in enumerate(pairs):
            g = grad[who][rows[row]]
            fgrad[1, who, keys[row], lanes] = dot_tn(far_half[i], g).astype(BF16)
        near_dscore, far_dscore = [], []
        for i, (who, row) in enumerate(pairs):
            nd = near_weight[i] * (near_dprod[who][rows[row]] - delta[i])
            near_dscore.append(nd.astype(BF16))
            far_dscore.append((far_weight[i] * (far_dprod[i] - delta[i])).astype(BF16))
        for i, (who, row) in enumerate(pairs):
            dq = dot_nn(near_dscore[i], near[0, who, :, lanes])
            dq = (dq + dot_nn(far_dscore[i], slots[0, who, keys[row], lanes])) * SCALE
            res[who][1, rows[row], lanes] = dq.astype(BF16)
        for i, (who, row) in enumerate(pairs):
            dk = dot_tn(far_dscore[i], query[who][rows[row]]) * SCALE
            fgrad[0, who, keys[row], lanes] = dk.astype(BF16)
        for who in both:
            two = slice(who * BLK, (who + 1) * BLK)
            near_kgrad = dot_tn(jnp.concatenate(near_dscore[two], axis=0), query[who]) * SCALE
            near_vgrad = dot_tn(jnp.concatenate(near_half[two], axis=0), grad[who])
            for kind, value in enumerate((near_kgrad, near_vgrad)):
                base[who, kind, :, lanes] = value[:TOK]
                first = (who * 2 + kind) * HEADS + head
                gwide[pl.ds(first, WINDOWS, stride=GROWS), :] = value[TOK : TOK + WINDOWS]
        return carry

    lax.fori_loop(0, HEADS, head_step, 0)
    gglob[...] = gwide[...].reshape(WINDOWS, GROWS, HEAD_DIM).astype(BF16)
    copies = []

    def send(value, output):
        copy = pltpu.make_async_copy(value, output, out_sem.at[len(copies)])
        copy.start()
        copies.append(copy)

    send(gglob, outputs[4])
    send(res_peer, outputs[1])
    send(res_own, outputs[0])
    for source in SEND_ORDER:
        for kind in range(2):
            for inner in range(BLK):
                rows = slice(inner * BLOCK, (inner + 1) * BLOCK)
                value = None
                for who in range(2):
                    code = table[who, source]
                    slot = lax.shift_right_logical(code, 1)
                    at = pl.ds(pl.multiple_of(slot * BLOCK, BLOCK), BLOCK)
                    here = (lax.bitwise_and(code, 1) == inner).astype(F32)
                    term = fgrad[kind, who, at, :].astype(F32) * here
                    value = term if value is None else value + term
                if source == NY:
                    base[1, kind, rows, :] += value
                else:
                    spare[source, kind, rows, :] = value.astype(BF16)
        if source != NY:
            part = scattered.at[source] if source < NY else parts[source - NY - 1]
            send(spare.at[source], part)
    send(base.at[1], outputs[3])
    send(base.at[0], outputs[2])
    for copy in copies:
        copy.wait()


def cut_kernel(core, *refs):
    inputs, outputs = refs[:4], refs[4:]
    for half in range(2):
        first = lax.bitwise_xor(core[0], half) * HALF
        columns = pl.ds(pl.multiple_of(first, HALF), HALF)
        for i in range(4):
            outputs[i // 2 * 2 + half][i % 2] = inputs[i][:, columns]


def cut(core, *inputs):
    vmem = pl.BlockSpec(memory_space=pltpu.VMEM)
    return pl.pallas_call(
        cut_kernel,
        out_shape=[jax.ShapeDtypeStruct((2, TOK, HALF), BF16)] * 4,
        in_specs=[pl.BlockSpec(memory_space=pltpu.SMEM)] + [vmem] * 4,
        out_specs=[vmem] * 4,
        cost_estimate=pl.CostEstimate(flops=0, bytes_accessed=2_000_000, transcendentals=0),
    )(core.astype(jnp.int32)[None], *inputs)


def attend(pos, far_own, far_peer, qdo_own, qdo_peer, glob, gathered, ring):
    smem = pl.BlockSpec(memory_space=pltpu.SMEM)
    vmem = pl.BlockSpec(memory_space=pltpu.VMEM)
    anywhere = pl.BlockSpec(memory_space=pl.ANY)
    piece = jax.ShapeDtypeStruct((2, TOK, HALF), BF16)
    return pl.pallas_call(
        attend_kernel,
        out_shape=[
            piece,
            piece,
            jax.ShapeDtypeStruct((2, TOK, HALF), F32),
            jax.ShapeDtypeStruct((2, TOK, HALF), F32),
            jax.ShapeDtypeStruct((WINDOWS, GROWS, HEAD_DIM), BF16),
        ]
        + [jax.ShapeDtypeStruct((NY, 2, TOK, HALF), BF16)]
        + [piece] * 7,
        in_specs=[smem] * 3 + [vmem] * 3 + [anywhere] * 9,
        out_specs=[anywhere] * 13,
        scratch_shapes=[
            pltpu.VMEM((2, 2, BLK * FKEYS, HALF), BF16),
            pltpu.VMEM((2, 2, NEAR, HALF), BF16),
            pltpu.VMEM((2, 2, BLK * FKEYS, HALF), BF16),
            pltpu.VMEM((WINDOWS * GROWS, HEAD_DIM), F32),
            pltpu.VMEM((2, TOK, HALF), BF16),
            pltpu.VMEM((2, TOK, HALF), BF16),
            pltpu.VMEM((2, 2, TOK, HALF), F32),
            pltpu.VMEM((WINDOWS, GROWS, HEAD_DIM), BF16),
            pltpu.VMEM((2 * NY, 2, TOK, HALF), BF16),
            pltpu.SMEM((2, 2 * NY), jnp.int32),
            pltpu.SemaphoreType.DMA((2 + 4 * NY,)),
            pltpu.SemaphoreType.DMA((5 + 2 * NY,)),
        ],
        compiler_params=pltpu.CompilerParams(vmem_limit_bytes=60 * 1024 * 1024),
        cost_estimate=pl.CostEstimate(
            flops=1_200_000_000, bytes_accessed=12_000_000, transcendentals=800_000
        ),
    )(pos, far_own, far_peer, qdo_own, qdo_peer, glob, gathered, *ring)


UP = [(i, (i + 1) % NY) for i in range(NY)]
DOWN = [(i, (i - 1) % NY) for i in range(NY)]
ROW_STEP, BACK_STEP = 1, 2
SWAP = [(0, 1), (1, 0)]


def plus(a, b):
    return (a.astype(F32) + b.astype(F32)).astype(BF16)


def per_device(query_rows, key_rows, value_rows, out_grad, far_blocks):
    my_y = lax.axis_index("y")
    my_c = lax.axis_index("c")
    my_w = lax.axis_index("x") * NZ + lax.axis_index("z")
    swap = functools.partial(lax.ppermute, axis_name="c", perm=SWAP)
    up = functools.partial(lax.ppermute, axis_name="y", perm=UP)
    down = functools.partial(lax.ppermute, axis_name="y", perm=DOWN)
    low = my_c == 0

    kv_own, kv_send, qdo_own, qdo_send = cut(my_c, key_rows, value_rows, query_rows, out_grad)
    gathered = lax.all_gather(kv_own, "y", axis=0)
    kv_peer = swap(kv_send)
    ring = [kv_peer] + [None] * (NY - 1)
    row = jnp.concatenate([kv_own[:, 0], kv_peer[:, 0]]).reshape(GROWS, HEAD_DIM)
    chains = ((up, 4, -1), (down, 3, 1))
    held = [kv_peer, kv_peer]
    for step in range(1, 5):
        for i, (move, count, sign) in enumerate(chains):
            if step <= count:
                held[i] = move(held[i])
        if step == ROW_STEP:
            row, held[0] = lax.optimization_barrier((row, held[0]))
            glob = lax.all_to_all(
                jnp.broadcast_to(row, (WINDOWS, GROWS, HEAD_DIM)), ("x", "z"), 0, 0, tiled=True
            )
            qdo_peer = swap(qdo_send)
            far_peer = swap(far_blocks)
        if step == 2:
            glob, held[1] = lax.optimization_barrier((glob, held[1]))
        if step == 3:
            qdo_peer, far_peer, held[0] = lax.optimization_barrier((qdo_peer, far_peer, held[0]))
        for i, (move, count, sign) in enumerate(chains):
            if step <= count:
                ring[(sign * step) % NY] = held[i]
    pos = jnp.stack([my_y, my_c, my_w]).astype(jnp.int32)
    res_own, res_peer, base_own, base_peer, gglob, scattered, *parts = attend(
        pos, far_blocks, far_peer, qdo_own, qdo_peer, glob, gathered, ring
    )
    far_own = (lax.psum_scatter(scattered, "y", scatter_dimension=0),)
    at = [4, 5]
    held = [parts[o - 1] for o in at]
    for step in range(1, 5):
        for i, (move, count, sign) in enumerate(chains):
            if step <= count:
                held[i] = move(held[i])
        if step == BACK_STEP:
            gglob, held[0] = lax.optimization_barrier((gglob, held[0]))
            gback = lax.all_to_all(gglob, ("x", "z"), 0, 0, tiled=True)
        for i, (move, count, sign) in enumerate(chains):
            if step <= count:
                at[i] = (at[i] + sign) % NY
                if at[i]:
                    held[i] = plus(held[i], parts[at[i] - 1])
    far_peer = held
    gsum = jnp.sum(gback.astype(F32), axis=0).reshape(2, 2, 1, HALF)
    res_back = swap(res_peer)
    first_row = lax.broadcasted_iota(jnp.int32, (1, TOK, 1), 1) == 0

    def finish(base, far, who):
        total = base + sum(term.astype(F32) for term in far)
        return (total + jnp.where(first_row, gsum[who], 0.0)).astype(BF16)

    peer_grad = finish(base_peer, far_peer, 1)
    base_own, _ = lax.optimization_barrier((base_own, peer_grad))
    peer_grad = swap(peer_grad)
    own_grad = finish(base_own, far_own, 0)

    def join(mine, other):
        return jnp.where(
            low,
            jnp.concatenate([mine, other], axis=1),
            jnp.concatenate([other, mine], axis=1),
        )

    return (
        join(res_own[0], res_back[0]),
        join(res_own[1], res_back[1]),
        join(own_grad[0], peer_grad[0]),
        join(own_grad[1], peer_grad[1]),
    )


def solution(mesh):
    fine = Mesh(mesh.devices.reshape(NX, NZ, NY, NC), ("x", "z", "y", "c"))
    spec = P(("y", "c", "x", "z"), None)
    return jax.shard_map(
        per_device, mesh=fine, in_specs=(spec,) * 5, out_specs=(spec,) * 4, check_vma=False
    )
```

```python
import functools
import math

import jax
import jax.numpy as jnp
from jax import lax
from jax.experimental import pallas as pl
from jax.experimental.pallas import tpu as pltpu
from jax.sharding import Mesh
from jax.sharding import PartitionSpec as P

HEAD_DIM = 128
BLOCK = 64
TOK = 128
BLK = 2
FAR = 8
NX, NZ, NY, NC = 4, 8, 8, 2
WINDOWS = NX * NZ
HALF = 512
HEADS = HALF // HEAD_DIM
NEAR = 256
GROWS = 4 * HEADS
SEND_ORDER = tuple(range(NY)) + (12, 13, 11, 14, 10, 15, 9, 8)
FKEYS = FAR * BLOCK
SCALE = 1.0 / math.sqrt(HEAD_DIM)
EXP_SCALE = SCALE * math.log2(math.e)
BF16 = jnp.bfloat16
F32 = jnp.float32


def dot_nt(a, b):
    return lax.dot_general(a, b, (((1,), (1,)), ((), ())), preferred_element_type=F32)


def dot_nn(a, b):
    return lax.dot_general(a, b, (((1,), (0,)), ((), ())), preferred_element_type=F32)


def dot_tn(a, b):
    return lax.dot_general(a, b, (((0,), (0,)), ((), ())), preferred_element_type=F32)


def attend_kernel(*refs):
    pos, far_own, far_peer, qdo_own, qdo_peer, glob = refs[:6]
    gathered = refs[6]
    ring = refs[7:15]
    outputs = refs[15:20]
    scattered = refs[20]
    parts = refs[21:28]
    slots, near, fgrad, gwide, res_own, res_peer, base, gglob, spare, table, in_sem, out_sem = refs[28:]
    my_y, my_c, my_w = pos[0], pos[1], pos[2]
    for who, far in enumerate((far_own, far_peer)):
        for row in range(BLK):
            for entry in range(FAR):
                block = far[row, entry]
                group = lax.shift_right_logical(block, 6)
                chain = lax.bitwise_xor(lax.bitwise_and(group, 1), my_c)
                offset = lax.bitwise_and(
                    lax.shift_right_logical(group, 1) - my_y * chain, NY - 1
                )
                inner = lax.bitwise_and(block, 1)
                table[who, chain * NY + offset] = (row * FAR + entry) * 2 + inner
    copies = []

    def fetch(value, output):
        copies.append(pltpu.make_async_copy(value, output, in_sem.at[len(copies)]))

    fetch(gathered.at[my_y, pl.ds(0, 2)], near.at[:, 0, :TOK, :])
    fetch(gathered.at[my_y, 2], near.at[0, 1, :TOK, :])
    fetch(ring[0], near.at[1, 1, :TOK, :])
    for source in range(2 * NY):
        for who in range(2):
            code = table[who, source]
            slot = lax.shift_right_logical(code, 1)
            inner = lax.bitwise_and(code, 1)
            at = pl.ds(pl.multiple_of(slot * BLOCK, BLOCK), BLOCK)
            rows = pl.ds(pl.multiple_of(inner * BLOCK, BLOCK), BLOCK)
            if source < NY:
                fetch(gathered.at[source, pl.ds(0, 2), rows, :], slots.at[:, who, at, :])
            else:
                their_y = lax.bitwise_and(my_y + (source - NY), NY - 1)
                fetch(gathered.at[their_y, 2, rows, :], slots.at[0, who, at, :])
                fetch(ring[source - NY].at[rows, :], slots.at[1, who, at, :])
    for copy in copies:
        copy.start()
    gwide[...] = glob[...].astype(F32).reshape(WINDOWS * GROWS, HEAD_DIM)
    for who in range(2):
        for kind in range(2):
            for head in range(HEADS):
                first = (who * 2 + kind) * HEADS + head
                near[kind, who, TOK : TOK + WINDOWS, head * HEAD_DIM : (head + 1) * HEAD_DIM] = (
                    gwide[pl.ds(first, WINDOWS, stride=GROWS), :].astype(BF16)
                )
            near[kind, who, TOK + WINDOWS :, :] = jnp.zeros((NEAR - TOK - WINDOWS, HALF), BF16)
    column = lax.broadcasted_iota(jnp.int32, (TOK, NEAR), 1)
    hidden = (column >= TOK + WINDOWS) | (column == TOK + my_w)
    for copy in copies:
        copy.wait()

    def head_step(head, carry):
        lanes = pl.ds(pl.multiple_of(head * HEAD_DIM, HEAD_DIM), HEAD_DIM)
        both = range(2)
        pairs = [(who, row) for who in both for row in range(BLK)]
        rows = [slice(row * BLOCK, (row + 1) * BLOCK) for row in range(BLK)]
        keys = [slice(row * FKEYS, (row + 1) * FKEYS) for row in range(BLK)]
        res = res_own, res_peer
        query = [qdo[0, :, lanes] for qdo in (qdo_own, qdo_peer)]
        grad = [qdo[1, :, lanes] for qdo in (qdo_own, qdo_peer)]
        near_score = [
            jnp.where(hidden, -1e30, dot_nt(query[who], near[0, who, :, lanes])) for who in both
        ]
        far_score = [
            dot_nt(query[who][rows[row]], slots[0, who, keys[row], lanes]) for who, row in pairs
        ]
        near_dprod = [dot_nt(grad[who], near[1, who, :, lanes]) for who in both]
        far_dprod = [
            dot_nt(grad[who][rows[row]], slots[1, who, keys[row], lanes]) for who, row in pairs
        ]
        near_weight, far_weight, near_half, far_half = [], [], [], []
        for i, (who, row) in enumerate(pairs):
            ns = near_score[who][rows[row]]
            top = jnp.maximum(
                jnp.max(ns, axis=1, keepdims=True), jnp.max(far_score[i], axis=1, keepdims=True)
            )
            near_exp = jnp.exp2((ns - top) * EXP_SCALE)
            far_exp = jnp.exp2((far_score[i] - top) * EXP_SCALE)
            inverse = 1.0 / (
                jnp.sum(near_exp, axis=1, keepdims=True) + jnp.sum(far_exp, axis=1, keepdims=True)
            )
            near_weight.append(near_exp * inverse)
            far_weight.append(far_exp * inverse)
            near_half.append(near_weight[i].astype(BF16))
            far_half.append(far_weight[i].astype(BF16))
        delta = []
        for i, (who, row) in enumerate(pairs):
            out = dot_nn(near_half[i], near[1, who, :, lanes])
            out = (out + dot_nn(far_half[i], slots[1, who, keys[row], lanes])).astype(BF16)
            res[who][0, rows[row], lanes] = out
            g = grad[who][rows[row]]
            delta.append(jnp.sum(g.astype(F32) * out.astype(F32), axis=1, keepdims=True))
        for i, (who, row) in enumerate(pairs):
            g = grad[who][rows[row]]
            fgrad[1, who, keys[row], lanes] = dot_tn(far_half[i], g).astype(BF16)
        near_dscore, far_dscore = [], []
        for i, (who, row) in enumerate(pairs):
            nd = near_weight[i] * (near_dprod[who][rows[row]] - delta[i])
            near_dscore.append(nd.astype(BF16))
            far_dscore.append((far_weight[i] * (far_dprod[i] - delta[i])).astype(BF16))
        for i, (who, row) in enumerate(pairs):
            dq = dot_nn(near_dscore[i], near[0, who, :, lanes])
            dq = (dq + dot_nn(far_dscore[i], slots[0, who, keys[row], lanes])) * SCALE
            res[who][1, rows[row], lanes] = dq.astype(BF16)
        for i, (who, row) in enumerate(pairs):
            dk = dot_tn(far_dscore[i], query[who][rows[row]]) * SCALE
            fgrad[0, who, keys[row], lanes] = dk.astype(BF16)
        for who in both:
            two = slice(who * BLK, (who + 1) * BLK)
            near_kgrad = dot_tn(jnp.concatenate(near_dscore[two], axis=0), query[who]) * SCALE
            near_vgrad = dot_tn(jnp.concatenate(near_half[two], axis=0), grad[who])
            for kind, value in enumerate((near_kgrad, near_vgrad)):
                base[who, kind, :, lanes] = value[:TOK]
                first = (who * 2 + kind) * HEADS + head
                gwide[pl.ds(first, WINDOWS, stride=GROWS), :] = value[TOK : TOK + WINDOWS]
        return carry

    lax.fori_loop(0, HEADS, head_step, 0)
    gglob[...] = gwide[...].reshape(WINDOWS, GROWS, HEAD_DIM).astype(BF16)
    copies = []

    def send(value, output):
        copy = pltpu.make_async_copy(value, output, out_sem.at[len(copies)])
        copy.start()
        copies.append(copy)

    send(gglob, outputs[4])
    send(res_peer, outputs[1])
    send(res_own, outputs[0])
    for source in SEND_ORDER:
        for kind in range(2):
            for inner in range(BLK):
                rows = slice(inner * BLOCK, (inner + 1) * BLOCK)
                value = None
                for who in range(2):
                    code = table[who, source]
                    slot = lax.shift_right_logical(code, 1)
                    at = pl.ds(pl.multiple_of(slot * BLOCK, BLOCK), BLOCK)
                    here = (lax.bitwise_and(code, 1) == inner).astype(F32)
                    term = fgrad[kind, who, at, :].astype(F32) * here
                    value = term if value is None else value + term
                if source == NY:
                    base[1, kind, rows, :] += value
                else:
                    spare[source, kind, rows, :] = value.astype(BF16)
        if source != NY:
            part = scattered.at[source] if source < NY else parts[source - NY - 1]
            send(spare.at[source], part)
    send(base.at[1], outputs[3])
    send(base.at[0], outputs[2])
    for copy in copies:
        copy.wait()


def cut_kernel(core, *refs):
    inputs, outputs = refs[:4], refs[4:]
    for half in range(2):
        first = lax.bitwise_xor(core[0], half) * HALF
        columns = pl.ds(pl.multiple_of(first, HALF), HALF)
        for i in range(4):
            outputs[i // 2 * 2 + half][i % 2] = inputs[i][:, columns]


def cut(core, *inputs):
    vmem = pl.BlockSpec(memory_space=pltpu.VMEM)
    return pl.pallas_call(
        cut_kernel,
        out_shape=[jax.ShapeDtypeStruct((2, TOK, HALF), BF16)] * 4,
        in_specs=[pl.BlockSpec(memory_space=pltpu.SMEM)] + [vmem] * 4,
        out_specs=[vmem] * 4,
        cost_estimate=pl.CostEstimate(flops=0, bytes_accessed=2_000_000, transcendentals=0),
    )(core.astype(jnp.int32)[None], *inputs)


def attend(pos, far_own, far_peer, qdo_own, qdo_peer, glob, gathered, ring):
    smem = pl.BlockSpec(memory_space=pltpu.SMEM)
    vmem = pl.BlockSpec(memory_space=pltpu.VMEM)
    anywhere = pl.BlockSpec(memory_space=pl.ANY)
    piece = jax.ShapeDtypeStruct((2, TOK, HALF), BF16)
    return pl.pallas_call(
        attend_kernel,
        out_shape=[
            piece,
            piece,
            jax.ShapeDtypeStruct((2, TOK, HALF), F32),
            jax.ShapeDtypeStruct((2, TOK, HALF), F32),
            jax.ShapeDtypeStruct((WINDOWS, GROWS, HEAD_DIM), BF16),
        ]
        + [jax.ShapeDtypeStruct((NY, 2, TOK, HALF), BF16)]
        + [piece] * 7,
        in_specs=[smem] * 3 + [vmem] * 3 + [anywhere] * 9,
        out_specs=[anywhere] * 13,
        scratch_shapes=[
            pltpu.VMEM((2, 2, BLK * FKEYS, HALF), BF16),
            pltpu.VMEM((2, 2, NEAR, HALF), BF16),
            pltpu.VMEM((2, 2, BLK * FKEYS, HALF), BF16),
            pltpu.VMEM((WINDOWS * GROWS, HEAD_DIM), F32),
            pltpu.VMEM((2, TOK, HALF), BF16),
            pltpu.VMEM((2, TOK, HALF), BF16),
            pltpu.VMEM((2, 2, TOK, HALF), F32),
            pltpu.VMEM((WINDOWS, GROWS, HEAD_DIM), BF16),
            pltpu.VMEM((2 * NY, 2, TOK, HALF), BF16),
            pltpu.SMEM((2, 2 * NY), jnp.int32),
            pltpu.SemaphoreType.DMA((3 + 6 * NY,)),
            pltpu.SemaphoreType.DMA((5 + 2 * NY,)),
        ],
        compiler_params=pltpu.CompilerParams(vmem_limit_bytes=60 * 1024 * 1024),
        cost_estimate=pl.CostEstimate(
            flops=1_200_000_000, bytes_accessed=12_000_000, transcendentals=800_000
        ),
    )(pos, far_own, far_peer, qdo_own, qdo_peer, glob, gathered, *ring)


UP = [(i, (i + 1) % NY) for i in range(NY)]
DOWN = [(i, (i - 1) % NY) for i in range(NY)]
ROW_STEP, BACK_STEP = 1, 2
SWAP = [(0, 1), (1, 0)]


def plus(a, b):
    return (a.astype(F32) + b.astype(F32)).astype(BF16)


def per_device(query_rows, key_rows, value_rows, out_grad, far_blocks):
    my_y = lax.axis_index("y")
    my_c = lax.axis_index("c")
    my_w = lax.axis_index("x") * NZ + lax.axis_index("z")
    swap = functools.partial(lax.ppermute, axis_name="c", perm=SWAP)
    up = functools.partial(lax.ppermute, axis_name="y", perm=UP)
    down = functools.partial(lax.ppermute, axis_name="y", perm=DOWN)
    low = my_c == 0

    kv_own, kv_send, qdo_own, qdo_send = cut(my_c, key_rows, value_rows, query_rows, out_grad)
    kv_peer = swap(kv_send)
    gathered = lax.all_gather(jnp.concatenate([kv_own, kv_peer[:1]]), "y", axis=0)
    ring = [kv_peer[1]] + [None] * (NY - 1)
    row = jnp.concatenate([kv_own[:, 0], kv_peer[:, 0]]).reshape(GROWS, HEAD_DIM)
    chains = ((up, 4, -1), (down, 3, 1))
    held = [ring[0], ring[0]]
    for step in range(1, 5):
        for i, (move, count, sign) in enumerate(chains):
            if step <= count:
                held[i] = move(held[i])
        if step == ROW_STEP:
            row, held[0] = lax.optimization_barrier((row, held[0]))
            glob = lax.all_to_all(
                jnp.broadcast_to(row, (WINDOWS, GROWS, HEAD_DIM)), ("x", "z"), 0, 0, tiled=True
            )
            qdo_peer = swap(qdo_send)
            far_peer = swap(far_blocks)
        if step == 3:
            glob, qdo_peer, far_peer, held[0] = lax.optimization_barrier(
                (glob, qdo_peer, far_peer, held[0])
            )
        for i, (move, count, sign) in enumerate(chains):
            if step <= count:
                ring[(sign * step) % NY] = held[i]
    pos = jnp.stack([my_y, my_c, my_w]).astype(jnp.int32)
    res_own, res_peer, base_own, base_peer, gglob, scattered, *parts = attend(
        pos, far_blocks, far_peer, qdo_own, qdo_peer, glob, gathered, ring
    )
    far_own = (lax.psum_scatter(scattered, "y", scatter_dimension=0),)
    at = [4, 5]
    held = [parts[o - 1] for o in at]
    for step in range(1, 5):
        for i, (move, count, sign) in enumerate(chains):
            if step <= count:
                held[i] = move(held[i])
        if step == BACK_STEP:
            gglob, held[0] = lax.optimization_barrier((gglob, held[0]))
            gback = lax.all_to_all(gglob, ("x", "z"), 0, 0, tiled=True)
        for i, (move, count, sign) in enumerate(chains):
            if step <= count:
                at[i] = (at[i] + sign) % NY
                if at[i]:
                    held[i] = plus(held[i], parts[at[i] - 1])
    far_peer = held
    gsum = jnp.sum(gback.astype(F32), axis=0).reshape(2, 2, 1, HALF)
    res_back = swap(res_peer)
    first_row = lax.broadcasted_iota(jnp.int32, (1, TOK, 1), 1) == 0

    def finish(base, far, who):
        total = base + sum(term.astype(F32) for term in far)
        return (total + jnp.where(first_row, gsum[who], 0.0)).astype(BF16)

    peer_grad = finish(base_peer, far_peer, 1)
    base_own, _ = lax.optimization_barrier((base_own, peer_grad))
    peer_grad = swap(peer_grad)
    own_grad = finish(base_own, far_own, 0)

    def join(mine, other):
        return jnp.where(
            low,
            jnp.concatenate([mine, other], axis=1),
            jnp.concatenate([other, mine], axis=1),
        )

    return (
        join(res_own[0], res_back[0]),
        join(res_own[1], res_back[1]),
        join(own_grad[0], peer_grad[0]),
        join(own_grad[1], peer_grad[1]),
    )


def solution(mesh):
    fine = Mesh(mesh.devices.reshape(NX, NZ, NY, NC), ("x", "z", "y", "c"))
    spec = P(("y", "c", "x", "z"), None)
    return jax.shard_map(
        per_device, mesh=fine, in_specs=(spec,) * 5, out_specs=(spec,) * 4, check_vma=False
    )
```

```python
import functools
import math

import jax
import jax.numpy as jnp
from jax import lax
from jax.experimental import pallas as pl
from jax.experimental.pallas import tpu as pltpu
from jax.sharding import Mesh
from jax.sharding import PartitionSpec as P

HEAD_DIM = 128
BLOCK = 64
TOK = 128
BLK = 2
FAR = 8
NX, NZ, NY, NC = 4, 8, 8, 2
WINDOWS = NX * NZ
HALF = 512
PIECE = 256
HEADS = HALF // HEAD_DIM
NEAR = 256
GROWS = 4 * HEADS
SEND_ORDER = tuple(range(NY)) + (12, 13, 11, 14, 10, 15, 9, 8)
FKEYS = FAR * BLOCK
SCALE = 1.0 / math.sqrt(HEAD_DIM)
EXP_SCALE = SCALE * math.log2(math.e)
BF16 = jnp.bfloat16
F32 = jnp.float32


def dot_nt(a, b):
    return lax.dot_general(a, b, (((1,), (1,)), ((), ())), preferred_element_type=F32)


def dot_nn(a, b):
    return lax.dot_general(a, b, (((1,), (0,)), ((), ())), preferred_element_type=F32)


def dot_tn(a, b):
    return lax.dot_general(a, b, (((0,), (0,)), ((), ())), preferred_element_type=F32)


def attend_kernel(*refs):
    pos, far_own, far_peer, qdo_own, qdo_peer, glob = refs[:6]
    gathered = refs[6]
    ring = refs[7:15]
    outputs = refs[15:20]
    scattered = refs[20]
    parts = refs[21:28]
    slots, near, fgrad, gwide, res_own, res_peer, base, gglob, spare, table, in_sem, out_sem = refs[28:]
    my_y, my_c, my_w = pos[0], pos[1], pos[2]
    for who, far in enumerate((far_own, far_peer)):
        for row in range(BLK):
            for entry in range(FAR):
                block = far[row, entry]
                group = lax.shift_right_logical(block, 6)
                chain = lax.bitwise_xor(lax.bitwise_and(group, 1), my_c)
                offset = lax.bitwise_and(
                    lax.shift_right_logical(group, 1) - my_y * chain, NY - 1
                )
                inner = lax.bitwise_and(block, 1)
                table[who, chain * NY + offset] = (row * FAR + entry) * 2 + inner
    copies = []

    def fetch(value, output):
        copies.append(pltpu.make_async_copy(value, output, in_sem.at[len(copies)]))

    fetch(gathered.at[my_y, pl.ds(0, 4)], near.at[:, 0, :TOK, :])
    fetch(gathered.at[my_y, 4], near.at[0, 1, :TOK, :])
    fetch(ring[0], near.at[pl.ds(1, 3), 1, :TOK, :])
    for source in range(2 * NY):
        for who in range(2):
            code = table[who, source]
            slot = lax.shift_right_logical(code, 1)
            inner = lax.bitwise_and(code, 1)
            at = pl.ds(pl.multiple_of(slot * BLOCK, BLOCK), BLOCK)
            rows = pl.ds(pl.multiple_of(inner * BLOCK, BLOCK), BLOCK)
            if source < NY:
                fetch(gathered.at[source, pl.ds(0, 4), rows, :], slots.at[:, who, at, :])
            else:
                their_y = lax.bitwise_and(my_y + (source - NY), NY - 1)
                fetch(gathered.at[their_y, 4, rows, :], slots.at[0, who, at, :])
                fetch(ring[source - NY].at[:, rows, :], slots.at[pl.ds(1, 3), who, at, :])
    for copy in copies:
        copy.start()
    gwide[...] = glob[...].astype(F32).reshape(WINDOWS * GROWS, HEAD_DIM)
    for who in range(2):
        for kind in range(2):
            for head in range(HEADS):
                first = (who * 2 + kind) * HEADS + head
                sub = slice(head % 2 * HEAD_DIM, (head % 2 + 1) * HEAD_DIM)
                near[kind * 2 + head // 2, who, TOK : TOK + WINDOWS, sub] = (
                    gwide[pl.ds(first, WINDOWS, stride=GROWS), :].astype(BF16)
                )
            for side in range(2):
                near[kind * 2 + side, who, TOK + WINDOWS :, :] = jnp.zeros(
                    (NEAR - TOK - WINDOWS, PIECE), BF16
                )
    column = lax.broadcasted_iota(jnp.int32, (TOK, NEAR), 1)
    hidden = (column >= TOK + WINDOWS) | (column == TOK + my_w)
    for copy in copies:
        copy.wait()

    def head_step(head, carry):
        lanes = pl.ds(pl.multiple_of(head * HEAD_DIM, HEAD_DIM), HEAD_DIM)
        side = lax.shift_right_logical(head, 1)
        sub = pl.ds(pl.multiple_of(lax.bitwise_and(head, 1) * HEAD_DIM, HEAD_DIM), HEAD_DIM)
        both = range(2)
        pairs = [(who, row) for who in both for row in range(BLK)]
        rows = [slice(row * BLOCK, (row + 1) * BLOCK) for row in range(BLK)]
        keys = [slice(row * FKEYS, (row + 1) * FKEYS) for row in range(BLK)]
        res = res_own, res_peer
        query = [qdo[0, :, lanes] for qdo in (qdo_own, qdo_peer)]
        grad = [qdo[1, :, lanes] for qdo in (qdo_own, qdo_peer)]
        near_score = [
            jnp.where(hidden, -1e30, dot_nt(query[who], near[side, who, :, sub])) for who in both
        ]
        far_score = [
            dot_nt(query[who][rows[row]], slots[side, who, keys[row], sub]) for who, row in pairs
        ]
        near_dprod = [dot_nt(grad[who], near[2 + side, who, :, sub]) for who in both]
        far_dprod = [
            dot_nt(grad[who][rows[row]], slots[2 + side, who, keys[row], sub]) for who, row in pairs
        ]
        near_weight, far_weight, near_half, far_half = [], [], [], []
        for i, (who, row) in enumerate(pairs):
            ns = near_score[who][rows[row]]
            top = jnp.maximum(
                jnp.max(ns, axis=1, keepdims=True), jnp.max(far_score[i], axis=1, keepdims=True)
            )
            near_exp = jnp.exp2((ns - top) * EXP_SCALE)
            far_exp = jnp.exp2((far_score[i] - top) * EXP_SCALE)
            inverse = 1.0 / (
                jnp.sum(near_exp, axis=1, keepdims=True) + jnp.sum(far_exp, axis=1, keepdims=True)
            )
            near_weight.append(near_exp * inverse)
            far_weight.append(far_exp * inverse)
            near_half.append(near_weight[i].astype(BF16))
            far_half.append(far_weight[i].astype(BF16))
        delta = []
        for i, (who, row) in enumerate(pairs):
            out = dot_nn(near_half[i], near[2 + side, who, :, sub])
            out = (out + dot_nn(far_half[i], slots[2 + side, who, keys[row], sub])).astype(BF16)
            res[who][0, rows[row], lanes] = out
            g = grad[who][rows[row]]
            delta.append(jnp.sum(g.astype(F32) * out.astype(F32), axis=1, keepdims=True))
        for i, (who, row) in enumerate(pairs):
            g = grad[who][rows[row]]
            fgrad[1, who, keys[row], lanes] = dot_tn(far_half[i], g).astype(BF16)
        near_dscore, far_dscore = [], []
        for i, (who, row) in enumerate(pairs):
            nd = near_weight[i] * (near_dprod[who][rows[row]] - delta[i])
            near_dscore.append(nd.astype(BF16))
            far_dscore.append((far_weight[i] * (far_dprod[i] - delta[i])).astype(BF16))
        for i, (who, row) in enumerate(pairs):
            dq = dot_nn(near_dscore[i], near[side, who, :, sub])
            dq = (dq + dot_nn(far_dscore[i], slots[side, who, keys[row], sub])) * SCALE
            res[who][1, rows[row], lanes] = dq.astype(BF16)
        for i, (who, row) in enumerate(pairs):
            dk = dot_tn(far_dscore[i], query[who][rows[row]]) * SCALE
            fgrad[0, who, keys[row], lanes] = dk.astype(BF16)
        for who in both:
            two = slice(who * BLK, (who + 1) * BLK)
            near_kgrad = dot_tn(jnp.concatenate(near_dscore[two], axis=0), query[who]) * SCALE
            near_vgrad = dot_tn(jnp.concatenate(near_half[two], axis=0), grad[who])
            for kind, value in enumerate((near_kgrad, near_vgrad)):
                base[who, kind, :, lanes] = value[:TOK]
                first = (who * 2 + kind) * HEADS + head
                gwide[pl.ds(first, WINDOWS, stride=GROWS), :] = value[TOK : TOK + WINDOWS]
        return carry

    lax.fori_loop(0, HEADS, head_step, 0)
    gglob[...] = gwide[...].reshape(WINDOWS, GROWS, HEAD_DIM).astype(BF16)
    copies = []

    def send(value, output):
        copy = pltpu.make_async_copy(value, output, out_sem.at[len(copies)])
        copy.start()
        copies.append(copy)

    send(gglob, outputs[4])
    send(res_peer, outputs[1])
    send(res_own, outputs[0])
    for source in SEND_ORDER:
        for kind in range(2):
            for inner in range(BLK):
                rows = slice(inner * BLOCK, (inner + 1) * BLOCK)
                value = None
                for who in range(2):
                    code = table[who, source]
                    slot = lax.shift_right_logical(code, 1)
                    at = pl.ds(pl.multiple_of(slot * BLOCK, BLOCK), BLOCK)
                    here = (lax.bitwise_and(code, 1) == inner).astype(F32)
                    term = fgrad[kind, who, at, :].astype(F32) * here
                    value = term if value is None else value + term
                if source == NY:
                    base[1, kind, rows, :] += value
                else:
                    spare[source, kind, rows, :] = value.astype(BF16)
        if source != NY:
            part = scattered.at[source] if source < NY else parts[source - NY - 1]
            send(spare.at[source], part)
    send(base.at[1], outputs[3])
    send(base.at[0], outputs[2])
    for copy in copies:
        copy.wait()


def cut_kernel(width, core, first, second, own, send):
    pieces = HALF // width
    for output, half in ((own, 0), (send, 1)):
        start = lax.bitwise_xor(core[0], half) * HALF
        for i in range(2):
            for piece in range(pieces):
                columns = pl.ds(pl.multiple_of(start + piece * width, width), width)
                output[i * pieces + piece] = (first, second)[i][:, columns]


def cut(core, first, second, width, room=0):
    vmem = pl.BlockSpec(memory_space=pltpu.VMEM)
    count = 2 * HALF // width
    return pl.pallas_call(
        functools.partial(cut_kernel, width),
        out_shape=[
            jax.ShapeDtypeStruct((count + room, TOK, width), BF16),
            jax.ShapeDtypeStruct((count, TOK, width), BF16),
        ],
        in_specs=[pl.BlockSpec(memory_space=pltpu.SMEM), vmem, vmem],
        out_specs=[vmem] * 2,
        cost_estimate=pl.CostEstimate(flops=0, bytes_accessed=1_000_000, transcendentals=0),
    )(core.astype(jnp.int32)[None], first, second)


def attend(pos, far_own, far_peer, qdo_own, qdo_peer, glob, gathered, ring):
    smem = pl.BlockSpec(memory_space=pltpu.SMEM)
    vmem = pl.BlockSpec(memory_space=pltpu.VMEM)
    anywhere = pl.BlockSpec(memory_space=pl.ANY)
    piece = jax.ShapeDtypeStruct((2, TOK, HALF), BF16)
    return pl.pallas_call(
        attend_kernel,
        out_shape=[
            piece,
            piece,
            jax.ShapeDtypeStruct((2, TOK, HALF), F32),
            jax.ShapeDtypeStruct((2, TOK, HALF), F32),
            jax.ShapeDtypeStruct((WINDOWS, GROWS, HEAD_DIM), BF16),
        ]
        + [jax.ShapeDtypeStruct((NY, 2, TOK, HALF), BF16)]
        + [piece] * 7,
        in_specs=[smem] * 3 + [vmem] * 3 + [anywhere] * 9,
        out_specs=[anywhere] * 13,
        scratch_shapes=[
            pltpu.VMEM((4, 2, BLK * FKEYS, PIECE), BF16),
            pltpu.VMEM((4, 2, NEAR, PIECE), BF16),
            pltpu.VMEM((2, 2, BLK * FKEYS, HALF), BF16),
            pltpu.VMEM((WINDOWS * GROWS, HEAD_DIM), F32),
            pltpu.VMEM((2, TOK, HALF), BF16),
            pltpu.VMEM((2, TOK, HALF), BF16),
            pltpu.VMEM((2, 2, TOK, HALF), F32),
            pltpu.VMEM((WINDOWS, GROWS, HEAD_DIM), BF16),
            pltpu.VMEM((2 * NY, 2, TOK, HALF), BF16),
            pltpu.SMEM((2, 2 * NY), jnp.int32),
            pltpu.SemaphoreType.DMA((3 + 6 * NY,)),
            pltpu.SemaphoreType.DMA((5 + 2 * NY,)),
        ],
        compiler_params=pltpu.CompilerParams(vmem_limit_bytes=60 * 1024 * 1024),
        cost_estimate=pl.CostEstimate(
            flops=1_200_000_000, bytes_accessed=12_000_000, transcendentals=800_000
        ),
    )(pos, far_own, far_peer, qdo_own, qdo_peer, glob, gathered, *ring)


UP = [(i, (i + 1) % NY) for i in range(NY)]
DOWN = [(i, (i - 1) % NY) for i in range(NY)]
ROW_STEP, BACK_STEP = 1, 2
SWAP = [(0, 1), (1, 0)]


def plus(a, b):
    return (a.astype(F32) + b.astype(F32)).astype(BF16)


def per_device(query_rows, key_rows, value_rows, out_grad, far_blocks):
    my_y = lax.axis_index("y")
    my_c = lax.axis_index("c")
    my_w = lax.axis_index("x") * NZ + lax.axis_index("z")
    swap = functools.partial(lax.ppermute, axis_name="c", perm=SWAP)
    up = functools.partial(lax.ppermute, axis_name="y", perm=UP)
    down = functools.partial(lax.ppermute, axis_name="y", perm=DOWN)
    low = my_c == 0

    kv_own, kv_send = cut(my_c, key_rows, value_rows, PIECE, room=1)
    kv_peer = swap(kv_send)
    kv_own = lax.dynamic_update_slice(kv_own, kv_peer[:1], (4, 0, 0))
    gathered = lax.all_gather(kv_own, "y", axis=0)
    ring = [kv_peer[1:]] + [None] * (NY - 1)
    qdo_own, qdo_send = cut(my_c, query_rows, out_grad, HALF)
    row = jnp.concatenate([kv_own[:4, 0], kv_peer[:, 0]]).reshape(GROWS, HEAD_DIM)
    chains = ((up, 4, -1), (down, 3, 1))
    held = [ring[0], ring[0]]
    for step in range(1, 5):
        for i, (move, count, sign) in enumerate(chains):
            if step <= count:
                held[i] = move(held[i])
        if step == ROW_STEP:
            row, held[0] = lax.optimization_barrier((row, held[0]))
            glob = lax.all_to_all(
                jnp.broadcast_to(row, (WINDOWS, GROWS, HEAD_DIM)), ("x", "z"), 0, 0, tiled=True
            )
            qdo_peer = swap(qdo_send)
            far_peer = swap(far_blocks)
        if step == 3:
            glob, qdo_peer, far_peer, held[0] = lax.optimization_barrier(
                (glob, qdo_peer, far_peer, held[0])
            )
        for i, (move, count, sign) in enumerate(chains):
            if step <= count:
                ring[(sign * step) % NY] = held[i]
    pos = jnp.stack([my_y, my_c, my_w]).astype(jnp.int32)
    res_own, res_peer, base_own, base_peer, gglob, scattered, *parts = attend(
        pos, far_blocks, far_peer, qdo_own, qdo_peer, glob, gathered, ring
    )
    far_own = (lax.psum_scatter(scattered, "y", scatter_dimension=0),)
    at = [4, 5]
    held = [parts[o - 1] for o in at]
    for step in range(1, 5):
        for i, (move, count, sign) in enumerate(chains):
            if step <= count:
                held[i] = move(held[i])
        if step == BACK_STEP:
            gglob, held[0] = lax.optimization_barrier((gglob, held[0]))
            gback = lax.all_to_all(gglob, ("x", "z"), 0, 0, tiled=True)
        for i, (move, count, sign) in enumerate(chains):
            if step <= count:
                at[i] = (at[i] + sign) % NY
                if at[i]:
                    held[i] = plus(held[i], parts[at[i] - 1])
    far_peer = held
    gsum = jnp.sum(gback.astype(F32), axis=0).reshape(2, 2, 1, HALF)
    res_back = swap(res_peer)
    first_row = lax.broadcasted_iota(jnp.int32, (1, TOK, 1), 1) == 0

    def finish(base, far, who):
        total = base + sum(term.astype(F32) for term in far)
        return (total + jnp.where(first_row, gsum[who], 0.0)).astype(BF16)

    peer_grad = finish(base_peer, far_peer, 1)
    base_own, _ = lax.optimization_barrier((base_own, peer_grad))
    peer_grad = swap(peer_grad)
    own_grad = finish(base_own, far_own, 0)

    def join(mine, other):
        return jnp.where(
            low,
            jnp.concatenate([mine, other], axis=1),
            jnp.concatenate([other, mine], axis=1),
        )

    return (
        join(res_own[0], res_back[0]),
        join(res_own[1], res_back[1]),
        join(own_grad[0], peer_grad[0]),
        join(own_grad[1], peer_grad[1]),
    )


def solution(mesh):
    fine = Mesh(mesh.devices.reshape(NX, NZ, NY, NC), ("x", "z", "y", "c"))
    spec = P(("y", "c", "x", "z"), None)
    return jax.shard_map(
        per_device, mesh=fine, in_specs=(spec,) * 5, out_specs=(spec,) * 4, check_vma=False
    )
```

```python
import functools
import math

import jax
import jax.numpy as jnp
from jax import lax
from jax.experimental import pallas as pl
from jax.experimental.pallas import tpu as pltpu
from jax.sharding import Mesh
from jax.sharding import PartitionSpec as P

HEAD_DIM = 128
BLOCK = 64
TOK = 128
BLK = 2
FAR = 8
NX, NZ, NY, NC = 4, 8, 8, 2
WINDOWS = NX * NZ
HALF = 512
PIECE = 256
HEADS = HALF // HEAD_DIM
NEAR = 256
GROWS = 4 * HEADS
SEND_ORDER = tuple(range(NY)) + (12, 13, 11, 14, 10, 15, 9, 8)
FKEYS = FAR * BLOCK
SCALE = 1.0 / math.sqrt(HEAD_DIM)
EXP_SCALE = SCALE * math.log2(math.e)
BF16 = jnp.bfloat16
F32 = jnp.float32


def dot_nt(a, b):
    return lax.dot_general(a, b, (((1,), (1,)), ((), ())), preferred_element_type=F32)


def dot_nn(a, b):
    return lax.dot_general(a, b, (((1,), (0,)), ((), ())), preferred_element_type=F32)


def dot_tn(a, b):
    return lax.dot_general(a, b, (((0,), (0,)), ((), ())), preferred_element_type=F32)


def attend_kernel(*refs):
    pos, far_own, far_peer, qdo_own, qdo_peer, glob = refs[:6]
    gathered = refs[6]
    ring = refs[7:15]
    outputs = refs[15:20]
    scattered = refs[20]
    parts = refs[21:28]
    slots, near, fgrad, gwide, res_own, res_peer, base, gglob, spare, table, in_sem, out_sem = refs[28:]
    my_y, my_c, my_w = pos[0], pos[1], pos[2]
    for who, far in enumerate((far_own, far_peer)):
        for row in range(BLK):
            for entry in range(FAR):
                block = far[row, entry]
                group = lax.shift_right_logical(block, 6)
                chain = lax.bitwise_xor(lax.bitwise_and(group, 1), my_c)
                offset = lax.bitwise_and(
                    lax.shift_right_logical(group, 1) - my_y * chain, NY - 1
                )
                inner = lax.bitwise_and(block, 1)
                table[who, chain * NY + offset] = (row * FAR + entry) * 2 + inner
    copies = []

    def fetch(value, output):
        copies.append(pltpu.make_async_copy(value, output, in_sem.at[len(copies)]))

    fetch(gathered.at[my_y, pl.ds(0, 4)], near.at[:, 0, :TOK, :])
    fetch(gathered.at[my_y, 4], near.at[0, 1, :TOK, :])
    fetch(ring[0], near.at[pl.ds(1, 3), 1, :TOK, :])
    for source in range(2 * NY):
        for who in range(2):
            code = table[who, source]
            slot = lax.shift_right_logical(code, 1)
            inner = lax.bitwise_and(code, 1)
            at = pl.ds(pl.multiple_of(slot * BLOCK, BLOCK), BLOCK)
            rows = pl.ds(pl.multiple_of(inner * BLOCK, BLOCK), BLOCK)
            if source < NY:
                fetch(gathered.at[source, pl.ds(0, 4), rows, :], slots.at[:, who, at, :])
            else:
                their_y = lax.bitwise_and(my_y + (source - NY), NY - 1)
                fetch(gathered.at[their_y, 4, rows, :], slots.at[0, who, at, :])
                fetch(ring[source - NY].at[:, rows, :], slots.at[pl.ds(1, 3), who, at, :])
    for copy in copies:
        copy.start()
    gwide[...] = glob[...].astype(F32).reshape(WINDOWS * GROWS, HEAD_DIM)
    for who in range(2):
        for kind in range(2):
            for head in range(HEADS):
                first = (who * 2 + kind) * HEADS + head
                sub = slice(head % 2 * HEAD_DIM, (head % 2 + 1) * HEAD_DIM)
                near[kind * 2 + head // 2, who, TOK : TOK + WINDOWS, sub] = (
                    gwide[pl.ds(first, WINDOWS, stride=GROWS), :].astype(BF16)
                )
            for side in range(2):
                near[kind * 2 + side, who, TOK + WINDOWS :, :] = jnp.zeros(
                    (NEAR - TOK - WINDOWS, PIECE), BF16
                )
    column = lax.broadcasted_iota(jnp.int32, (TOK, NEAR), 1)
    hidden = (column >= TOK + WINDOWS) | (column == TOK + my_w)
    for copy in copies:
        copy.wait()

    def head_step(head, carry):
        lanes = pl.ds(pl.multiple_of(head * HEAD_DIM, HEAD_DIM), HEAD_DIM)
        side = lax.shift_right_logical(head, 1)
        sub = pl.ds(pl.multiple_of(lax.bitwise_and(head, 1) * HEAD_DIM, HEAD_DIM), HEAD_DIM)
        both = range(2)
        pairs = [(who, row) for who in both for row in range(BLK)]
        rows = [slice(row * BLOCK, (row + 1) * BLOCK) for row in range(BLK)]
        keys = [slice(row * FKEYS, (row + 1) * FKEYS) for row in range(BLK)]
        res = res_own, res_peer
        query = [qdo[0, :, lanes] for qdo in (qdo_own, qdo_peer)]
        grad = [qdo[1, :, lanes] for qdo in (qdo_own, qdo_peer)]
        near_score = [
            jnp.where(hidden, -1e30, dot_nt(query[who], near[side, who, :, sub])) for who in both
        ]
        far_score = [
            dot_nt(query[who][rows[row]], slots[side, who, keys[row], sub]) for who, row in pairs
        ]
        near_dprod = [dot_nt(grad[who], near[2 + side, who, :, sub]) for who in both]
        far_dprod = [
            dot_nt(grad[who][rows[row]], slots[2 + side, who, keys[row], sub]) for who, row in pairs
        ]
        near_weight, far_weight, near_half, far_half = [], [], [], []
        for i, (who, row) in enumerate(pairs):
            ns = near_score[who][rows[row]]
            top = jnp.maximum(
                jnp.max(ns, axis=1, keepdims=True), jnp.max(far_score[i], axis=1, keepdims=True)
            )
            near_exp = jnp.exp2((ns - top) * EXP_SCALE)
            far_exp = jnp.exp2((far_score[i] - top) * EXP_SCALE)
            inverse = 1.0 / (
                jnp.sum(near_exp, axis=1, keepdims=True) + jnp.sum(far_exp, axis=1, keepdims=True)
            )
            near_weight.append(near_exp * inverse)
            far_weight.append(far_exp * inverse)
            near_half.append(near_weight[i].astype(BF16))
            far_half.append(far_weight[i].astype(BF16))
        delta = []
        for i, (who, row) in enumerate(pairs):
            out = dot_nn(near_half[i], near[2 + side, who, :, sub])
            out = (out + dot_nn(far_half[i], slots[2 + side, who, keys[row], sub])).astype(BF16)
            res[who][0, rows[row], lanes] = out
            g = grad[who][rows[row]]
            delta.append(jnp.sum(g.astype(F32) * out.astype(F32), axis=1, keepdims=True))
        for i, (who, row) in enumerate(pairs):
            g = grad[who][rows[row]]
            fgrad[1, who, keys[row], lanes] = dot_tn(far_half[i], g).astype(BF16)
        near_dscore, far_dscore = [], []
        for i, (who, row) in enumerate(pairs):
            nd = near_weight[i] * (near_dprod[who][rows[row]] - delta[i])
            near_dscore.append(nd.astype(BF16))
            far_dscore.append((far_weight[i] * (far_dprod[i] - delta[i])).astype(BF16))
        for i, (who, row) in enumerate(pairs):
            dq = dot_nn(near_dscore[i], near[side, who, :, sub])
            dq = (dq + dot_nn(far_dscore[i], slots[side, who, keys[row], sub])) * SCALE
            res[who][1, rows[row], lanes] = dq.astype(BF16)
        for i, (who, row) in enumerate(pairs):
            dk = dot_tn(far_dscore[i], query[who][rows[row]]) * SCALE
            fgrad[0, who, keys[row], lanes] = dk.astype(BF16)
        for who in both:
            two = slice(who * BLK, (who + 1) * BLK)
            near_kgrad = dot_tn(jnp.concatenate(near_dscore[two], axis=0), query[who]) * SCALE
            near_vgrad = dot_tn(jnp.concatenate(near_half[two], axis=0), grad[who])
            for kind, value in enumerate((near_kgrad, near_vgrad)):
                base[who, kind, :, lanes] = value[:TOK]
                first = (who * 2 + kind) * HEADS + head
                gwide[pl.ds(first, WINDOWS, stride=GROWS), :] = value[TOK : TOK + WINDOWS]
        return carry

    lax.fori_loop(0, HEADS, head_step, 0)
    gglob[...] = gwide[...].reshape(WINDOWS, GROWS, HEAD_DIM).astype(BF16)
    copies = []

    def send(value, output):
        copy = pltpu.make_async_copy(value, output, out_sem.at[len(copies)])
        copy.start()
        copies.append(copy)

    send(gglob, outputs[4])
    send(res_peer, outputs[1])
    send(res_own, outputs[0])
    for source in SEND_ORDER:
        for kind in range(2):
            for inner in range(BLK):
                rows = slice(inner * BLOCK, (inner + 1) * BLOCK)
                value = None
                for who in range(2):
                    code = table[who, source]
                    slot = lax.shift_right_logical(code, 1)
                    at = pl.ds(pl.multiple_of(slot * BLOCK, BLOCK), BLOCK)
                    here = (lax.bitwise_and(code, 1) == inner).astype(F32)
                    term = fgrad[kind, who, at, :].astype(F32) * here
                    value = term if value is None else value + term
                if source == NY:
                    base[1, kind, rows, :] += value
                else:
                    spare[source, kind, rows, :] = value.astype(BF16)
        if source != NY:
            part = scattered.at[source] if source < NY else parts[source - NY - 1]
            send(spare.at[source], part)
    send(base.at[1], outputs[3])
    send(base.at[0], outputs[2])
    for copy in copies:
        copy.wait()


def cut_kernel(width, core, first, second, own, send):
    pieces = HALF // width
    for output, half in ((own, 0), (send, 1)):
        start = lax.bitwise_xor(core[0], half) * HALF
        for i in range(2):
            for piece in range(pieces):
                columns = pl.ds(pl.multiple_of(start + piece * width, width), width)
                output[i * pieces + piece] = (first, second)[i][:, columns]


def cut(core, first, second, width, room=0):
    vmem = pl.BlockSpec(memory_space=pltpu.VMEM)
    count = 2 * HALF // width
    return pl.pallas_call(
        functools.partial(cut_kernel, width),
        out_shape=[
            jax.ShapeDtypeStruct((count + room, TOK, width), BF16),
            jax.ShapeDtypeStruct((count, TOK, width), BF16),
        ],
        in_specs=[pl.BlockSpec(memory_space=pltpu.SMEM), vmem, vmem],
        out_specs=[vmem] * 2,
        cost_estimate=pl.CostEstimate(flops=0, bytes_accessed=1_000_000, transcendentals=0),
    )(core.astype(jnp.int32)[None], first, second)


def attend(pos, far_own, far_peer, qdo_own, qdo_peer, glob, gathered, ring):
    smem = pl.BlockSpec(memory_space=pltpu.SMEM)
    vmem = pl.BlockSpec(memory_space=pltpu.VMEM)
    anywhere = pl.BlockSpec(memory_space=pl.ANY)
    piece = jax.ShapeDtypeStruct((2, TOK, HALF), BF16)
    return pl.pallas_call(
        attend_kernel,
        out_shape=[
            piece,
            piece,
            jax.ShapeDtypeStruct((2, TOK, HALF), F32),
            jax.ShapeDtypeStruct((2, TOK, HALF), F32),
            jax.ShapeDtypeStruct((WINDOWS, GROWS, HEAD_DIM), BF16),
        ]
        + [jax.ShapeDtypeStruct((NY, 2, TOK, HALF), BF16)]
        + [piece] * 7,
        in_specs=[smem] * 3 + [vmem] * 3 + [anywhere] * 9,
        out_specs=[anywhere] * 13,
        scratch_shapes=[
            pltpu.VMEM((4, 2, BLK * FKEYS, PIECE), BF16),
            pltpu.VMEM((4, 2, NEAR, PIECE), BF16),
            pltpu.VMEM((2, 2, BLK * FKEYS, HALF), BF16),
            pltpu.VMEM((WINDOWS * GROWS, HEAD_DIM), F32),
            pltpu.VMEM((2, TOK, HALF), BF16),
            pltpu.VMEM((2, TOK, HALF), BF16),
            pltpu.VMEM((2, 2, TOK, HALF), F32),
            pltpu.VMEM((WINDOWS, GROWS, HEAD_DIM), BF16),
            pltpu.VMEM((2 * NY, 2, TOK, HALF), BF16),
            pltpu.SMEM((2, 2 * NY), jnp.int32),
            pltpu.SemaphoreType.DMA((3 + 6 * NY,)),
            pltpu.SemaphoreType.DMA((5 + 2 * NY,)),
        ],
        compiler_params=pltpu.CompilerParams(vmem_limit_bytes=60 * 1024 * 1024),
        cost_estimate=pl.CostEstimate(
            flops=1_200_000_000, bytes_accessed=12_000_000, transcendentals=800_000
        ),
    )(pos, far_own, far_peer, qdo_own, qdo_peer, glob, gathered, *ring)


UP = [(i, (i + 1) % NY) for i in range(NY)]
DOWN = [(i, (i - 1) % NY) for i in range(NY)]
ROW_STEP, BACK_STEP = 2, 2
SWAP = [(0, 1), (1, 0)]


def plus(a, b):
    return (a.astype(F32) + b.astype(F32)).astype(BF16)


def per_device(query_rows, key_rows, value_rows, out_grad, far_blocks):
    my_y = lax.axis_index("y")
    my_c = lax.axis_index("c")
    my_w = lax.axis_index("x") * NZ + lax.axis_index("z")
    swap = functools.partial(lax.ppermute, axis_name="c", perm=SWAP)
    up = functools.partial(lax.ppermute, axis_name="y", perm=UP)
    down = functools.partial(lax.ppermute, axis_name="y", perm=DOWN)
    low = my_c == 0

    kv_own, kv_send = cut(my_c, key_rows, value_rows, PIECE, room=1)
    kv_peer = swap(kv_send)
    kv_own = lax.dynamic_update_slice(kv_own, kv_peer[:1], (4, 0, 0))
    gathered = lax.all_gather(kv_own, "y", axis=0)
    ring = [kv_peer[1:]] + [None] * (NY - 1)
    qdo_own, qdo_send = cut(my_c, query_rows, out_grad, HALF)
    row = jnp.concatenate([kv_own[:4, 0], kv_peer[:, 0]]).reshape(GROWS, HEAD_DIM)
    chains = ((up, 4, -1), (down, 3, 1))
    held = [ring[0], ring[0]]
    for step in range(1, 5):
        for i, (move, count, sign) in enumerate(chains):
            if step <= count:
                held[i] = move(held[i])
        if step == ROW_STEP:
            row, held[0] = lax.optimization_barrier((row, held[0]))
            glob = lax.all_to_all(
                jnp.broadcast_to(row, (WINDOWS, GROWS, HEAD_DIM)), ("x", "z"), 0, 0, tiled=True
            )
            qdo_peer = swap(qdo_send)
            far_peer = swap(far_blocks)
        if step == 3:
            glob, qdo_peer, far_peer, held[0] = lax.optimization_barrier(
                (glob, qdo_peer, far_peer, held[0])
            )
        for i, (move, count, sign) in enumerate(chains):
            if step <= count:
                ring[(sign * step) % NY] = held[i]
    pos = jnp.stack([my_y, my_c, my_w]).astype(jnp.int32)
    res_own, res_peer, base_own, base_peer, gglob, scattered, *parts = attend(
        pos, far_blocks, far_peer, qdo_own, qdo_peer, glob, gathered, ring
    )
    far_own = (lax.psum_scatter(scattered, "y", scatter_dimension=0),)
    at = [4, 5]
    held = [parts[o - 1] for o in at]
    for step in range(1, 5):
        for i, (move, count, sign) in enumerate(chains):
            if step <= count:
                held[i] = move(held[i])
        if step == BACK_STEP:
            gglob, held[0] = lax.optimization_barrier((gglob, held[0]))
            gback = lax.all_to_all(gglob, ("x", "z"), 0, 0, tiled=True)
        for i, (move, count, sign) in enumerate(chains):
            if step <= count:
                at[i] = (at[i] + sign) % NY
                if at[i]:
                    held[i] = plus(held[i], parts[at[i] - 1])
    far_peer = held
    gsum = jnp.sum(gback.astype(F32), axis=0).reshape(2, 2, 1, HALF)
    res_back = swap(res_peer)
    first_row = lax.broadcasted_iota(jnp.int32, (1, TOK, 1), 1) == 0

    def finish(base, far, who):
        total = base + sum(term.astype(F32) for term in far)
        return (total + jnp.where(first_row, gsum[who], 0.0)).astype(BF16)

    peer_grad = finish(base_peer, far_peer, 1)
    base_own, _ = lax.optimization_barrier((base_own, peer_grad))
    peer_grad = swap(peer_grad)
    own_grad = finish(base_own, far_own, 0)

    def join(mine, other):
        return jnp.where(
            low,
            jnp.concatenate([mine, other], axis=1),
            jnp.concatenate([other, mine], axis=1),
        )

    return (
        join(res_own[0], res_back[0]),
        join(res_own[1], res_back[1]),
        join(own_grad[0], peer_grad[0]),
        join(own_grad[1], peer_grad[1]),
    )


def solution(mesh):
    fine = Mesh(mesh.devices.reshape(NX, NZ, NY, NC), ("x", "z", "y", "c"))
    spec = P(("y", "c", "x", "z"), None)
    return jax.shard_map(
        per_device, mesh=fine, in_specs=(spec,) * 5, out_specs=(spec,) * 4, check_vma=False
    )
```

```python
import functools
import math

import jax
import jax.numpy as jnp
from jax import lax
from jax.experimental import pallas as pl
from jax.experimental.pallas import tpu as pltpu
from jax.sharding import Mesh
from jax.sharding import PartitionSpec as P

HEAD_DIM = 128
BLOCK = 64
TOK = 128
BLK = 2
FAR = 8
NX, NZ, NY, NC = 4, 8, 8, 2
WINDOWS = NX * NZ
HALF = 512
PIECE = 256
HEADS = HALF // HEAD_DIM
NEAR = 256
GROWS = 4 * HEADS
SEND_ORDER = tuple(range(NY)) + (12, 13, 11, 14, 10, 15, 9, 8)
FKEYS = FAR * BLOCK
SCALE = 1.0 / math.sqrt(HEAD_DIM)
EXP_SCALE = SCALE * math.log2(math.e)
BF16 = jnp.bfloat16
F32 = jnp.float32


def dot_nt(a, b):
    return lax.dot_general(a, b, (((1,), (1,)), ((), ())), preferred_element_type=F32)


def dot_nn(a, b):
    return lax.dot_general(a, b, (((1,), (0,)), ((), ())), preferred_element_type=F32)


def dot_tn(a, b):
    return lax.dot_general(a, b, (((0,), (0,)), ((), ())), preferred_element_type=F32)


def attend_kernel(*refs):
    pos, far_own, far_peer, qdo_own, qdo_peer, glob = refs[:6]
    gathered = refs[6]
    ring = refs[7:15]
    outputs = refs[15:20]
    scattered = refs[20]
    parts = refs[21:28]
    slots, near, fgrad, gwide, res_own, res_peer, base, gglob, spare, table, in_sem, out_sem = refs[28:]
    my_y, my_c, my_w = pos[0], pos[1], pos[2]
    for who, far in enumerate((far_own, far_peer)):
        for row in range(BLK):
            for entry in range(FAR):
                block = far[row, entry]
                group = lax.shift_right_logical(block, 6)
                chain = lax.bitwise_xor(lax.bitwise_and(group, 1), my_c)
                offset = lax.bitwise_and(
                    lax.shift_right_logical(group, 1) - my_y * chain, NY - 1
                )
                inner = lax.bitwise_and(block, 1)
                table[who, chain * NY + offset] = (row * FAR + entry) * 2 + inner
    copies = []

    def fetch(value, output):
        copies.append(pltpu.make_async_copy(value, output, in_sem.at[len(copies)]))

    fetch(gathered.at[my_y, pl.ds(0, 4)], near.at[:, 0, :TOK, :])
    fetch(gathered.at[my_y, 4], near.at[0, 1, :TOK, :])
    fetch(ring[0], near.at[pl.ds(1, 3), 1, :TOK, :])
    for source in range(2 * NY):
        for who in range(2):
            code = table[who, source]
            slot = lax.shift_right_logical(code, 1)
            inner = lax.bitwise_and(code, 1)
            at = pl.ds(pl.multiple_of(slot * BLOCK, BLOCK), BLOCK)
            rows = pl.ds(pl.multiple_of(inner * BLOCK, BLOCK), BLOCK)
            if source < NY:
                fetch(gathered.at[source, pl.ds(0, 4), rows, :], slots.at[:, who, at, :])
            else:
                their_y = lax.bitwise_and(my_y + (source - NY), NY - 1)
                fetch(gathered.at[their_y, 4, rows, :], slots.at[0, who, at, :])
                fetch(ring[source - NY].at[:, rows, :], slots.at[pl.ds(1, 3), who, at, :])
    for copy in copies:
        copy.start()
    gwide[...] = glob[...].astype(F32).reshape(WINDOWS * GROWS, HEAD_DIM)
    for who in range(2):
        for kind in range(2):
            for head in range(HEADS):
                first = (who * 2 + kind) * HEADS + head
                sub = slice(head % 2 * HEAD_DIM, (head % 2 + 1) * HEAD_DIM)
                near[kind * 2 + head // 2, who, TOK : TOK + WINDOWS, sub] = (
                    gwide[pl.ds(first, WINDOWS, stride=GROWS), :].astype(BF16)
                )
            for side in range(2):
                near[kind * 2 + side, who, TOK + WINDOWS :, :] = jnp.zeros(
                    (NEAR - TOK - WINDOWS, PIECE), BF16
                )
    column = lax.broadcasted_iota(jnp.int32, (TOK, NEAR), 1)
    hidden = (column >= TOK + WINDOWS) | (column == TOK + my_w)
    for copy in copies:
        copy.wait()

    def head_step(head, carry):
        lanes = pl.ds(pl.multiple_of(head * HEAD_DIM, HEAD_DIM), HEAD_DIM)
        side = lax.shift_right_logical(head, 1)
        sub = pl.ds(pl.multiple_of(lax.bitwise_and(head, 1) * HEAD_DIM, HEAD_DIM), HEAD_DIM)
        both = range(2)
        pairs = [(who, row) for who in both for row in range(BLK)]
        rows = [slice(row * BLOCK, (row + 1) * BLOCK) for row in range(BLK)]
        keys = [slice(row * FKEYS, (row + 1) * FKEYS) for row in range(BLK)]
        res = res_own, res_peer
        query = [qdo[0, :, lanes] for qdo in (qdo_own, qdo_peer)]
        grad = [qdo[1, :, lanes] for qdo in (qdo_own, qdo_peer)]
        near_score = [
            jnp.where(hidden, -1e30, dot_nt(query[who], near[side, who, :, sub])) for who in both
        ]
        far_score = [
            dot_nt(query[who][rows[row]], slots[side, who, keys[row], sub]) for who, row in pairs
        ]
        near_dprod = [dot_nt(grad[who], near[2 + side, who, :, sub]) for who in both]
        far_dprod = [
            dot_nt(grad[who][rows[row]], slots[2 + side, who, keys[row], sub]) for who, row in pairs
        ]
        near_weight, far_weight, near_half, far_half = [], [], [], []
        for i, (who, row) in enumerate(pairs):
            ns = near_score[who][rows[row]]
            top = jnp.maximum(
                jnp.max(ns, axis=1, keepdims=True), jnp.max(far_score[i], axis=1, keepdims=True)
            )
            near_exp = jnp.exp2((ns - top) * EXP_SCALE)
            far_exp = jnp.exp2((far_score[i] - top) * EXP_SCALE)
            inverse = 1.0 / (
                jnp.sum(near_exp, axis=1, keepdims=True) + jnp.sum(far_exp, axis=1, keepdims=True)
            )
            near_weight.append(near_exp * inverse)
            far_weight.append(far_exp * inverse)
            near_half.append(near_weight[i].astype(BF16))
            far_half.append(far_weight[i].astype(BF16))
        delta = []
        for i, (who, row) in enumerate(pairs):
            out = dot_nn(near_half[i], near[2 + side, who, :, sub])
            out = (out + dot_nn(far_half[i], slots[2 + side, who, keys[row], sub])).astype(BF16)
            res[who][0, rows[row], lanes] = out
            g = grad[who][rows[row]]
            delta.append(jnp.sum(g.astype(F32) * out.astype(F32), axis=1, keepdims=True))
        for i, (who, row) in enumerate(pairs):
            g = grad[who][rows[row]]
            fgrad[1, who, keys[row], lanes] = dot_tn(far_half[i], g).astype(BF16)
        near_dscore, far_dscore = [], []
        for i, (who, row) in enumerate(pairs):
            nd = near_weight[i] * (near_dprod[who][rows[row]] - delta[i])
            near_dscore.append(nd.astype(BF16))
            far_dscore.append((far_weight[i] * (far_dprod[i] - delta[i])).astype(BF16))
        for i, (who, row) in enumerate(pairs):
            dq = dot_nn(near_dscore[i], near[side, who, :, sub])
            dq = (dq + dot_nn(far_dscore[i], slots[side, who, keys[row], sub])) * SCALE
            res[who][1, rows[row], lanes] = dq.astype(BF16)
        for i, (who, row) in enumerate(pairs):
            dk = dot_tn(far_dscore[i], query[who][rows[row]]) * SCALE
            fgrad[0, who, keys[row], lanes] = dk.astype(BF16)
        for who in both:
            two = slice(who * BLK, (who + 1) * BLK)
            near_kgrad = dot_tn(jnp.concatenate(near_dscore[two], axis=0), query[who]) * SCALE
            near_vgrad = dot_tn(jnp.concatenate(near_half[two], axis=0), grad[who])
            for kind, value in enumerate((near_kgrad, near_vgrad)):
                base[who, kind, :, lanes] = value[:TOK]
                first = (who * 2 + kind) * HEADS + head
                gwide[pl.ds(first, WINDOWS, stride=GROWS), :] = value[TOK : TOK + WINDOWS]
        return carry

    lax.fori_loop(0, HEADS, head_step, 0)
    gglob[...] = gwide[...].reshape(WINDOWS, GROWS, HEAD_DIM).astype(BF16)
    copies = []

    def send(value, output):
        copy = pltpu.make_async_copy(value, output, out_sem.at[len(copies)])
        copy.start()
        copies.append(copy)

    send(gglob, outputs[4])
    send(res_peer, outputs[1])
    send(res_own, outputs[0])
    for source in SEND_ORDER:
        for kind in range(2):
            for inner in range(BLK):
                rows = slice(inner * BLOCK, (inner + 1) * BLOCK)
                value = None
                for who in range(2):
                    code = table[who, source]
                    slot = lax.shift_right_logical(code, 1)
                    at = pl.ds(pl.multiple_of(slot * BLOCK, BLOCK), BLOCK)
                    here = (lax.bitwise_and(code, 1) == inner).astype(F32)
                    term = fgrad[kind, who, at, :].astype(F32) * here
                    value = term if value is None else value + term
                if source == NY:
                    base[1, kind, rows, :] += value
                else:
                    spare[source, kind, rows, :] = value.astype(BF16)
        if source != NY:
            part = scattered.at[source] if source < NY else parts[source - NY - 1]
            send(spare.at[source], part)
    send(base.at[1], outputs[3])
    send(base.at[0], outputs[2])
    for copy in copies:
        copy.wait()


def cut_kernel(width, core, first, second, own, send):
    pieces = HALF // width
    for output, half in ((own, 0), (send, 1)):
        start = lax.bitwise_xor(core[0], half) * HALF
        for i in range(2):
            for piece in range(pieces):
                columns = pl.ds(pl.multiple_of(start + piece * width, width), width)
                output[i * pieces + piece] = (first, second)[i][:, columns]


def cut(core, first, second, width, room=0):
    vmem = pl.BlockSpec(memory_space=pltpu.VMEM)
    count = 2 * HALF // width
    return pl.pallas_call(
        functools.partial(cut_kernel, width),
        out_shape=[
            jax.ShapeDtypeStruct((count + room, TOK, width), BF16),
            jax.ShapeDtypeStruct((count, TOK, width), BF16),
        ],
        in_specs=[pl.BlockSpec(memory_space=pltpu.SMEM), vmem, vmem],
        out_specs=[vmem] * 2,
        cost_estimate=pl.CostEstimate(flops=0, bytes_accessed=1_000_000, transcendentals=0),
    )(core.astype(jnp.int32)[None], first, second)


def attend(pos, far_own, far_peer, qdo_own, qdo_peer, glob, gathered, ring):
    smem = pl.BlockSpec(memory_space=pltpu.SMEM)
    vmem = pl.BlockSpec(memory_space=pltpu.VMEM)
    anywhere = pl.BlockSpec(memory_space=pl.ANY)
    piece = jax.ShapeDtypeStruct((2, TOK, HALF), BF16)
    return pl.pallas_call(
        attend_kernel,
        out_shape=[
            piece,
            piece,
            jax.ShapeDtypeStruct((2, TOK, HALF), F32),
            jax.ShapeDtypeStruct((2, TOK, HALF), F32),
            jax.ShapeDtypeStruct((WINDOWS, GROWS, HEAD_DIM), BF16),
        ]
        + [jax.ShapeDtypeStruct((NY, 2, TOK, HALF), BF16)]
        + [piece] * 7,
        in_specs=[smem] * 3 + [vmem] * 3 + [anywhere] * 9,
        out_specs=[anywhere] * 13,
        scratch_shapes=[
            pltpu.VMEM((4, 2, BLK * FKEYS, PIECE), BF16),
            pltpu.VMEM((4, 2, NEAR, PIECE), BF16),
            pltpu.VMEM((2, 2, BLK * FKEYS, HALF), BF16),
            pltpu.VMEM((WINDOWS * GROWS, HEAD_DIM), F32),
            pltpu.VMEM((2, TOK, HALF), BF16),
            pltpu.VMEM((2, TOK, HALF), BF16),
            pltpu.VMEM((2, 2, TOK, HALF), F32),
            pltpu.VMEM((WINDOWS, GROWS, HEAD_DIM), BF16),
            pltpu.VMEM((2 * NY, 2, TOK, HALF), BF16),
            pltpu.SMEM((2, 2 * NY), jnp.int32),
            pltpu.SemaphoreType.DMA((3 + 6 * NY,)),
            pltpu.SemaphoreType.DMA((5 + 2 * NY,)),
        ],
        compiler_params=pltpu.CompilerParams(vmem_limit_bytes=60 * 1024 * 1024),
        cost_estimate=pl.CostEstimate(
            flops=1_200_000_000, bytes_accessed=12_000_000, transcendentals=800_000
        ),
    )(pos, far_own, far_peer, qdo_own, qdo_peer, glob, gathered, *ring)


UP = [(i, (i + 1) % NY) for i in range(NY)]
DOWN = [(i, (i - 1) % NY) for i in range(NY)]
BACK_STEP = 2
SWAP = [(0, 1), (1, 0)]


def plus(a, b):
    return (a.astype(F32) + b.astype(F32)).astype(BF16)


def per_device(query_rows, key_rows, value_rows, out_grad, far_blocks):
    my_y = lax.axis_index("y")
    my_c = lax.axis_index("c")
    my_w = lax.axis_index("x") * NZ + lax.axis_index("z")
    swap = functools.partial(lax.ppermute, axis_name="c", perm=SWAP)
    up = functools.partial(lax.ppermute, axis_name="y", perm=UP)
    down = functools.partial(lax.ppermute, axis_name="y", perm=DOWN)
    low = my_c == 0

    kv_own, kv_send = cut(my_c, key_rows, value_rows, PIECE, room=1)
    kv_peer = swap(kv_send)
    kv_own = lax.dynamic_update_slice(kv_own, kv_peer[:1], (4, 0, 0))
    gathered = lax.all_gather(kv_own, "y", axis=0)
    ring = [kv_peer[1:]] + [None] * (NY - 1)
    qdo_own, qdo_send = cut(my_c, query_rows, out_grad, HALF)
    row = jnp.concatenate([kv_own[:4, 0], kv_peer[:, 0]]).reshape(GROWS, HEAD_DIM)
    chains = ((up, 4, -1), (down, 3, 1))
    held = [ring[0], ring[0]]
    for step in range(1, 5):
        for i, (move, count, sign) in enumerate(chains):
            if step <= count:
                held[i] = move(held[i])
        if step == 1:
            row, held[1] = lax.optimization_barrier((row, held[1]))
            qdo_peer = swap(qdo_send)
            far_peer = swap(far_blocks)
        if step == 2:
            row, held[0] = lax.optimization_barrier((row, held[0]))
            row, held[1] = lax.optimization_barrier((row, held[1]))
            glob = lax.all_to_all(
                jnp.broadcast_to(row, (WINDOWS, GROWS, HEAD_DIM)), ("x", "z"), 0, 0, tiled=True
            )
        if step == 3:
            glob, qdo_peer, far_peer, held[0] = lax.optimization_barrier(
                (glob, qdo_peer, far_peer, held[0])
            )
        for i, (move, count, sign) in enumerate(chains):
            if step <= count:
                ring[(sign * step) % NY] = held[i]
    pos = jnp.stack([my_y, my_c, my_w]).astype(jnp.int32)
    res_own, res_peer, base_own, base_peer, gglob, scattered, *parts = attend(
        pos, far_blocks, far_peer, qdo_own, qdo_peer, glob, gathered, ring
    )
    far_own = (lax.psum_scatter(scattered, "y", scatter_dimension=0),)
    at = [4, 5]
    held = [parts[o - 1] for o in at]
    for step in range(1, 5):
        for i, (move, count, sign) in enumerate(chains):
            if step <= count:
                held[i] = move(held[i])
        if step == BACK_STEP:
            gglob, held[0] = lax.optimization_barrier((gglob, held[0]))
            gback = lax.all_to_all(gglob, ("x", "z"), 0, 0, tiled=True)
        for i, (move, count, sign) in enumerate(chains):
            if step <= count:
                at[i] = (at[i] + sign) % NY
                if at[i]:
                    held[i] = plus(held[i], parts[at[i] - 1])
    far_peer = held
    gsum = jnp.sum(gback.astype(F32), axis=0).reshape(2, 2, 1, HALF)
    res_back = swap(res_peer)
    first_row = lax.broadcasted_iota(jnp.int32, (1, TOK, 1), 1) == 0

    def finish(base, far, who):
        total = base + sum(term.astype(F32) for term in far)
        return (total + jnp.where(first_row, gsum[who], 0.0)).astype(BF16)

    peer_grad = finish(base_peer, far_peer, 1)
    base_own, _ = lax.optimization_barrier((base_own, peer_grad))
    peer_grad = swap(peer_grad)
    own_grad = finish(base_own, far_own, 0)

    def join(mine, other):
        return jnp.where(
            low,
            jnp.concatenate([mine, other], axis=1),
            jnp.concatenate([other, mine], axis=1),
        )

    return (
        join(res_own[0], res_back[0]),
        join(res_own[1], res_back[1]),
        join(own_grad[0], peer_grad[0]),
        join(own_grad[1], peer_grad[1]),
    )


def solution(mesh):
    fine = Mesh(mesh.devices.reshape(NX, NZ, NY, NC), ("x", "z", "y", "c"))
    spec = P(("y", "c", "x", "z"), None)
    return jax.shard_map(
        per_device, mesh=fine, in_specs=(spec,) * 5, out_specs=(spec,) * 4, check_vma=False
    )
```

```python
import functools
import math

import jax
import jax.numpy as jnp
from jax import lax
from jax.experimental import pallas as pl
from jax.experimental.pallas import tpu as pltpu
from jax.sharding import Mesh
from jax.sharding import PartitionSpec as P

HEAD_DIM = 128
BLOCK = 64
TOK = 128
BLK = 2
FAR = 8
NX, NZ, NY, NC = 4, 8, 8, 2
WINDOWS = NX * NZ
HALF = 512
PIECE = 256
HEADS = HALF // HEAD_DIM
NEAR = 256
GROWS = 4 * HEADS
SEND_ORDER = tuple(range(NY)) + (12, 13, 11, 14, 10, 15, 9, 8)
FKEYS = FAR * BLOCK
SCALE = 1.0 / math.sqrt(HEAD_DIM)
EXP_SCALE = SCALE * math.log2(math.e)
BF16 = jnp.bfloat16
F32 = jnp.float32


def dot_nt(a, b):
    return lax.dot_general(a, b, (((1,), (1,)), ((), ())), preferred_element_type=F32)


def dot_nn(a, b):
    return lax.dot_general(a, b, (((1,), (0,)), ((), ())), preferred_element_type=F32)


def dot_tn(a, b):
    return lax.dot_general(a, b, (((0,), (0,)), ((), ())), preferred_element_type=F32)


def attend_kernel(*refs):
    pos, far_own, far_peer, qdo_own, qdo_peer, glob = refs[:6]
    gathered = refs[6]
    ring = refs[7:15]
    outputs = refs[15:20]
    scattered = refs[20]
    parts = refs[21:28]
    slots, near, fgrad, gwide, res_own, res_peer, base, gglob, spare, table, in_sem, out_sem = refs[28:]
    my_y, my_c, my_w = pos[0], pos[1], pos[2]
    for who, far in enumerate((far_own, far_peer)):
        for row in range(BLK):
            for entry in range(FAR):
                block = far[row, entry]
                group = lax.shift_right_logical(block, 6)
                chain = lax.bitwise_xor(lax.bitwise_and(group, 1), my_c)
                offset = lax.bitwise_and(
                    lax.shift_right_logical(group, 1) - my_y * chain, NY - 1
                )
                inner = lax.bitwise_and(block, 1)
                table[who, chain * NY + offset] = (row * FAR + entry) * 2 + inner
    copies = []

    def fetch(value, output):
        copies.append(pltpu.make_async_copy(value, output, in_sem.at[len(copies)]))

    fetch(gathered.at[my_y, pl.ds(0, 4)], near.at[:, 0, :TOK, :])
    fetch(gathered.at[my_y, 4], near.at[0, 1, :TOK, :])
    fetch(ring[0], near.at[pl.ds(1, 3), 1, :TOK, :])
    for source in range(2 * NY):
        for who in range(2):
            code = table[who, source]
            slot = lax.shift_right_logical(code, 1)
            inner = lax.bitwise_and(code, 1)
            at = pl.ds(pl.multiple_of(slot * BLOCK, BLOCK), BLOCK)
            rows = pl.ds(pl.multiple_of(inner * BLOCK, BLOCK), BLOCK)
            if source < NY:
                fetch(gathered.at[source, pl.ds(0, 4), rows, :], slots.at[:, who, at, :])
            else:
                their_y = lax.bitwise_and(my_y + (source - NY), NY - 1)
                fetch(gathered.at[their_y, 4, rows, :], slots.at[0, who, at, :])
                fetch(ring[source - NY].at[:, rows, :], slots.at[pl.ds(1, 3), who, at, :])
    for copy in copies:
        copy.start()
    gwide[...] = glob[...].astype(F32).reshape(WINDOWS * GROWS, HEAD_DIM)
    for who in range(2):
        for kind in range(2):
            for head in range(HEADS):
                first = (who * 2 + kind) * HEADS + head
                sub = slice(head % 2 * HEAD_DIM, (head % 2 + 1) * HEAD_DIM)
                near[kind * 2 + head // 2, who, TOK : TOK + WINDOWS, sub] = (
                    gwide[pl.ds(first, WINDOWS, stride=GROWS), :].astype(BF16)
                )
            for side in range(2):
                near[kind * 2 + side, who, TOK + WINDOWS :, :] = jnp.zeros(
                    (NEAR - TOK - WINDOWS, PIECE), BF16
                )
    column = lax.broadcasted_iota(jnp.int32, (TOK, NEAR), 1)
    hidden = (column >= TOK + WINDOWS) | (column == TOK + my_w)
    for copy in copies:
        copy.wait()

    def head_step(head, carry):
        lanes = pl.ds(pl.multiple_of(head * HEAD_DIM, HEAD_DIM), HEAD_DIM)
        side = lax.shift_right_logical(head, 1)
        sub = pl.ds(pl.multiple_of(lax.bitwise_and(head, 1) * HEAD_DIM, HEAD_DIM), HEAD_DIM)
        both = range(2)
        pairs = [(who, row) for who in both for row in range(BLK)]
        rows = [slice(row * BLOCK, (row + 1) * BLOCK) for row in range(BLK)]
        keys = [slice(row * FKEYS, (row + 1) * FKEYS) for row in range(BLK)]
        res = res_own, res_peer
        query = [qdo[0, :, lanes] for qdo in (qdo_own, qdo_peer)]
        grad = [qdo[1, :, lanes] for qdo in (qdo_own, qdo_peer)]
        near_score = [
            jnp.where(hidden, -1e30, dot_nt(query[who], near[side, who, :, sub])) for who in both
        ]
        far_score = [
            dot_nt(query[who][rows[row]], slots[side, who, keys[row], sub]) for who, row in pairs
        ]
        near_dprod = [dot_nt(grad[who], near[2 + side, who, :, sub]) for who in both]
        far_dprod = [
            dot_nt(grad[who][rows[row]], slots[2 + side, who, keys[row], sub]) for who, row in pairs
        ]
        near_weight, far_weight, near_half, far_half = [], [], [], []
        for i, (who, row) in enumerate(pairs):
            ns = near_score[who][rows[row]]
            top = jnp.maximum(
                jnp.max(ns, axis=1, keepdims=True), jnp.max(far_score[i], axis=1, keepdims=True)
            )
            near_exp = jnp.exp2((ns - top) * EXP_SCALE)
            far_exp = jnp.exp2((far_score[i] - top) * EXP_SCALE)
            inverse = 1.0 / (
                jnp.sum(near_exp, axis=1, keepdims=True) + jnp.sum(far_exp, axis=1, keepdims=True)
            )
            near_weight.append(near_exp * inverse)
            far_weight.append(far_exp * inverse)
            near_half.append(near_weight[i].astype(BF16))
            far_half.append(far_weight[i].astype(BF16))
        delta = []
        for i, (who, row) in enumerate(pairs):
            out = dot_nn(near_half[i], near[2 + side, who, :, sub])
            out = (out + dot_nn(far_half[i], slots[2 + side, who, keys[row], sub])).astype(BF16)
            res[who][0, rows[row], lanes] = out
            g = grad[who][rows[row]]
            delta.append(jnp.sum(g.astype(F32) * out.astype(F32), axis=1, keepdims=True))
        for i, (who, row) in enumerate(pairs):
            g = grad[who][rows[row]]
            fgrad[1, who, keys[row], lanes] = dot_tn(far_half[i], g).astype(BF16)
        near_dscore, far_dscore = [], []
        for i, (who, row) in enumerate(pairs):
            nd = near_weight[i] * (near_dprod[who][rows[row]] - delta[i])
            near_dscore.append(nd.astype(BF16))
            far_dscore.append((far_weight[i] * (far_dprod[i] - delta[i])).astype(BF16))
        for i, (who, row) in enumerate(pairs):
            dq = dot_nn(near_dscore[i], near[side, who, :, sub])
            dq = (dq + dot_nn(far_dscore[i], slots[side, who, keys[row], sub])) * SCALE
            res[who][1, rows[row], lanes] = dq.astype(BF16)
        for i, (who, row) in enumerate(pairs):
            dk = dot_tn(far_dscore[i], query[who][rows[row]]) * SCALE
            fgrad[0, who, keys[row], lanes] = dk.astype(BF16)
        for who in both:
            two = slice(who * BLK, (who + 1) * BLK)
            near_kgrad = dot_tn(jnp.concatenate(near_dscore[two], axis=0), query[who]) * SCALE
            near_vgrad = dot_tn(jnp.concatenate(near_half[two], axis=0), grad[who])
            for kind, value in enumerate((near_kgrad, near_vgrad)):
                base[who, kind, :, lanes] = value[:TOK]
                first = (who * 2 + kind) * HEADS + head
                gwide[pl.ds(first, WINDOWS, stride=GROWS), :] = value[TOK : TOK + WINDOWS]
        return carry

    lax.fori_loop(0, HEADS, head_step, 0)
    gglob[...] = gwide[...].reshape(WINDOWS, GROWS, HEAD_DIM).astype(BF16)
    copies = []

    def send(value, output):
        copy = pltpu.make_async_copy(value, output, out_sem.at[len(copies)])
        copy.start()
        copies.append(copy)

    send(gglob, outputs[4])
    send(res_peer, outputs[1])
    send(res_own, outputs[0])
    for source in SEND_ORDER:
        for kind in range(2):
            for inner in range(BLK):
                rows = slice(inner * BLOCK, (inner + 1) * BLOCK)
                value = None
                for who in range(2):
                    code = table[who, source]
                    slot = lax.shift_right_logical(code, 1)
                    at = pl.ds(pl.multiple_of(slot * BLOCK, BLOCK), BLOCK)
                    here = (lax.bitwise_and(code, 1) == inner).astype(F32)
                    term = fgrad[kind, who, at, :].astype(F32) * here
                    value = term if value is None else value + term
                if source == NY:
                    base[1, kind, rows, :] += value
                else:
                    spare[source, kind, rows, :] = value.astype(BF16)
        if source != NY:
            part = scattered.at[source] if source < NY else parts[source - NY - 1]
            send(spare.at[source], part)
    send(base.at[1], outputs[3])
    send(base.at[0], outputs[2])
    for copy in copies:
        copy.wait()


def cut_kernel(width, core, first, second, own, send):
    pieces = HALF // width
    for output, half in ((own, 0), (send, 1)):
        start = lax.bitwise_xor(core[0], half) * HALF
        for i in range(2):
            for piece in range(pieces):
                columns = pl.ds(pl.multiple_of(start + piece * width, width), width)
                output[i * pieces + piece] = (first, second)[i][:, columns]


def cut(core, first, second, width, room=0):
    vmem = pl.BlockSpec(memory_space=pltpu.VMEM)
    count = 2 * HALF // width
    return pl.pallas_call(
        functools.partial(cut_kernel, width),
        out_shape=[
            jax.ShapeDtypeStruct((count + room, TOK, width), BF16),
            jax.ShapeDtypeStruct((count, TOK, width), BF16),
        ],
        in_specs=[pl.BlockSpec(memory_space=pltpu.SMEM), vmem, vmem],
        out_specs=[vmem] * 2,
        cost_estimate=pl.CostEstimate(flops=0, bytes_accessed=1_000_000, transcendentals=0),
    )(core.astype(jnp.int32)[None], first, second)


def attend(pos, far_own, far_peer, qdo_own, qdo_peer, glob, gathered, ring):
    smem = pl.BlockSpec(memory_space=pltpu.SMEM)
    vmem = pl.BlockSpec(memory_space=pltpu.VMEM)
    anywhere = pl.BlockSpec(memory_space=pl.ANY)
    piece = jax.ShapeDtypeStruct((2, TOK, HALF), BF16)
    return pl.pallas_call(
        attend_kernel,
        out_shape=[
            piece,
            piece,
            jax.ShapeDtypeStruct((2, TOK, HALF), F32),
            jax.ShapeDtypeStruct((2, TOK, HALF), F32),
            jax.ShapeDtypeStruct((WINDOWS, GROWS, HEAD_DIM), BF16),
        ]
        + [jax.ShapeDtypeStruct((NY, 2, TOK, HALF), BF16)]
        + [piece] * 7,
        in_specs=[smem] * 3 + [vmem] * 3 + [anywhere] * 9,
        out_specs=[anywhere] * 13,
        scratch_shapes=[
            pltpu.VMEM((4, 2, BLK * FKEYS, PIECE), BF16),
            pltpu.VMEM((4, 2, NEAR, PIECE), BF16),
            pltpu.VMEM((2, 2, BLK * FKEYS, HALF), BF16),
            pltpu.VMEM((WINDOWS * GROWS, HEAD_DIM), F32),
            pltpu.VMEM((2, TOK, HALF), BF16),
            pltpu.VMEM((2, TOK, HALF), BF16),
            pltpu.VMEM((2, 2, TOK, HALF), F32),
            pltpu.VMEM((WINDOWS, GROWS, HEAD_DIM), BF16),
            pltpu.VMEM((2 * NY, 2, TOK, HALF), BF16),
            pltpu.SMEM((2, 2 * NY), jnp.int32),
            pltpu.SemaphoreType.DMA((3 + 6 * NY,)),
            pltpu.SemaphoreType.DMA((5 + 2 * NY,)),
        ],
        compiler_params=pltpu.CompilerParams(vmem_limit_bytes=60 * 1024 * 1024),
        cost_estimate=pl.CostEstimate(
            flops=1_200_000_000, bytes_accessed=12_000_000, transcendentals=800_000
        ),
    )(pos, far_own, far_peer, qdo_own, qdo_peer, glob, gathered, *ring)


UP = [(i, (i + 1) % NY) for i in range(NY)]
DOWN = [(i, (i - 1) % NY) for i in range(NY)]
ROW_STEP, BACK_STEP = 1, 1
SWAP = [(0, 1), (1, 0)]


def plus(a, b):
    return (a.astype(F32) + b.astype(F32)).astype(BF16)


def per_device(query_rows, key_rows, value_rows, out_grad, far_blocks):
    my_y = lax.axis_index("y")
    my_c = lax.axis_index("c")
    my_w = lax.axis_index("x") * NZ + lax.axis_index("z")
    swap = functools.partial(lax.ppermute, axis_name="c", perm=SWAP)
    up = functools.partial(lax.ppermute, axis_name="y", perm=UP)
    down = functools.partial(lax.ppermute, axis_name="y", perm=DOWN)
    low = my_c == 0

    def home(terms, sign):
        pairs = [
            (2 * y + c, (y - sign) % NY * 2 + 1 - c) for y in range(NY) for c in range(NC)
        ]
        return lax.ppermute(terms, ("y", "c"), pairs)

    kv_own, kv_send = cut(my_c, key_rows, value_rows, PIECE, room=1)
    kv_peer = swap(kv_send)
    kv_own = lax.dynamic_update_slice(kv_own, kv_peer[:1], (4, 0, 0))
    gathered = lax.all_gather(kv_own, "y", axis=0)
    ring = [kv_peer[1:]] + [None] * (NY - 1)
    qdo_own, qdo_send = cut(my_c, query_rows, out_grad, HALF)
    row = jnp.concatenate([kv_own[:4, 0], kv_peer[:, 0]]).reshape(GROWS, HEAD_DIM)
    chains = ((up, 4, -1), (down, 3, 1))
    held = [ring[0], ring[0]]
    for step in range(1, 5):
        for i, (move, count, sign) in enumerate(chains):
            if step <= count:
                held[i] = move(held[i])
        if step == ROW_STEP:
            row, held[0] = lax.optimization_barrier((row, held[0]))
            glob = lax.all_to_all(
                jnp.broadcast_to(row, (WINDOWS, GROWS, HEAD_DIM)), ("x", "z"), 0, 0, tiled=True
            )
            qdo_peer = swap(qdo_send)
            far_peer = swap(far_blocks)
        if step == 3:
            glob, qdo_peer, far_peer, held[0] = lax.optimization_barrier(
                (glob, qdo_peer, far_peer, held[0])
            )
        for i, (move, count, sign) in enumerate(chains):
            if step <= count:
                ring[(sign * step) % NY] = held[i]
    pos = jnp.stack([my_y, my_c, my_w]).astype(jnp.int32)
    res_own, res_peer, base_own, base_peer, gglob, scattered, *parts = attend(
        pos, far_blocks, far_peer, qdo_own, qdo_peer, glob, gathered, ring
    )
    base_other = swap(base_peer)
    far_own = (lax.psum_scatter(scattered, "y", scatter_dimension=0),)
    at = [4, 5]
    held = [parts[o - 1] for o in at]
    for step in range(1, 5):
        for i, (move, count, sign) in enumerate(chains):
            if step < count:
                held[i] = move(held[i])
            elif step == count:
                held[i] = home(held[i], sign)
        if step == BACK_STEP:
            gglob, held[0] = lax.optimization_barrier((gglob, held[0]))
            gback = lax.all_to_all(gglob, ("x", "z"), 0, 0, tiled=True)
        for i, (move, count, sign) in enumerate(chains):
            if step <= count:
                at[i] = (at[i] + sign) % NY
                if at[i]:
                    held[i] = plus(held[i], parts[at[i] - 1])
    far_peer = held
    gsum = jnp.sum(gback.astype(F32), axis=0).reshape(2, 2, 1, HALF)
    gsum = gsum[0], swap(gsum[1])
    res_back = swap(res_peer)
    first_row = lax.broadcasted_iota(jnp.int32, (1, TOK, 1), 1) == 0

    def finish(base, far, who):
        total = base + sum(term.astype(F32) for term in far)
        return (total + jnp.where(first_row, gsum[who], 0.0)).astype(BF16)

    other_grad = finish(base_other, far_peer, 1)
    own_grad = finish(base_own, far_own, 0)

    def join(mine, other):
        return jnp.where(
            low,
            jnp.concatenate([mine, other], axis=1),
            jnp.concatenate([other, mine], axis=1),
        )

    return (
        join(res_own[0], res_back[0]),
        join(res_own[1], res_back[1]),
        join(own_grad[0], other_grad[0]),
        join(own_grad[1], other_grad[1]),
    )


def solution(mesh):
    fine = Mesh(mesh.devices.reshape(NX, NZ, NY, NC), ("x", "z", "y", "c"))
    spec = P(("y", "c", "x", "z"), None)
    return jax.shard_map(
        per_device, mesh=fine, in_specs=(spec,) * 5, out_specs=(spec,) * 4, check_vma=False
    )
```

```python
import functools
import math

import jax
import jax.numpy as jnp
from jax import lax
from jax.experimental import pallas as pl
from jax.experimental.pallas import tpu as pltpu
from jax.sharding import Mesh
from jax.sharding import PartitionSpec as P

HEAD_DIM = 128
BLOCK = 64
TOK = 128
BLK = 2
FAR = 8
NX, NZ, NY, NC = 4, 8, 8, 2
WINDOWS = NX * NZ
HALF = 512
PIECE = 256
HEADS = HALF // HEAD_DIM
NEAR = 256
GROWS = 4 * HEADS
SEND_ORDER = tuple(range(NY)) + (12, 13, 11, 14, 10, 15, 9, 8)
FKEYS = FAR * BLOCK
SCALE = 1.0 / math.sqrt(HEAD_DIM)
EXP_SCALE = SCALE * math.log2(math.e)
BF16 = jnp.bfloat16
F32 = jnp.float32


def dot_nt(a, b):
    return lax.dot_general(a, b, (((1,), (1,)), ((), ())), preferred_element_type=F32)


def dot_nn(a, b):
    return lax.dot_general(a, b, (((1,), (0,)), ((), ())), preferred_element_type=F32)


def dot_tn(a, b):
    return lax.dot_general(a, b, (((0,), (0,)), ((), ())), preferred_element_type=F32)


def attend_kernel(*refs):
    pos, far_own, far_peer, qdo_own, qdo_peer, glob = refs[:6]
    gathered = refs[6]
    ring = refs[7:15]
    outputs = refs[15:20]
    scattered = refs[20]
    parts = refs[21:28]
    slots, near, fgrad, gwide, res_own, res_peer, base, gglob, spare, table, in_sem, out_sem = refs[28:]
    my_y, my_c, my_w = pos[0], pos[1], pos[2]
    for who, far in enumerate((far_own, far_peer)):
        for row in range(BLK):
            for entry in range(FAR):
                block = far[row, entry]
                group = lax.shift_right_logical(block, 6)
                chain = lax.bitwise_xor(lax.bitwise_and(group, 1), my_c)
                offset = lax.bitwise_and(
                    lax.shift_right_logical(group, 1) - my_y * chain, NY - 1
                )
                inner = lax.bitwise_and(block, 1)
                table[who, chain * NY + offset] = (row * FAR + entry) * 2 + inner
    copies = []

    def fetch(value, output):
        copies.append(pltpu.make_async_copy(value, output, in_sem.at[len(copies)]))

    fetch(gathered.at[my_y, pl.ds(0, 4)], near.at[:, 0, :TOK, :])
    fetch(gathered.at[my_y, 4], near.at[0, 1, :TOK, :])
    fetch(ring[0], near.at[pl.ds(1, 3), 1, :TOK, :])
    for source in range(2 * NY):
        for who in range(2):
            code = table[who, source]
            slot = lax.shift_right_logical(code, 1)
            inner = lax.bitwise_and(code, 1)
            at = pl.ds(pl.multiple_of(slot * BLOCK, BLOCK), BLOCK)
            rows = pl.ds(pl.multiple_of(inner * BLOCK, BLOCK), BLOCK)
            if source < NY:
                fetch(gathered.at[source, pl.ds(0, 4), rows, :], slots.at[:, who, at, :])
            else:
                their_y = lax.bitwise_and(my_y + (source - NY), NY - 1)
                fetch(gathered.at[their_y, 4, rows, :], slots.at[0, who, at, :])
                fetch(ring[source - NY].at[:, rows, :], slots.at[pl.ds(1, 3), who, at, :])
    for copy in copies:
        copy.start()
    gwide[...] = glob[...].astype(F32).reshape(WINDOWS * GROWS, HEAD_DIM)
    for who in range(2):
        for kind in range(2):
            for head in range(HEADS):
                first = (who * 2 + kind) * HEADS + head
                sub = slice(head % 2 * HEAD_DIM, (head % 2 + 1) * HEAD_DIM)
                near[kind * 2 + head // 2, who, TOK : TOK + WINDOWS, sub] = (
                    gwide[pl.ds(first, WINDOWS, stride=GROWS), :].astype(BF16)
                )
            for side in range(2):
                near[kind * 2 + side, who, TOK + WINDOWS :, :] = jnp.zeros(
                    (NEAR - TOK - WINDOWS, PIECE), BF16
                )
    column = lax.broadcasted_iota(jnp.int32, (TOK, NEAR), 1)
    hidden = (column >= TOK + WINDOWS) | (column == TOK + my_w)
    for copy in copies:
        copy.wait()

    def head_step(head, carry):
        lanes = pl.ds(pl.multiple_of(head * HEAD_DIM, HEAD_DIM), HEAD_DIM)
        side = lax.shift_right_logical(head, 1)
        sub = pl.ds(pl.multiple_of(lax.bitwise_and(head, 1) * HEAD_DIM, HEAD_DIM), HEAD_DIM)
        both = range(2)
        pairs = [(who, row) for who in both for row in range(BLK)]
        rows = [slice(row * BLOCK, (row + 1) * BLOCK) for row in range(BLK)]
        keys = [slice(row * FKEYS, (row + 1) * FKEYS) for row in range(BLK)]
        res = res_own, res_peer
        query = [qdo[0, :, lanes] for qdo in (qdo_own, qdo_peer)]
        grad = [qdo[1, :, lanes] for qdo in (qdo_own, qdo_peer)]
        near_score = [
            jnp.where(hidden, -1e30, dot_nt(query[who], near[side, who, :, sub])) for who in both
        ]
        far_score = [
            dot_nt(query[who][rows[row]], slots[side, who, keys[row], sub]) for who, row in pairs
        ]
        near_dprod = [dot_nt(grad[who], near[2 + side, who, :, sub]) for who in both]
        far_dprod = [
            dot_nt(grad[who][rows[row]], slots[2 + side, who, keys[row], sub]) for who, row in pairs
        ]
        near_weight, far_weight, near_half, far_half = [], [], [], []
        for i, (who, row) in enumerate(pairs):
            ns = near_score[who][rows[row]]
            top = jnp.maximum(
                jnp.max(ns, axis=1, keepdims=True), jnp.max(far_score[i], axis=1, keepdims=True)
            )
            near_exp = jnp.exp2((ns - top) * EXP_SCALE)
            far_exp = jnp.exp2((far_score[i] - top) * EXP_SCALE)
            inverse = 1.0 / (
                jnp.sum(near_exp, axis=1, keepdims=True) + jnp.sum(far_exp, axis=1, keepdims=True)
            )
            near_weight.append(near_exp * inverse)
            far_weight.append(far_exp * inverse)
            near_half.append(near_weight[i].astype(BF16))
            far_half.append(far_weight[i].astype(BF16))
        delta = []
        for i, (who, row) in enumerate(pairs):
            out = dot_nn(near_half[i], near[2 + side, who, :, sub])
            out = (out + dot_nn(far_half[i], slots[2 + side, who, keys[row], sub])).astype(BF16)
            res[who][0, rows[row], lanes] = out
            g = grad[who][rows[row]]
            delta.append(jnp.sum(g.astype(F32) * out.astype(F32), axis=1, keepdims=True))
        for i, (who, row) in enumerate(pairs):
            g = grad[who][rows[row]]
            fgrad[1, who, keys[row], lanes] = dot_tn(far_half[i], g).astype(BF16)
        near_dscore, far_dscore = [], []
        for i, (who, row) in enumerate(pairs):
            nd = near_weight[i] * (near_dprod[who][rows[row]] - delta[i])
            near_dscore.append(nd.astype(BF16))
            far_dscore.append((far_weight[i] * (far_dprod[i] - delta[i])).astype(BF16))
        for i, (who, row) in enumerate(pairs):
            dq = dot_nn(near_dscore[i], near[side, who, :, sub])
            dq = (dq + dot_nn(far_dscore[i], slots[side, who, keys[row], sub])) * SCALE
            res[who][1, rows[row], lanes] = dq.astype(BF16)
        for i, (who, row) in enumerate(pairs):
            dk = dot_tn(far_dscore[i], query[who][rows[row]]) * SCALE
            fgrad[0, who, keys[row], lanes] = dk.astype(BF16)
        for who in both:
            two = slice(who * BLK, (who + 1) * BLK)
            near_kgrad = dot_tn(jnp.concatenate(near_dscore[two], axis=0), query[who]) * SCALE
            near_vgrad = dot_tn(jnp.concatenate(near_half[two], axis=0), grad[who])
            for kind, value in enumerate((near_kgrad, near_vgrad)):
                base[who, kind, :, lanes] = value[:TOK]
                first = (who * 2 + kind) * HEADS + head
                gwide[pl.ds(first, WINDOWS, stride=GROWS), :] = value[TOK : TOK + WINDOWS]
        return carry

    lax.fori_loop(0, HEADS, head_step, 0, unroll=True)
    gglob[...] = gwide[...].reshape(WINDOWS, GROWS, HEAD_DIM).astype(BF16)
    copies = []

    def send(value, output):
        copy = pltpu.make_async_copy(value, output, out_sem.at[len(copies)])
        copy.start()
        copies.append(copy)

    send(gglob, outputs[4])
    send(res_peer, outputs[1])
    send(res_own, outputs[0])
    for source in SEND_ORDER:
        for kind in range(2):
            for inner in range(BLK):
                rows = slice(inner * BLOCK, (inner + 1) * BLOCK)
                value = None
                for who in range(2):
                    code = table[who, source]
                    slot = lax.shift_right_logical(code, 1)
                    at = pl.ds(pl.multiple_of(slot * BLOCK, BLOCK), BLOCK)
                    here = (lax.bitwise_and(code, 1) == inner).astype(F32)
                    term = fgrad[kind, who, at, :].astype(F32) * here
                    value = term if value is None else value + term
                if source == NY:
                    base[1, kind, rows, :] += value
                else:
                    spare[source, kind, rows, :] = value.astype(BF16)
        if source != NY:
            part = scattered.at[source] if source < NY else parts[source - NY - 1]
            send(spare.at[source], part)
    send(base.at[1], outputs[3])
    send(base.at[0], outputs[2])
    for copy in copies:
        copy.wait()


def cut_kernel(width, core, first, second, own, send):
    pieces = HALF // width
    for output, half in ((own, 0), (send, 1)):
        start = lax.bitwise_xor(core[0], half) * HALF
        for i in range(2):
            for piece in range(pieces):
                columns = pl.ds(pl.multiple_of(start + piece * width, width), width)
                output[i * pieces + piece] = (first, second)[i][:, columns]


def cut(core, first, second, width, room=0):
    vmem = pl.BlockSpec(memory_space=pltpu.VMEM)
    count = 2 * HALF // width
    return pl.pallas_call(
        functools.partial(cut_kernel, width),
        out_shape=[
            jax.ShapeDtypeStruct((count + room, TOK, width), BF16),
            jax.ShapeDtypeStruct((count, TOK, width), BF16),
        ],
        in_specs=[pl.BlockSpec(memory_space=pltpu.SMEM), vmem, vmem],
        out_specs=[vmem] * 2,
        cost_estimate=pl.CostEstimate(flops=0, bytes_accessed=1_000_000, transcendentals=0),
    )(core.astype(jnp.int32)[None], first, second)


def attend(pos, far_own, far_peer, qdo_own, qdo_peer, glob, gathered, ring):
    smem = pl.BlockSpec(memory_space=pltpu.SMEM)
    vmem = pl.BlockSpec(memory_space=pltpu.VMEM)
    anywhere = pl.BlockSpec(memory_space=pl.ANY)
    piece = jax.ShapeDtypeStruct((2, TOK, HALF), BF16)
    return pl.pallas_call(
        attend_kernel,
        out_shape=[
            piece,
            piece,
            jax.ShapeDtypeStruct((2, TOK, HALF), F32),
            jax.ShapeDtypeStruct((2, TOK, HALF), F32),
            jax.ShapeDtypeStruct((WINDOWS, GROWS, HEAD_DIM), BF16),
        ]
        + [jax.ShapeDtypeStruct((NY, 2, TOK, HALF), BF16)]
        + [piece] * 7,
        in_specs=[smem] * 3 + [vmem] * 3 + [anywhere] * 9,
        out_specs=[anywhere] * 13,
        scratch_shapes=[
            pltpu.VMEM((4, 2, BLK * FKEYS, PIECE), BF16),
            pltpu.VMEM((4, 2, NEAR, PIECE), BF16),
            pltpu.VMEM((2, 2, BLK * FKEYS, HALF), BF16),
            pltpu.VMEM((WINDOWS * GROWS, HEAD_DIM), F32),
            pltpu.VMEM((2, TOK, HALF), BF16),
            pltpu.VMEM((2, TOK, HALF), BF16),
            pltpu.VMEM((2, 2, TOK, HALF), F32),
            pltpu.VMEM((WINDOWS, GROWS, HEAD_DIM), BF16),
            pltpu.VMEM((2 * NY, 2, TOK, HALF), BF16),
            pltpu.SMEM((2, 2 * NY), jnp.int32),
            pltpu.SemaphoreType.DMA((3 + 6 * NY,)),
            pltpu.SemaphoreType.DMA((5 + 2 * NY,)),
        ],
        compiler_params=pltpu.CompilerParams(vmem_limit_bytes=60 * 1024 * 1024),
        cost_estimate=pl.CostEstimate(
            flops=1_200_000_000, bytes_accessed=12_000_000, transcendentals=800_000
        ),
    )(pos, far_own, far_peer, qdo_own, qdo_peer, glob, gathered, *ring)


UP = [(i, (i + 1) % NY) for i in range(NY)]
DOWN = [(i, (i - 1) % NY) for i in range(NY)]
ROW_STEP, BACK_STEP = 1, 1
SWAP = [(0, 1), (1, 0)]


def plus(a, b):
    return (a.astype(F32) + b.astype(F32)).astype(BF16)


def per_device(query_rows, key_rows, value_rows, out_grad, far_blocks):
    my_y = lax.axis_index("y")
    my_c = lax.axis_index("c")
    my_w = lax.axis_index("x") * NZ + lax.axis_index("z")
    swap = functools.partial(lax.ppermute, axis_name="c", perm=SWAP)
    up = functools.partial(lax.ppermute, axis_name="y", perm=UP)
    down = functools.partial(lax.ppermute, axis_name="y", perm=DOWN)
    low = my_c == 0

    def home(terms, sign):
        pairs = [
            (2 * y + c, (y - sign) % NY * 2 + 1 - c) for y in range(NY) for c in range(NC)
        ]
        return lax.ppermute(terms, ("y", "c"), pairs)

    kv_own, kv_send = cut(my_c, key_rows, value_rows, PIECE, room=1)
    kv_peer = swap(kv_send)
    kv_own = lax.dynamic_update_slice(kv_own, kv_peer[:1], (4, 0, 0))
    gathered = lax.all_gather(kv_own, "y", axis=0)
    ring = [kv_peer[1:]] + [None] * (NY - 1)
    qdo_own, qdo_send = cut(my_c, query_rows, out_grad, HALF)
    row = jnp.concatenate([kv_own[:4, 0], kv_peer[:, 0]]).reshape(GROWS, HEAD_DIM)
    chains = ((up, 4, -1), (down, 3, 1))
    held = [ring[0], ring[0]]
    for step in range(1, 5):
        for i, (move, count, sign) in enumerate(chains):
            if step <= count:
                held[i] = move(held[i])
        if step == ROW_STEP:
            row, held[0] = lax.optimization_barrier((row, held[0]))
            glob = lax.all_to_all(
                jnp.broadcast_to(row, (WINDOWS, GROWS, HEAD_DIM)), ("x", "z"), 0, 0, tiled=True
            )
            qdo_peer = swap(qdo_send)
            far_peer = swap(far_blocks)
        if step == 3:
            glob, qdo_peer, far_peer, held[0] = lax.optimization_barrier(
                (glob, qdo_peer, far_peer, held[0])
            )
        for i, (move, count, sign) in enumerate(chains):
            if step <= count:
                ring[(sign * step) % NY] = held[i]
    pos = jnp.stack([my_y, my_c, my_w]).astype(jnp.int32)
    res_own, res_peer, base_own, base_peer, gglob, scattered, *parts = attend(
        pos, far_blocks, far_peer, qdo_own, qdo_peer, glob, gathered, ring
    )
    base_other = swap(base_peer)
    far_own = (lax.psum_scatter(scattered, "y", scatter_dimension=0),)
    at = [4, 5]
    held = [parts[o - 1] for o in at]
    for step in range(1, 5):
        for i, (move, count, sign) in enumerate(chains):
            if step < count:
                held[i] = move(held[i])
            elif step == count:
                held[i] = home(held[i], sign)
        if step == BACK_STEP:
            gglob, held[0] = lax.optimization_barrier((gglob, held[0]))
            gback = lax.all_to_all(gglob, ("x", "z"), 0, 0, tiled=True)
        for i, (move, count, sign) in enumerate(chains):
            if step <= count:
                at[i] = (at[i] + sign) % NY
                if at[i]:
                    held[i] = plus(held[i], parts[at[i] - 1])
    far_peer = held
    gsum = jnp.sum(gback.astype(F32), axis=0).reshape(2, 2, 1, HALF)
    gsum = gsum[0], swap(gsum[1])
    res_back = swap(res_peer)
    first_row = lax.broadcasted_iota(jnp.int32, (1, TOK, 1), 1) == 0

    def finish(base, far, who):
        total = base + sum(term.astype(F32) for term in far)
        return (total + jnp.where(first_row, gsum[who], 0.0)).astype(BF16)

    other_grad = finish(base_other, far_peer, 1)
    own_grad = finish(base_own, far_own, 0)

    def join(mine, other):
        return jnp.where(
            low,
            jnp.concatenate([mine, other], axis=1),
            jnp.concatenate([other, mine], axis=1),
        )

    return (
        join(res_own[0], res_back[0]),
        join(res_own[1], res_back[1]),
        join(own_grad[0], other_grad[0]),
        join(own_grad[1], other_grad[1]),
    )


def solution(mesh):
    fine = Mesh(mesh.devices.reshape(NX, NZ, NY, NC), ("x", "z", "y", "c"))
    spec = P(("y", "c", "x", "z"), None)
    return jax.shard_map(
        per_device, mesh=fine, in_specs=(spec,) * 5, out_specs=(spec,) * 4, check_vma=False
    )
```
